128 devices in a mesh: node: 8 (over y, core), local: 16 (over z, x).
Axes of the slice: x: 4, y: 4, z: 4, core: 2. Of those that a mesh axis runs over, the one named last changes fastest.
Arguments:
- out_grad: bfloat16 [16384, 3584], P(('node', 'local')), may hold values from -6 to 6
- gates: bfloat16 [16384, 2], P(('node', 'local')), may hold values from 0.099609375 to 2
- expert_ids: int32 [16384, 2], P(('node', 'local')), may hold values from 0 to 31, as said below
- saved_pre: bfloat16 [128, 128, 12, 1024], P(('node', 'local')), may hold values from -6 to 6
- w_gate_up: bfloat16 [128, 3584, 1024], P(('node', 'local')), may hold values from -0.09375 to 0.09375
- w_down: bfloat16 [128, 512, 3584], P(('node', 'local')), may hold values from -0.125 to 0.125
Outputs:
- input_grad: bfloat16 [16384, 3584], P(('node', 'local'))
- gate_grad: float32 [16384, 2], P(('node', 'local'))
- down_grad: bfloat16 [128, 512, 3584], P(('node', 'local'))
The draws below stay inside these ranges and needn't reach their ends.
Inputs may be any that keep to these rules, and one draw needn't show every extreme that they name: `expert_ids`: each token names 2 different experts, all of one node group (expert e belongs to group e // 4). Among the tokens of one device, at most 24 name experts of any one group and at most 12 name any one expert; on every device some group has exactly 24 tokens and some expert exactly 12.
All inputs are finite; a program needn't handle non-finite values.
Results may differ from the reference program's by a relative error of at most 0.0057.
Values may be sent and summed in bfloat16 or wider, within the bound.
A program may use at most 192 MiB of HBM per device.

```python
import math
import jax
import jax.numpy as jnp
from jax import lax

D = 3584
FF = 2048
HID = 512
TOPK = 2
TOK_DEV = 128
SLICES = 4
EXP_GROUP = 4
EXPERTS = 32
TOKENS = 16384
UNITS = 128
GROUP_CAP = 24
SLOT_CAP = 12
N_NODE = 8
N_LOCAL = 16
DEVICES = 128


def pick_block(noise_rows, popular, hot_group, order):
    group_count = EXPERTS // EXP_GROUP
    expert_axis = jnp.arange(EXPERTS, dtype=jnp.int32)
    group_axis = jnp.arange(group_count, dtype=jnp.int32)
    group_of = expert_axis // EXP_GROUP
    member = (group_of[None, :] == group_axis[:, None]).astype(jnp.int32)

    def advance(carry, inputs):
        expert_load, group_load = carry
        noise_row, position = inputs
        forced = position < GROUP_CAP
        has_room = (expert_load < SLOT_CAP).astype(jnp.int32)
        room_left = jnp.sum(member * has_room[None, :], axis=1)
        base_score = noise_row + popular
        best_score = jnp.max(jnp.where(member == 1, base_score[None, :], -1), axis=1)
        eligible = (group_load < GROUP_CAP) & (room_left >= TOPK)
        group_score = jnp.where(eligible, best_score * group_count + group_axis, -1)
        group_score = jnp.where(forced, (group_axis == hot_group).astype(jnp.int32), group_score)
        picked_group = lax.top_k(group_score, 1)[1][0]
        expert_score = jnp.where(forced, noise_row - expert_load * 8192, base_score)
        expert_score = expert_score * EXPERTS + expert_axis
        usable = (group_of == picked_group) & (has_room == 1)
        expert_score = jnp.where(usable, expert_score, -2 ** 30)
        chosen = lax.top_k(expert_score, TOPK)[1].astype(jnp.int32)
        added = jnp.sum((chosen[:, None] == expert_axis[None, :]).astype(jnp.int32), axis=0)
        new_groups = group_load + (group_axis == picked_group).astype(jnp.int32)
        return ((expert_load + added, new_groups), chosen)
    start = (jnp.zeros((EXPERTS,), jnp.int32), jnp.zeros((group_count,), jnp.int32))
    _, picks = lax.scan(advance, start, (noise_rows, jnp.arange(TOK_DEV, dtype=jnp.int32)))
    return picks[order]


def draw_expert_ids(key, part):
    key = jax.random.fold_in(key, 5)
    blocks = TOKENS // TOK_DEV
    key_pop, key_noise, key_hot, key_perm = jax.random.split(key, 4)
    popular = jax.random.randint(key_pop, (EXPERTS,), 0, 3000, dtype=jnp.int32)
    noise = jax.random.randint(key_noise, (blocks, TOK_DEV, EXPERTS), 0, 1000, dtype=jnp.int32)
    hot = jax.random.randint(key_hot, (blocks,), 0, EXPERTS // EXP_GROUP, dtype=jnp.int32)
    orders = jax.vmap(lambda single: jax.random.permutation(single, TOK_DEV))(jax.random.split(key_perm, blocks))
    picks = jax.vmap(pick_block, in_axes=(0, None, 0, 0))(noise, popular, hot, orders)
    return picks.reshape(TOKENS, TOPK).astype(jnp.int32)


def steps_of(stream_key, dims, cuts, smallest, high):
    def one(dim, blocks):
        steps = jax.random.uniform(jax.random.fold_in(jax.random.fold_in(stream_key, 6), dim), (blocks,), jnp.float32, smallest / len(cuts), high / len(cuts))
        return jnp.repeat(jnp.exp(steps), dims[dim] // blocks).reshape((-1,) + (1,) * (len(dims) - dim - 1))

    factor_of = one(*cuts[0])
    for cut in cuts[1:]:
        factor_of = factor_of * one(*cut)
    return factor_of


def gaussian(rng, dims, width, limit, pieces=(), held_as=jnp.bfloat16):
    level = steps_of(rng, dims, pieces, -0.22, 0.18) if pieces else 1.0
    result = jax.random.normal(rng, dims, jnp.float32) * width * level
    return jnp.minimum(jnp.maximum(result, -limit), limit).astype(held_as)


def setup_inputs(seed: int = 0) -> dict:
    splits = jax.random.split(jax.random.key(seed), 7)
    return {
        "out_grad": gaussian(splits[0], (TOKENS, D), 1.0, 6.0, ((0, 128),)),
        "gates": jnp.clip(jnp.exp(math.log(2.0) - 2.9996462 * jax.random.uniform(splits[1], (TOKENS, TOPK), jnp.float32) ** steps_of(splits[1], (TOKENS, TOPK), ((0, 128),), -0.2, 0.2)), 0.099609375, 2.0).astype(jnp.bfloat16),
        "expert_ids": draw_expert_ids(jax.random.fold_in(splits[6], 71), 0),
        "saved_pre": gaussian(splits[3], (UNITS, DEVICES, SLOT_CAP, 2 * HID), 1.0, 6.0, ((0, 128),)),
        "w_gate_up": gaussian(splits[4], (UNITS, D, 2 * HID), D ** -0.5, 0.09375, ((0, 128),)),
        "w_down": gaussian(splits[5], (UNITS, HID, D), FF ** -0.5, 0.125, ((0, 128),)),
    }


def expert_backward(rows, weights_here, saved, gate_up, down):
    hidden_units = down.shape[0]
    gate_pre = saved[:, :hidden_units].astype(jnp.float32)
    up_pre = saved[:, hidden_units:].astype(jnp.float32)
    sigma = jax.nn.sigmoid(gate_pre)
    activation = gate_pre * sigma
    hidden = activation * up_pre
    d_act = lax.dot_general(rows, down, (((1,), (1,)), ((), ())), preferred_element_type=jnp.float32)
    gate_part = jnp.sum(hidden * d_act, axis=-1).astype(jnp.bfloat16)
    scale = weights_here.astype(jnp.float32)[:, None]
    d_hidden = scale * d_act
    d_gate = d_hidden * up_pre * sigma * (1.0 + gate_pre * (1.0 - sigma))
    d_up = d_hidden * activation
    d_pre = jnp.concatenate([d_gate, d_up], axis=-1).astype(jnp.bfloat16)
    x_part = lax.dot_general(d_pre, gate_up, (((1,), (1,)), ((), ())), preferred_element_type=jnp.float32).astype(jnp.bfloat16)
    weighted = (scale * hidden).astype(jnp.bfloat16)
    w_grad = lax.dot_general(weighted, rows, (((0,), (0,)), ((), ())), preferred_element_type=jnp.float32).astype(jnp.bfloat16)
    return x_part, gate_part, w_grad


def reference(out_grad, gates, expert_ids, saved_pre, w_gate_up, w_down):
    devices_all = N_NODE * N_LOCAL
    routed = expert_ids.reshape(devices_all, TOK_DEV, TOPK)
    onehot = (routed[..., None] == jnp.arange(EXPERTS, dtype=jnp.int32)).astype(jnp.int32)
    per_token = jnp.sum(onehot, axis=2)
    earlier = jnp.cumsum(per_token, axis=1) - per_token
    rank = jnp.sum(earlier[:, :, None, :] * onehot, axis=-1)
    source = jnp.arange(devices_all, dtype=jnp.int32)[:, None, None]
    position = ((routed * devices_all + source) * SLOT_CAP + rank).reshape(-1)
    token_of = jnp.broadcast_to(jnp.arange(TOKENS, dtype=jnp.int32).reshape(devices_all, TOK_DEV, 1), routed.shape).reshape(-1)
    pair_of = jnp.arange(TOKENS * TOPK, dtype=jnp.int32)
    slot_total = EXPERTS * devices_all * SLOT_CAP
    token_table = jnp.full((slot_total,), TOKENS, jnp.int32).at[position].set(token_of).reshape(EXPERTS, devices_all * SLOT_CAP)
    pair_table = jnp.full((slot_total,), TOKENS * TOPK, jnp.int32).at[position].set(pair_of).reshape(EXPERTS, devices_all * SLOT_CAP)
    padded_rows = jnp.concatenate([out_grad, jnp.zeros((1, D), out_grad.dtype)], axis=0)
    padded_gates = jnp.concatenate([gates.reshape(-1), jnp.zeros((1,), gates.dtype)])

    def per_unit(carry, unit):
        dx_total, gate_total = carry
        expert = (unit // N_LOCAL) * EXP_GROUP + (unit % N_LOCAL) // SLICES
        tokens_here = token_table[expert]
        pairs_here = pair_table[expert]
        rows = padded_rows[tokens_here]
        weights_here = padded_gates[pairs_here]
        saved = saved_pre[unit].reshape(devices_all * SLOT_CAP, 2 * HID)
        x_part, gate_part, w_grad = expert_backward(rows, weights_here, saved, w_gate_up[unit], w_down[unit])
        x_part = lax.optimization_barrier(x_part)
        gate_part = lax.optimization_barrier(gate_part)
        dx_total = dx_total.at[tokens_here].add(x_part.astype(jnp.float32))
        gate_total = gate_total.at[pairs_here].add(gate_part.astype(jnp.float32))
        return (dx_total, gate_total), w_grad

    start = (jnp.zeros((TOKENS + 1, D), jnp.float32), jnp.zeros((TOKENS * TOPK + 1,), jnp.float32))
    (dx_total, gate_total), down_grad = lax.scan(per_unit, start, jnp.arange(devices_all, dtype=jnp.int32))
    input_grad = dx_total[:TOKENS].astype(jnp.bfloat16)
    gate_grad = gate_total[:TOKENS * TOPK].reshape(TOKENS, TOPK)
    return (input_grad, gate_grad, down_grad)
```

```python
import functools

import jax
import jax.numpy as jnp
from jax import lax
from jax.experimental import pallas as pl
from jax.experimental.pallas import tpu as pltpu
from jax.sharding import PartitionSpec as P

NX = 4
PAD = 16
MESH = pl.DeviceIdType.MESH
F32 = jnp.float32
BF16 = jnp.bfloat16


def iota(shape, dim):
    return lax.broadcasted_iota(jnp.int32, shape, dim)


def mm(a, b):
    return jnp.dot(a, b, preferred_element_type=F32)


def mm_nt(a, b):
    return lax.dot_general(a, b, (((1,), (1,)), ((), ())), preferred_element_type=F32)


def kernel(
    B, C, SLOT,
    ids_ref, gates_ref, og_ref, saved_hbm, wgu_hbm, wd_hbm,
    ig_ref, gg_ref, dg_hbm,
    wgu, wd, send, recv, back, Y, GB, XP, RA, RB, GPS, GPR, S, wT, dtile, mt, dpre, dact,
    wsem, ssem, dsem, s1s, s1r, ags, agr, gbs, gbr, xps, rar, rbr, gps, gpr, rets, backr,
):
    T, D = og_ref.shape
    H = wd.shape[0]
    BLK = B * SLOT
    HALF = BLK // 2
    MSG = B * PAD
    ROWS = NX * BLK
    NSLOT = XP.shape[0]
    n = lax.axis_index("node")
    l = lax.axis_index("local")
    z, x = l // NX, l % NX
    right = (n, z * NX + (x + 1) % NX)
    left = (n, z * NX + (x + NX - 1) % NX)

    def peer(c, d):
        return ((n + d) % B, ((z + c) % C) * NX + x)

    def source(c, d):
        return ((n + B - d) % B, ((z + C - c) % C) * NX + x)

    def along(k):
        return (n, z * NX + (x + k) % NX)

    barrier = pltpu.get_barrier_semaphore()
    count = 0
    for c in range(C):
        for d in range(B):
            if c or d:
                pl.semaphore_signal(barrier, inc=1, device_id=peer(c, d), device_id_type=MESH)
                count += 1
    for k in range(1, NX):
        pl.semaphore_signal(barrier, inc=1, device_id=along(k), device_id_type=MESH)
        count += 1

    wd_copy = pltpu.make_async_copy(wd_hbm, wd, wsem.at[0])
    wgu_copy = pltpu.make_async_copy(wgu_hbm, wgu, wsem.at[1])

    def saved_start(c):
        slot = c % 2

        def one(i, _):
            j, d = i // B, i % B
            q = ((n + B - d) % B) * (C * NX) + ((z + C - c) % C) * NX + (x + j) % NX
            pltpu.make_async_copy(
                saved_hbm.at[q], S.at[slot, pl.ds(pl.multiple_of(i * PAD, PAD), PAD)], ssem.at[slot]
            ).start()
            return 0

        lax.fori_loop(0, NX * B, one, 0)

    def saved_wait(c):
        slot = c % 2
        pltpu.make_async_copy(S.at[slot], S.at[slot], ssem.at[slot]).wait()

    wd_copy.start()
    saved_start(0)
    wgu_copy.start()
    if C > 1:
        saved_start(1)

    lane = iota((T, 128), 1)

    def expert(k):
        return ids_ref[:, k : k + 1]

    hits = [lane == expert(k) for k in range(2)]
    per_token = hits[0].astype(F32) + hits[1].astype(F32)
    before = (iota((T, T), 1) < iota((T, T), 0)).astype(F32).astype(BF16)
    earlier = mm(before, per_token.astype(BF16))

    def rank(k):
        return jnp.sum(jnp.where(hits[k], earlier, 0.0), axis=1, keepdims=True).astype(jnp.int32)

    def block(k):
        e = expert(k)
        node = lax.shift_right_logical(e, jnp.int32(C.bit_length() - 1))
        zz = e & (C - 1)
        return ((zz - z + C) & (C - 1)) * B + ((node - n + B) & (B - 1))

    ranks = [rank(k) for k in range(2)]
    blocks = [block(k) for k in range(2)]
    slots = iota((T, C * MSG), 1)
    pick = jnp.zeros((T, C * MSG), F32)
    gate_rows = jnp.zeros((C * MSG, 128), F32)
    for k in range(2):
        pick += (slots == blocks[k] * PAD + ranks[k]).astype(F32)
        row_of = (slots == blocks[k] * PAD + SLOT).astype(F32)
        gate_at = jnp.where(lane == ranks[k], gates_ref[:, k : k + 1].astype(F32), 0.0)
        gate_rows += mm(jnp.transpose(row_of).astype(BF16), gate_at.astype(BF16))
    mt[...] = pick.astype(BF16)
    pick_t = jnp.transpose(pick).astype(BF16)
    TILE = 512 if D % 512 == 0 else D
    for i in range(D // TILE):
        cols = slice(i * TILE, (i + 1) * TILE)
        send[:, cols] = mm(pick_t, og_ref[:, cols]).astype(BF16)
    send[:, :128] = (send[:, :128].astype(F32) + gate_rows).astype(BF16)

    pl.semaphore_wait(barrier, count)

    for c in range(C):
        for d in range(B):
            rows = pl.ds((c * B + d) * PAD, PAD)
            if c or d:
                pltpu.make_async_remote_copy(
                    src_ref=send.at[rows], dst_ref=recv.at[rows], send_sem=s1s, recv_sem=s1r.at[c],
                    device_id=peer(c, d), device_id_type=MESH,
                ).start()
    recv[:PAD] = send[:PAD]

    i96, s128 = iota((BLK, MSG), 0), iota((BLK, MSG), 1)
    compact = (
        (i96 == SLOT * lax.shift_right_logical(s128, jnp.int32(4)) + (s128 & 15)) & ((s128 & 15) < SLOT)
    ).astype(F32).astype(BF16)
    s128b, i96b = iota((MSG, BLK), 0), iota((MSG, BLK), 1)
    expand = (
        (i96b == SLOT * lax.shift_right_logical(s128b, jnp.int32(4)) + (s128b & 15)) & ((s128b & 15) < SLOT)
    ).astype(F32).astype(BF16)
    gate_pick = (iota((PAD, MSG), 1) == iota((PAD, MSG), 0) * PAD + SLOT).astype(F32).astype(BF16)
    src_row, src_col = iota((BLK, PAD), 0), iota((BLK, PAD), 1)
    of_source = ((src_row >= SLOT * src_col) & (src_row < SLOT * src_col + SLOT)).astype(F32).astype(BF16)
    sc_row, sc_col = iota((PAD, BLK), 0), iota((PAD, BLK), 1)
    by_source = ((sc_col >= SLOT * sc_row) & (sc_col < SLOT * sc_row + SLOT)).astype(F32).astype(BF16)
    row_id = iota((BLK, 128), 0)
    src_id = jnp.zeros((BLK, 128), jnp.int32)
    for d in range(1, B):
        src_id += (row_id >= SLOT * d).astype(jnp.int32)
    slot_mask = iota((BLK, 128), 1) == row_id - SLOT * src_id

    def yrows(c, j, lo=0, size=None):
        return pl.ds(c * ROWS + j * BLK + lo, BLK if size is None else size)

    def remote(src, dst, ssem_, rsem_, dev):
        pltpu.make_async_remote_copy(
            src_ref=src, dst_ref=dst, send_sem=ssem_, recv_sem=rsem_, device_id=dev, device_id_type=MESH
        ).start()

    def wait_for(ref, sem):
        pltpu.make_async_copy(ref, ref, sem).wait()

    def gather_start(c):
        lo = PAD if c == 0 else 0
        if MSG > lo:
            wait_for(recv.at[pl.ds(c * MSG + lo, MSG - lo)], s1r.at[c])
        for i in range(D // TILE):
            cols = slice(i * TILE, (i + 1) * TILE)
            Y[yrows(c, 0), cols] = mm(compact, recv[c * MSG : (c + 1) * MSG, cols]).astype(BF16)
        GB[c, 0] = mm(gate_pick, recv[c * MSG : (c + 1) * MSG, :128]).astype(BF16)
        remote(Y.at[yrows(c, 0)], Y.at[yrows(c, 3)], ags, agr.at[c, 0], right)
        remote(Y.at[yrows(c, 0)], Y.at[yrows(c, 1)], ags, agr.at[c, 1], left)
        for k in range(1, NX):
            remote(GB.at[c, 0], GB.at[c, NX - k], gbs, gbr.at[c], along(k))

    def gather_forward(c):
        wait_for(Y.at[yrows(c, 3)], agr.at[c, 0])
        remote(Y.at[yrows(c, 3, 0, HALF)], Y.at[yrows(c, 2, 0, HALF)], ags, agr.at[c, 2], right)
        wait_for(Y.at[yrows(c, 1)], agr.at[c, 1])
        remote(Y.at[yrows(c, 1, HALF, HALF)], Y.at[yrows(c, 2, HALF, HALF)], ags, agr.at[c, 2], left)

    def compute(c):
        slot = c % 2
        xs = c % NSLOT
        wait_for(Y.at[yrows(c, 2)], agr.at[c, 2])
        wait_for(GB.at[c, pl.ds(1, NX - 1)], gbr.at[c])
        if c == 0:
            wd_copy.wait()
        NT = 256 if H % 256 == 0 else H
        for i in range(H // NT):
            dact[:, i * NT : (i + 1) * NT] = mm_nt(Y[c * ROWS : (c + 1) * ROWS, :], wd[i * NT : (i + 1) * NT, :])
        saved_wait(c)
        for j in range(NX):
            rows = slice(j * BLK, (j + 1) * BLK)
            pre = mm(compact, S[slot, j * MSG : (j + 1) * MSG, :])
            a, b = pre[:, :H], pre[:, H:]
            da = dact[rows, :]
            spread = mm(of_source, GB[c, j])
            scale = jnp.sum(jnp.where(slot_mask, spread, 0.0), axis=1, keepdims=True)
            s = jax.nn.sigmoid(a)
            act = a * s
            hidden = act * b
            part = jnp.sum(hidden * da, axis=1, keepdims=True)
            parts = jnp.where(slot_mask, part, 0.0).astype(BF16)
            GPS[c, j] = mm(by_source, parts).astype(BF16)
            dh = scale * da
            dpre[rows, :H] = (dh * b * s * (1.0 + a * (1.0 - s))).astype(BF16)
            dpre[rows, H:] = (dh * act).astype(BF16)
            dact[rows, :] = scale * hidden
        wT[:, c * ROWS : (c + 1) * ROWS] = jnp.transpose(dact[...]).astype(BF16)
        for k in range(1, NX):
            remote(GPS.at[c, k], GPR.at[c, NX - k], gps, gpr.at[c], along(k))
        if c + 2 < C:
            saved_start(c + 2)
        if c == 0:
            wgu_copy.wait()
        if c >= NSLOT:
            wait_for(XP.at[xs, pl.ds(BLK, ROWS - BLK)], xps.at[c - NSLOT])
        NU = 256 if D % 256 == 0 else D

        def tile(i, _):
            cols = pl.ds(pl.multiple_of(i * NU, NU), NU)
            XP[xs, :, cols] = mm_nt(dpre[...], wgu[cols, :]).astype(BF16)
            return 0

        lax.fori_loop(0, D // NU, tile, 0)

        def rows_of(j, lo, size):
            return pl.ds(j * BLK + lo, size)

        remote(XP.at[xs, rows_of(2, 0, HALF)], RA.at[c, 0], xps.at[c], rar.at[c, 0], right)
        remote(XP.at[xs, rows_of(2, HALF, HALF)], RA.at[c, 1], xps.at[c], rar.at[c, 1], left)
        remote(XP.at[xs, rows_of(1, HALF, HALF)], RB.at[c, 0, pl.ds(HALF, HALF)], xps.at[c], rbr.at[c, 0], right)
        remote(XP.at[xs, rows_of(3, 0, HALF)], RB.at[c, 1, pl.ds(0, HALF)], xps.at[c], rbr.at[c, 1], left)

    def reduce_middle(c):
        xs = c % NSLOT
        for side, j, lo, dev in ((0, 1, 0, right), (1, 3, HALF, left)):
            wait_for(RA.at[c, side], rar.at[c, side])
            rows = slice(j * BLK + lo, j * BLK + lo + HALF)
            XP[xs, rows, :] = (XP[xs, rows, :].astype(F32) + RA[c, side].astype(F32)).astype(BF16)
            remote(
                XP.at[xs, pl.ds(j * BLK + lo, HALF)], RB.at[c, side, pl.ds(lo, HALF)],
                xps.at[c], rbr.at[c, side], dev,
            )

    def reduce_end(c):
        xs = c % NSLOT
        wait_for(GPR.at[c, pl.ds(1, NX - 1)], gpr.at[c])
        total = GPS[c, 0].astype(F32)
        for k in range(1, NX):
            total += GPR[c, k].astype(F32)
        high = total.astype(BF16)
        low = (total - high.astype(F32)).astype(BF16)
        up = iota((MSG, PAD), 0) - iota((MSG, PAD), 1) * PAD
        gate_back = mm((up == SLOT).astype(F32).astype(BF16), high)
        gate_back += mm((up == SLOT + 1).astype(F32).astype(BF16), low)
        wait_for(RB.at[c, 0], rbr.at[c, 0])
        wait_for(RB.at[c, 1], rbr.at[c, 1])
        for i in range(D // TILE):
            cols = slice(i * TILE, (i + 1) * TILE)
            whole = XP[xs, :BLK, cols].astype(F32) + RB[c, 0, :, cols].astype(F32) + RB[c, 1, :, cols].astype(F32)
            out = mm(expand, whole.astype(BF16))
            if i == 0:
                recv[c * MSG : (c + 1) * MSG, :128] = (out[:, :128] + gate_back).astype(BF16)
                if TILE > 128:
                    recv[c * MSG : (c + 1) * MSG, 128:TILE] = out[:, 128:].astype(BF16)
            else:
                recv[c * MSG : (c + 1) * MSG, cols] = out.astype(BF16)
        for d in range(B):
            rows = pl.ds((c * B + d) * PAD, PAD)
            if c or d:
                remote(recv.at[rows], back.at[rows], rets, backr.at[c], source(c, d))
        if c == 0:
            back[:PAD] = recv[:PAD]

    NG = 256 if D % 256 == 0 else D
    tiles = D // NG

    def weight_grad():
        def out_copy(i, s):
            return pltpu.make_async_copy(
                dtile.at[s], dg_hbm.at[:, pl.ds(pl.multiple_of(i * NG, NG), NG)], dsem.at[s]
            )

        def tile(i, _):
            s = i % 2

            @pl.when(i >= 2)
            def _():
                out_copy(i - 2, s).wait()

            cols = pl.ds(pl.multiple_of(i * NG, NG), NG)
            dtile[s] = mm(wT[...], Y[:, cols]).astype(BF16)
            out_copy(i, s).start()
            return 0

        lax.fori_loop(0, tiles, tile, 0)
        for i in range(max(tiles - 2, 0), tiles):
            out_copy(i, i % 2).wait()

    gather_start(0)
    if C == 4:
        gather_start(1)
        gather_forward(0)
        gather_start(2)
        gather_forward(1)
        compute(0)
        gather_start(3)
        gather_forward(2)
        compute(1)
        reduce_middle(0)
        gather_forward(3)
        compute(2)
        reduce_end(0)
        reduce_middle(1)
        compute(3)
        reduce_end(1)
        reduce_middle(2)
        weight_grad()
        reduce_end(2)
        reduce_middle(3)
        reduce_end(3)
    else:
        for c in range(C):
            if c:
                gather_start(c)
            gather_forward(c)
            compute(c)
            reduce_middle(c)
            reduce_end(c)
        weight_grad()

    for c in range(C):
        lo = PAD if c == 0 else 0
        if MSG > lo:
            wait_for(back.at[pl.ds(c * MSG + lo, MSG - lo)], backr.at[c])
    for i in range(D // TILE):
        cols = slice(i * TILE, (i + 1) * TILE)
        ig_ref[:, cols] = mm(mt[...], back[:, cols]).astype(BF16)
    for k in range(2):
        at = slots - blocks[k] * PAD
        rows = ((at == SLOT) | (at == SLOT + 1)).astype(F32).astype(BF16)
        found = mm(rows, back[:, :128])
        gg_ref[:, k : k + 1] = jnp.sum(jnp.where(lane == ranks[k], found, 0.0), axis=1, keepdims=True)

    total = C * MSG - PAD
    wait_for(send.at[pl.ds(0, total)], s1s)
    wait_for(recv.at[pl.ds(0, total)], rets)
    wait_for(Y.at[pl.ds(0, C * 3 * BLK)], ags)
    for c in range(C):
        wait_for(GB.at[c, pl.ds(1, NX - 1)], gbs)
        wait_for(GPS.at[c, pl.ds(1, NX - 1)], gps)
    for c in range(max(0, C - NSLOT), C):
        wait_for(XP.at[c % NSLOT, pl.ds(BLK, ROWS - BLK)], xps.at[c])


def body(out_grad, gates, expert_ids, saved_pre, w_gate_up, w_down):
    T, D = out_grad.shape
    B = lax.axis_size("node")
    C = lax.axis_size("local") // NX
    Q, SLOT = saved_pre.shape[1:3]
    H = w_down.shape[1]
    saved = jnp.pad(saved_pre[0], ((0, 0), (0, PAD - SLOT), (0, 0)))
    BLK, MSG = B * SLOT, B * PAD
    ROWS = NX * BLK
    NSLOT = min(3, C)
    vm = pl.BlockSpec(memory_space=pltpu.VMEM)
    anywhere = pl.BlockSpec(memory_space=pl.ANY)
    dma = pltpu.SemaphoreType.DMA
    NG = 256 if D % 256 == 0 else D
    ig, gg, dg = pl.pallas_call(
        functools.partial(kernel, B, C, SLOT),
        out_shape=(
            jax.ShapeDtypeStruct((T, D), BF16),
            jax.ShapeDtypeStruct((T, 2), F32),
            jax.ShapeDtypeStruct((H, D), BF16),
        ),
        in_specs=[vm, vm, vm, anywhere, anywhere, anywhere],
        out_specs=(vm, vm, anywhere),
        scratch_shapes=[
            pltpu.VMEM((D, 2 * H), BF16),
            pltpu.VMEM((H, D), BF16),
            pltpu.VMEM((C * MSG, D), BF16),
            pltpu.VMEM((C * MSG, D), BF16),
            pltpu.VMEM((C * MSG, D), BF16),
            pltpu.VMEM((C * ROWS, D), BF16),
            pltpu.VMEM((C, NX, PAD, 128), BF16),
            pltpu.VMEM((NSLOT, ROWS, D), BF16),
            pltpu.VMEM((C, 2, BLK // 2, D), BF16),
            pltpu.VMEM((C, 2, BLK, D), BF16),
            pltpu.VMEM((C, NX, PAD, 128), BF16),
            pltpu.VMEM((C, NX, PAD, 128), BF16),
            pltpu.VMEM((2, NX * MSG, 2 * H), BF16),
            pltpu.VMEM((H, C * ROWS), BF16),
            pltpu.VMEM((2, H, NG), BF16),
            pltpu.VMEM((T, C * MSG), BF16),
            pltpu.VMEM((ROWS, 2 * H), BF16),
            pltpu.VMEM((ROWS, H), F32),
            dma((2,)),
            dma((2,)),
            dma((2,)),
            dma,
            dma((C,)),
            dma,
            dma((C, 3)),
            dma,
            dma((C,)),
            dma((C,)),
            dma((C, 2)),
            dma((C, 2)),
            dma,
            dma((C,)),
            dma,
            dma((C,)),
        ],
        compiler_params=pltpu.CompilerParams(
            collective_id=0, has_side_effects=True, vmem_limit_bytes=63 * 1024 * 1024
        ),
        cost_estimate=pl.CostEstimate(
            flops=2 * C * ROWS * D * 4 * H, bytes_accessed=25_000_000, transcendentals=C * ROWS * H
        ),
        name="moe_backward",
    )(expert_ids, gates, out_grad, saved, w_gate_up[0], w_down[0])
    return ig, gg, dg[None]


def solution(mesh):
    in_specs = (
        P(("node", "local"), None),
        P(("node", "local"), None),
        P(("node", "local"), None),
        P(("node", "local"), None, None, None),
        P(("node", "local"), None, None),
        P(("node", "local"), None, None),
    )
    out_specs = (
        P(("node", "local"), None),
        P(("node", "local"), None),
        P(("node", "local"), None, None),
    )
    return jax.shard_map(body, mesh=mesh, in_specs=in_specs, out_specs=out_specs, check_vma=False)
```

```python
import functools

import jax
import jax.numpy as jnp
from jax import lax
from jax.experimental import pallas as pl
from jax.experimental.pallas import tpu as pltpu
from jax.sharding import PartitionSpec as P

NX = 4
PAD = 16
TILE = 256
MESH = pl.DeviceIdType.MESH
F32 = jnp.float32
BF16 = jnp.bfloat16


def split(D):
    return max(TILE, 9 * D // 14 // TILE * TILE)


def iota(shape, dim):
    return lax.broadcasted_iota(jnp.int32, shape, dim)


def shr(v, bits):
    return lax.shift_right_logical(v, jnp.full(v.shape, bits, jnp.int32))


def log2(size):
    return size.bit_length() - 1


def mm(a, b):
    return jnp.dot(a, b, preferred_element_type=F32)


def mm_nt(a, b):
    return lax.dot_general(a, b, (((1,), (1,)), ((), ())), preferred_element_type=F32)


def hot(mask):
    return mask.astype(F32).astype(BF16)


def kernel(
    B, C, SLOT,
    ids_ref, gates_ref, og_ref, saved_hbm, wgu_hbm, wd_hbm,
    ig_ref, gg_ref, dg_hbm,
    wgu, wd, send, recv, back, Y, GB, XP, RA, RB, GPS, GPR, saved, dtile, mt, dpre, dact,
    IDS, TB, sendB, backB, RAB, RBB, selT, perm, permT,
    wsem, ssem, dsem, s1s, s1r, ags, agr, gbs, gbr, xps, rar, rbr, gps, gpr, rets, backr,
    idss, idsr, tbs, tbr, sbs, sbr, xpbs, bbr, pbs, rabr, rbbr,
):
    T, D = og_ref.shape
    H = wd.shape[0]
    DA = split(D)
    DB = D - DA
    BLK = B * SLOT
    HALF = BLK // 2
    MSG = B * PAD
    MB = NX * SLOT
    ROWS = NX * BLK
    NSLOT = XP.shape[0]
    LB, LC = log2(B), log2(C)
    colsA, colsB = pl.ds(0, DA), pl.ds(DA, DB)
    n = lax.axis_index("node")
    l = lax.axis_index("local")
    z, x = l // NX, l % NX
    right = (n, z * NX + (x + 1) % NX)
    left = (n, z * NX + (x + NX - 1) % NX)

    def peer(c, d):
        return ((n + d) % B, ((z + c) % C) * NX + x)

    def source(c, d):
        return ((n + B - d) % B, ((z + C - c) % C) * NX + x)

    def along(k):
        return (n, z * NX + (x + k) % NX)

    def remote(src, dst, ssem_, rsem_, dev):
        pltpu.make_async_remote_copy(
            src_ref=src, dst_ref=dst, send_sem=ssem_, recv_sem=rsem_, device_id=dev, device_id_type=MESH
        ).start()

    def wait_for(ref, sem):
        pltpu.make_async_copy(ref, ref, sem).wait()

    barrier = pltpu.get_barrier_semaphore()
    count = 0
    for k in range(1, NX):
        pl.semaphore_signal(barrier, inc=1, device_id=along(k), device_id_type=MESH)
        count += 1
    for c in range(C):
        for d in range(B):
            if c or d:
                pl.semaphore_signal(barrier, inc=1, device_id=peer(c, d), device_id_type=MESH)
                count += 1

    wd_copy = pltpu.make_async_copy(wd_hbm, wd, wsem.at[0])
    wgu_copy = pltpu.make_async_copy(wgu_hbm, wgu, wsem.at[1])

    Q = C * NX * B

    def staged(r):
        return NSLOT - 1, pl.ds(r // 2 % 2 * Q, Q), pl.ds(r % 2 * 2 * H, 2 * H)

    def stage(r):
        return pltpu.make_async_copy(saved_hbm.at[r], XP.at[staged(r)], ssem.at[r % 4])

    for r in range(4):
        stage(r).start()
    wd_copy.start()
    wgu_copy.start()

    IDS[0, :2] = ids_ref[...]
    TB[:T] = og_ref[:, DA:]
    NE = max(8, B * C)
    before = hot(iota((T, T), 0) < iota((T, T), 1))
    expert_row = iota((NE, T), 0)

    def route(ids):
        experts = [ids[k : k + 1] for k in range(2)]
        hits = [expert_row == e for e in experts]
        per_token = hits[0].astype(F32) + hits[1].astype(F32)
        earlier = mm(per_token.astype(BF16), before)
        out = []
        for k in range(2):
            rank = jnp.sum(jnp.where(hits[k], earlier, 0.0), axis=0, keepdims=True).astype(jnp.int32)
            zz = experts[k] & (C - 1)
            node = shr(experts[k], LC)
            blk = ((zz - z + C) & (C - 1)) * B + ((node - n + B) & (B - 1))
            out.append((blk, rank))
        return out

    own = route(ids_ref[...])
    slots = iota((C * MSG, T), 0)
    lane_slot = iota((128, T), 0)
    pick = jnp.zeros((C * MSG, T), F32)
    gate_rows = jnp.zeros((C * MSG, 128), F32)
    gates = gates_ref[...].astype(F32)
    for k, (blk, rank) in enumerate(own):
        pick += (slots == blk * PAD + rank).astype(F32)
        gate_at = jnp.where(lane_slot == rank, gates[k : k + 1], 0.0).astype(BF16)
        gate_rows += mm_nt(hot(slots == blk * PAD + SLOT), gate_at)
    mt[...] = jnp.transpose(pick).astype(BF16)
    pick = pick.astype(BF16)

    pl.semaphore_wait(barrier, count)

    for k in range(1, NX):
        remote(IDS.at[0], IDS.at[NX - k], idss, idsr, along(k))
    remote(TB.at[pl.ds(0, T)], TB.at[pl.ds(3 * T, T)], tbs, tbr.at[0], right)
    remote(TB.at[pl.ds(0, T)], TB.at[pl.ds(T, T)], tbs, tbr.at[1], left)

    for c in range(C):
        rows = slice(c * MSG, (c + 1) * MSG)
        for i in range(DA // TILE):
            cols = slice(i * TILE, (i + 1) * TILE)
            send[rows, cols] = mm(pick[rows], og_ref[:, cols]).astype(BF16)
        send[rows, :128] = (send[rows, :128].astype(F32) + gate_rows[rows]).astype(BF16)
        for d in range(B):
            at = pl.ds((c * B + d) * PAD, PAD)
            if c or d:
                remote(send.at[at, colsA], recv.at[at], s1s, s1r.at[c], peer(c, d))
    recv[:PAD] = send[:PAD, :DA]

    def row_parts(i):
        j = jnp.zeros(i.shape, jnp.int32)
        for k in range(1, NX):
            j += (i >= k * BLK).astype(jnp.int32)
        rest = i - j * BLK
        return j, shr(rest, LB), rest & (B - 1)

    _, r_i, d_i = row_parts(iota((BLK, MSG), 0))
    compact = hot(iota((BLK, MSG), 1) == d_i * PAD + r_i)
    _, r_l, d_l = row_parts(iota((MSG, BLK), 1))
    expand = hot(iota((MSG, BLK), 0) == d_l * PAD + r_l)
    gate_pick = hot(iota((PAD, MSG), 1) == iota((PAD, MSG), 0) * PAD + SLOT)
    of_source = hot((iota((BLK, PAD), 0) & (B - 1)) == iota((BLK, PAD), 1))
    by_source = hot((iota((PAD, BLK), 1) & (B - 1)) == iota((PAD, BLK), 0))
    slot_mask = iota((BLK, 128), 1) == shr(iota((BLK, 128), 0), LB)
    j_i, r_i, d_i = row_parts(iota((ROWS, ROWS), 0))
    perm[...] = hot(iota((ROWS, ROWS), 1) == d_i * MB + j_i * SLOT + r_i)
    j_l, r_l, d_l = row_parts(iota((ROWS, ROWS), 1))
    permT[...] = hot(iota((ROWS, ROWS), 0) == d_l * MB + j_l * SLOT + r_l)

    def sort_saved():
        row, col = iota((Q, Q), 0), iota((Q, Q), 1)
        cc, jj, dd = shr(row, LB + 2), shr(row, LB) & (NX - 1), row & (B - 1)
        q = ((n + B - dd) & (B - 1)) * (C * NX) + ((z + C - cc) & (C - 1)) * NX + ((x + jj) & (NX - 1))
        order = hot(col == q)
        for p in range(SLOT // 2):
            stage(2 * p).wait()
            stage(2 * p + 1).wait()
            pair = [mm(order, XP[staged(2 * p + h)]) for h in range(2)]
            for g in range(C * NX):
                both = jnp.concatenate([v[g * B : (g + 1) * B] for v in pair], axis=0)
                saved[g * BLK + 2 * B * p : g * BLK + 2 * B * (p + 1), :] = both.astype(BF16)
            if p + 2 < SLOT // 2:
                stage(2 * p + 4).start()
                stage(2 * p + 5).start()

    def b_forward():
        h = T // 2
        wait_for(TB.at[pl.ds(3 * T, T)], tbr.at[0])
        remote(TB.at[pl.ds(3 * T, h)], TB.at[pl.ds(2 * T, h)], tbs, tbr.at[2], right)
        wait_for(TB.at[pl.ds(T, T)], tbr.at[1])
        remote(TB.at[pl.ds(T + h, h)], TB.at[pl.ds(2 * T + h, h)], tbs, tbr.at[2], left)

    def b_routes():
        wait_for(IDS.at[pl.ds(1, NX - 1)], idsr)
        return [own] + [route(IDS[j, :2]) for j in range(1, NX)]

    def b_part(ref, c, lead):
        lo = MB if c == 0 else 0
        return ref.at[lead, pl.ds(lo, ROWS - lo)] if lead is not None else ref.at[pl.ds(lo, ROWS - lo)]

    def b_select(c, routes):
        slot = c % 2
        at = iota((ROWS, T), 0)
        parts = []
        for j in range(NX):
            part = jnp.zeros((ROWS, T), F32)
            for blk, rank in routes[j]:
                part += (at == (blk - c * B) * MB + j * SLOT + rank).astype(F32)
            parts.append(part)
            selT[j * T : (j + 1) * T, c * ROWS : (c + 1) * ROWS] = jnp.transpose(part).astype(BF16)
        sel = jnp.concatenate(parts, axis=1).astype(BF16)
        if c == 0:
            wait_for(TB.at[pl.ds(2 * T, T)], tbr.at[2])
        if c >= 2 and (B > 1 or c > 2):
            wait_for(b_part(sendB, c - 2, slot), sbs.at[slot])
        for i in range(DB // TILE):
            cols = slice(i * TILE, (i + 1) * TILE)
            sendB[slot, :, cols] = mm(sel, TB[:, cols]).astype(BF16)
        for d in range(B):
            if c or d:
                remote(
                    sendB.at[slot, pl.ds(d * MB, MB)], Y.at[pl.ds(c * ROWS + d * MB, MB), colsB],
                    sbs.at[slot], sbr.at[c], peer(c, d),
                )
            else:
                Y[:MB, DA:] = sendB[slot, :MB]

    def b_land(c):
        lo = MB if c == 0 else 0
        if ROWS > lo:
            wait_for(Y.at[pl.ds(c * ROWS + lo, ROWS - lo), colsB], sbr.at[c])
        rows = slice(c * ROWS, (c + 1) * ROWS)
        for i in range(DB // TILE):
            cols = slice(DA + i * TILE, DA + (i + 1) * TILE)
            Y[rows, cols] = mm(perm[...], Y[rows, cols]).astype(BF16)

    def yrows(c, j, lo=0, size=None):
        return pl.ds(c * ROWS + j * BLK + lo, BLK if size is None else size)

    def gather_start(c):
        lo = PAD if c == 0 else 0
        if MSG > lo:
            wait_for(recv.at[pl.ds(c * MSG + lo, MSG - lo)], s1r.at[c])
        own_rows = slice(c * ROWS, c * ROWS + BLK)
        for i in range(DA // TILE):
            cols = slice(i * TILE, (i + 1) * TILE)
            Y[own_rows, cols] = mm(compact, recv[c * MSG : (c + 1) * MSG, cols]).astype(BF16)
        GB[c, 0] = mm(gate_pick, recv[c * MSG : (c + 1) * MSG, :128]).astype(BF16)
        remote(Y.at[yrows(c, 0), colsA], Y.at[yrows(c, 3), colsA], ags, agr.at[c, 0], right)
        remote(Y.at[yrows(c, 0), colsA], Y.at[yrows(c, 1), colsA], ags, agr.at[c, 1], left)
        for k in range(1, NX):
            remote(GB.at[c, 0], GB.at[c, NX - k], gbs, gbr.at[c], along(k))

    def gather_forward(c):
        wait_for(Y.at[yrows(c, 3), colsA], agr.at[c, 0])
        remote(Y.at[yrows(c, 3, 0, HALF), colsA], Y.at[yrows(c, 2, 0, HALF), colsA], ags, agr.at[c, 2], right)
        wait_for(Y.at[yrows(c, 1), colsA], agr.at[c, 1])
        remote(Y.at[yrows(c, 1, HALF, HALF), colsA], Y.at[yrows(c, 2, HALF, HALF), colsA], ags, agr.at[c, 2], left)

    def compute(c):
        xs = c % NSLOT
        wait_for(Y.at[yrows(c, 2), colsA], agr.at[c, 2])
        wait_for(GB.at[c, pl.ds(1, NX - 1)], gbr.at[c])
        b_land(c)
        if c == 0:
            wd_copy.wait()
            wait_for(send.at[pl.ds(0, C * MSG - PAD), colsA], s1s)
        NT = min(TILE, H)
        for i in range(H // NT):
            dact[:, i * NT : (i + 1) * NT] = mm_nt(Y[c * ROWS : (c + 1) * ROWS, :], wd[i * NT : (i + 1) * NT, :])
        for j in range(NX):
            rows = slice(j * BLK, (j + 1) * BLK)
            at = c * ROWS + j * BLK
            a = saved[at : at + BLK, :H].astype(F32)
            b = saved[at : at + BLK, H:].astype(F32)
            da = dact[rows, :]
            spread = mm(of_source, GB[c, j])
            scale = jnp.sum(jnp.where(slot_mask, spread, 0.0), axis=1, keepdims=True)
            s = jax.nn.sigmoid(a)
            act = a * s
            hidden = act * b
            part = jnp.sum(hidden * da, axis=1, keepdims=True)
            parts = jnp.where(slot_mask, part, 0.0).astype(BF16)
            GPS[c, j] = mm(by_source, parts).astype(BF16)
            dh = scale * da
            dpre[rows, :H] = (dh * b * s * (1.0 + a * (1.0 - s))).astype(BF16)
            dpre[rows, H:] = (dh * act).astype(BF16)
            dact[rows, :] = scale * hidden
        for k in range(1, NX):
            remote(GPS.at[c, k], GPR.at[c, NX - k], gps, gpr.at[c], along(k))
        if c == 0:
            wgu_copy.wait()
        if c >= NSLOT:
            o = c - NSLOT
            wait_for(XP.at[xs, pl.ds(BLK, ROWS - BLK), colsA], xps.at[o])
            lo = MB if o == 0 else 0
            if ROWS > lo:
                wait_for(XP.at[xs, pl.ds(lo, ROWS - lo), colsB], xpbs.at[o])

        def tile_b(i, _):
            cols = pl.ds(pl.multiple_of(DA + i * TILE, TILE), TILE)
            XP[xs, :, cols] = mm(permT[...], mm_nt(dpre[...], wgu[cols, :]).astype(BF16)).astype(BF16)
            return 0

        lax.fori_loop(0, DB // TILE, tile_b, 0)
        for d in range(B):
            rows = pl.ds(d * MB, MB)
            if c or d:
                remote(
                    XP.at[xs, rows, colsB], backB.at[pl.ds((c * B + d) * MB, MB)],
                    xpbs.at[c], bbr.at[c], source(c, d),
                )
            else:
                backB[:MB] = XP[xs, :MB, DA:]

        def tile_a(i, _):
            cols = pl.ds(pl.multiple_of(i * TILE, TILE), TILE)
            XP[xs, :, cols] = mm_nt(dpre[...], wgu[cols, :]).astype(BF16)
            return 0

        lax.fori_loop(0, DA // TILE, tile_a, 0)

        def part_of(j, lo):
            return XP.at[xs, pl.ds(j * BLK + lo, HALF), colsA]

        remote(part_of(2, 0), RA.at[c, 0], xps.at[c], rar.at[c, 0], right)
        remote(part_of(2, HALF), RA.at[c, 1], xps.at[c], rar.at[c, 1], left)
        remote(part_of(1, HALF), RB.at[c, 0, pl.ds(HALF, HALF)], xps.at[c], rbr.at[c, 0], right)
        remote(part_of(3, 0), RB.at[c, 1, pl.ds(0, HALF)], xps.at[c], rbr.at[c, 1], left)
        send[:H, c * ROWS : (c + 1) * ROWS] = jnp.transpose(dact[...]).astype(BF16)

    def reduce_middle(c):
        xs = c % NSLOT
        for side, j, lo, dev in ((0, 1, 0, right), (1, 3, HALF, left)):
            wait_for(RA.at[c, side], rar.at[c, side])
            rows = slice(j * BLK + lo, j * BLK + lo + HALF)
            XP[xs, rows, :DA] = (XP[xs, rows, :DA].astype(F32) + RA[c, side].astype(F32)).astype(BF16)
            remote(
                XP.at[xs, pl.ds(j * BLK + lo, HALF), colsA], RB.at[c, side, pl.ds(lo, HALF)],
                xps.at[c], rbr.at[c, side], dev,
            )

    def reduce_end(c):
        xs = c % NSLOT
        wait_for(GPR.at[c, pl.ds(1, NX - 1)], gpr.at[c])
        total = GPS[c, 0].astype(F32)
        for k in range(1, NX):
            total += GPR[c, k].astype(F32)
        high = total.astype(BF16)
        low = (total - high.astype(F32)).astype(BF16)
        up = iota((MSG, PAD), 0) - iota((MSG, PAD), 1) * PAD
        gate_back = mm(hot(up == SLOT), high) + mm(hot(up == SLOT + 1), low)
        wait_for(RB.at[c, 0], rbr.at[c, 0])
        wait_for(RB.at[c, 1], rbr.at[c, 1])
        msg = slice(c * MSG, (c + 1) * MSG)
        for i in range(DA // TILE):
            cols = slice(i * TILE, (i + 1) * TILE)
            whole = XP[xs, :BLK, cols].astype(F32) + RB[c, 0, :, cols].astype(F32) + RB[c, 1, :, cols].astype(F32)
            out = mm(expand, whole.astype(BF16))
            if i == 0:
                recv[msg, :128] = (out[:, :128] + gate_back).astype(BF16)
                recv[msg, 128:TILE] = out[:, 128:].astype(BF16)
            else:
                recv[msg, cols] = out.astype(BF16)
        for d in range(B):
            rows = pl.ds((c * B + d) * PAD, PAD)
            if c or d:
                remote(recv.at[rows], back.at[rows], rets, backr.at[c], source(c, d))
        if c == 0:
            back[:PAD] = recv[:PAD]

    def b_sum():
        for c in range(C):
            lo = MB if c == 0 else 0
            if ROWS > lo:
                wait_for(backB.at[pl.ds(c * ROWS + lo, ROWS - lo)], bbr.at[c])
        wait_for(TB.at[pl.ds(0, 3 * T)], tbs)
        for i in range(DB // TILE):
            cols = slice(i * TILE, (i + 1) * TILE)
            TB[:, cols] = mm(selT[...], backB[:, cols]).astype(BF16)
        h = T // 2
        remote(TB.at[pl.ds(2 * T, h)], RAB.at[0], pbs, rabr.at[0], right)
        remote(TB.at[pl.ds(2 * T + h, h)], RAB.at[1], pbs, rabr.at[1], left)
        remote(TB.at[pl.ds(T + h, h)], RBB.at[0, pl.ds(h, h)], pbs, rbbr.at[0], right)
        remote(TB.at[pl.ds(3 * T, h)], RBB.at[1, pl.ds(0, h)], pbs, rbbr.at[1], left)

    def b_middle():
        h = T // 2
        for side, j, lo, dev in ((0, 1, 0, right), (1, 3, h, left)):
            wait_for(RAB.at[side], rabr.at[side])
            rows = slice(j * T + lo, j * T + lo + h)
            TB[rows, :] = (TB[rows, :].astype(F32) + RAB[side].astype(F32)).astype(BF16)
            remote(TB.at[pl.ds(j * T + lo, h)], RBB.at[side, pl.ds(lo, h)], pbs, rbbr.at[side], dev)

    def b_end():
        wait_for(RBB.at[0], rbbr.at[0])
        wait_for(RBB.at[1], rbbr.at[1])
        ig_ref[:, DA:] = (TB[:T].astype(F32) + RBB[0].astype(F32) + RBB[1].astype(F32)).astype(BF16)

    tiles = D // TILE

    def weight_grad(first, last):
        def out_copy(i, s):
            return pltpu.make_async_copy(
                dtile.at[s], dg_hbm.at[:, pl.ds(pl.multiple_of(i * TILE, TILE), TILE)], dsem.at[s]
            )

        def tile(i, _):
            s = i % 2

            @pl.when(i >= first + 2)
            def _():
                out_copy(i - 2, s).wait()

            cols = pl.ds(pl.multiple_of(i * TILE, TILE), TILE)
            dtile[s] = mm(send[:H, : C * ROWS], Y[:, cols]).astype(BF16)
            out_copy(i, s).start()
            return 0

        lax.fori_loop(first, last, tile, 0)
        for i in range(max(last - 2, first), last):
            out_copy(i, i % 2).wait()

    if C == 4:
        b_forward()
        gather_start(0)
        routes = b_routes()
        b_select(0, routes)
        gather_start(1)
        b_select(1, routes)
        gather_forward(0)
        sort_saved()
        gather_start(2)
        gather_forward(1)
        b_select(2, routes)
        gather_start(3)
        b_select(3, routes)
        compute(0)
        gather_forward(2)
        compute(1)
        gather_forward(3)
        reduce_middle(0)
        compute(2)
        reduce_end(0)
        reduce_middle(1)
        compute(3)
        reduce_end(1)
        reduce_middle(2)
        weight_grad(0, tiles // 2)
        b_sum()
        reduce_end(2)
        reduce_middle(3)
        b_middle()
        weight_grad(tiles // 2, tiles)
        reduce_end(3)
        b_end()
    else:
        b_forward()
        sort_saved()
        routes = b_routes()
        for c in range(C):
            b_select(c, routes)
            gather_start(c)
            gather_forward(c)
            compute(c)
            reduce_middle(c)
            reduce_end(c)
        b_sum()
        b_middle()
        b_end()
        weight_grad(0, tiles)

    for c in range(C):
        lo = PAD if c == 0 else 0
        if MSG > lo:
            wait_for(back.at[pl.ds(c * MSG + lo, MSG - lo)], backr.at[c])
    for i in range(DA // TILE):
        cols = slice(i * TILE, (i + 1) * TILE)
        ig_ref[:, cols] = mm(mt[...], back[:, cols]).astype(BF16)
    back_gates = jnp.transpose(back[:, :128].astype(F32)).astype(BF16)
    for k, (blk, rank) in enumerate(own):
        at = slots - blk * PAD
        found = mm(back_gates, hot((at == SLOT) | (at == SLOT + 1)))
        gg_ref[k : k + 1, :] = jnp.sum(jnp.where(lane_slot == rank, found, 0.0), axis=0, keepdims=True)

    wait_for(recv.at[pl.ds(0, C * MSG - PAD)], rets)
    wait_for(Y.at[pl.ds(0, C * 3 * BLK), colsA], ags)
    wait_for(IDS.at[pl.ds(1, NX - 1)], idss)
    wait_for(TB.at[pl.ds(0, 3 * T)], pbs)
    for c in range(C):
        wait_for(GB.at[c, pl.ds(1, NX - 1)], gbs)
        wait_for(GPS.at[c, pl.ds(1, NX - 1)], gps)
    for c in range(max(0, C - 2), C):
        lo = MB if c == 0 else 0
        if ROWS > lo:
            wait_for(sendB.at[c % 2, pl.ds(lo, ROWS - lo)], sbs.at[c % 2])
    for c in range(max(0, C - NSLOT), C):
        lo = MB if c == 0 else 0
        wait_for(XP.at[c % NSLOT, pl.ds(BLK, ROWS - BLK), colsA], xps.at[c])
        if ROWS > lo:
            wait_for(XP.at[c % NSLOT, pl.ds(lo, ROWS - lo), colsB], xpbs.at[c])


def body(out_grad, gates, expert_ids, saved_pre, w_gate_up, w_down):
    T, D = out_grad.shape
    B = lax.axis_size("node")
    C = lax.axis_size("local") // NX
    Q, SLOT = saved_pre.shape[1:3]
    H = w_down.shape[1]
    DA = split(D)
    DB = D - DA
    saved = jnp.transpose(saved_pre[0], (1, 0, 2))
    BLK, MSG = B * SLOT, B * PAD
    ROWS = NX * BLK
    NSLOT = min(3, C)
    vm = pl.BlockSpec(memory_space=pltpu.VMEM)
    anywhere = pl.BlockSpec(memory_space=pl.ANY)
    dma = pltpu.SemaphoreType.DMA
    ig, gg, dg = pl.pallas_call(
        functools.partial(kernel, B, C, SLOT),
        out_shape=(
            jax.ShapeDtypeStruct((T, D), BF16),
            jax.ShapeDtypeStruct((2, T), F32),
            jax.ShapeDtypeStruct((H, D), BF16),
        ),
        in_specs=[vm, vm, vm, anywhere, anywhere, anywhere],
        out_specs=(vm, vm, anywhere),
        scratch_shapes=[
            pltpu.VMEM((D, 2 * H), BF16),
            pltpu.VMEM((H, D), BF16),
            pltpu.VMEM((max(C * MSG, H), max(DA, C * ROWS)), BF16),
            pltpu.VMEM((C * MSG, DA), BF16),
            pltpu.VMEM((C * MSG, DA), BF16),
            pltpu.VMEM((C * ROWS, D), BF16),
            pltpu.VMEM((C, NX, PAD, 128), BF16),
            pltpu.VMEM((NSLOT, ROWS, D), BF16),
            pltpu.VMEM((C, 2, BLK // 2, DA), BF16),
            pltpu.VMEM((C, 2, BLK, DA), BF16),
            pltpu.VMEM((C, NX, PAD, 128), BF16),
            pltpu.VMEM((C, NX, PAD, 128), BF16),
            pltpu.VMEM((C * ROWS, 2 * H), BF16),
            pltpu.VMEM((2, H, TILE), BF16),
            pltpu.VMEM((T, C * MSG), BF16),
            pltpu.VMEM((ROWS, 2 * H), BF16),
            pltpu.VMEM((ROWS, H), F32),
            pltpu.VMEM((NX, 8, T), jnp.int32),
            pltpu.VMEM((NX * T, DB), BF16),
            pltpu.VMEM((2, ROWS, DB), BF16),
            pltpu.VMEM((C * ROWS, DB), BF16),
            pltpu.VMEM((2, T // 2, DB), BF16),
            pltpu.VMEM((2, T, DB), BF16),
            pltpu.VMEM((NX * T, C * ROWS), BF16),
            pltpu.VMEM((ROWS, ROWS), BF16),
            pltpu.VMEM((ROWS, ROWS), BF16),
            dma((2,)),
            dma((4,)),
            dma((2,)),
            dma,
            dma((C,)),
            dma,
            dma((C, 3)),
            dma,
            dma((C,)),
            dma((C,)),
            dma((C, 2)),
            dma((C, 2)),
            dma,
            dma((C,)),
            dma,
            dma((C,)),
            dma,
            dma,
            dma,
            dma((3,)),
            dma((2,)),
            dma((C,)),
            dma((C,)),
            dma((C,)),
            dma,
            dma((2,)),
            dma((2,)),
        ],
        compiler_params=pltpu.CompilerParams(
            collective_id=0, has_side_effects=True, vmem_limit_bytes=63 * 1024 * 1024
        ),
        cost_estimate=pl.CostEstimate(
            flops=2 * C * ROWS * D * 4 * H, bytes_accessed=25_000_000, transcendentals=C * ROWS * H
        ),
        name="moe_backward",
    )(expert_ids.T, gates.T, out_grad, saved, w_gate_up[0], w_down[0])
    return ig, gg.T, dg[None]


def solution(mesh):
    in_specs = (
        P(("node", "local"), None),
        P(("node", "local"), None),
        P(("node", "local"), None),
        P(("node", "local"), None, None, None),
        P(("node", "local"), None, None),
        P(("node", "local"), None, None),
    )
    out_specs = (
        P(("node", "local"), None),
        P(("node", "local"), None),
        P(("node", "local"), None, None),
    )
    return jax.shard_map(body, mesh=mesh, in_specs=in_specs, out_specs=out_specs, check_vma=False)
```

```python
import functools

import jax
import jax.numpy as jnp
from jax import lax
from jax.experimental import pallas as pl
from jax.experimental.pallas import tpu as pltpu
from jax.sharding import PartitionSpec as P

NX = 4
PAD = 16
TILE = 256
MESH = pl.DeviceIdType.MESH
F32 = jnp.float32
BF16 = jnp.bfloat16


def split(D):
    return max(TILE, 11 * D // 14 // TILE * TILE)


def iota(shape, dim):
    return lax.broadcasted_iota(jnp.int32, shape, dim)


def shr(v, bits):
    return lax.shift_right_logical(v, jnp.full(v.shape, bits, jnp.int32))


def log2(size):
    return size.bit_length() - 1


def mm(a, b):
    return jnp.dot(a, b, preferred_element_type=F32)


def mm_nt(a, b):
    return lax.dot_general(a, b, (((1,), (1,)), ((), ())), preferred_element_type=F32)


def hot(mask):
    return mask.astype(F32).astype(BF16)


def kernel(
    B, C, SLOT,
    ids_ref, gates_ref, og_ref, saved_hbm, wgu_hbm, wd_hbm,
    ig_ref, gg_ref, dg_hbm,
    wgu, wd, send, recv, back, Y, GB, XP, RA, RB, GPS, GPR, saved, dtile, mt, dpre, dact,
    IDS, TB, sendB, backB, RAB, RBB, selT, perm, permT,
    wsem, ssem, dsem, s1s, s1r, ags, agr, gbs, gbr, xps, rar, rbr, gps, gpr, rets, backr,
    idss, idsr, tbs, tbr, sbs, sbr, xpbs, bbr, pbs, rabr, rbbr,
):
    T, D = og_ref.shape
    H = wd.shape[0]
    DA = split(D)
    DB = D - DA
    BLK = B * SLOT
    HALF = BLK // 2
    MSG = B * PAD
    MB = NX * SLOT
    ROWS = NX * BLK
    NSLOT = XP.shape[0]
    LB, LC = log2(B), log2(C)
    colsA, colsB = pl.ds(0, DA), pl.ds(DA, DB)
    n = lax.axis_index("node")
    l = lax.axis_index("local")
    z, x = l // NX, l % NX
    right = (n, z * NX + (x + 1) % NX)
    left = (n, z * NX + (x + NX - 1) % NX)

    CORES = 2 if B > C else 1
    YS = B // CORES
    y, core = n // CORES, n % CORES
    LCO = log2(CORES)
    even = YS == C

    def offsets(c, d):
        return (d % C, (c + C - d % C) % C, d // C) if even else (c, d // CORES, d % CORES)

    def peer(c, d):
        dz, dy, dc = offsets(c, d)
        return (((y + dy) % YS) * CORES + (core + dc) % CORES, ((z + dz) % C) * NX + x)

    def source(c, d):
        dz, dy, dc = offsets(c, d)
        return (((y + YS - dy) % YS) * CORES + (core + CORES - dc) % CORES, ((z + C - dz) % C) * NX + x)

    def along(k):
        return (n, z * NX + (x + k) % NX)

    def remote(src, dst, ssem_, rsem_, dev):
        pltpu.make_async_remote_copy(
            src_ref=src, dst_ref=dst, send_sem=ssem_, recv_sem=rsem_, device_id=dev, device_id_type=MESH
        ).start()

    def wait_for(ref, sem):
        pltpu.make_async_copy(ref, ref, sem).wait()

    barrier = pltpu.get_barrier_semaphore()
    count = 0
    for k in range(1, NX):
        pl.semaphore_signal(barrier, inc=1, device_id=along(k), device_id_type=MESH)
        count += 1
    for c in range(C):
        for d in range(B):
            if c or d:
                pl.semaphore_signal(barrier, inc=1, device_id=peer(c, d), device_id_type=MESH)
                count += 1

    wd_copy = pltpu.make_async_copy(wd_hbm, wd, wsem.at[0])
    wgu_copy = pltpu.make_async_copy(wgu_hbm, wgu, wsem.at[1])

    Q = C * NX * B

    def staged(r):
        return NSLOT - 1, pl.ds(r // 2 % 2 * Q, Q), pl.ds(r % 2 * 2 * H, 2 * H)

    def stage(r):
        return pltpu.make_async_copy(saved_hbm.at[r], XP.at[staged(r)], ssem.at[r % 4])

    for r in range(4):
        stage(r).start()
    wd_copy.start()
    wgu_copy.start()

    IDS[0, :2] = ids_ref[...]
    TB[:T] = og_ref[:, DA:]
    NE = max(8, B * C)
    before = hot(iota((T, T), 0) < iota((T, T), 1))
    expert_row = iota((NE, T), 0)

    def route(ids):
        experts = [ids[k : k + 1] for k in range(2)]
        hits = [expert_row == e for e in experts]
        per_token = hits[0].astype(F32) + hits[1].astype(F32)
        earlier = mm(per_token.astype(BF16), before)
        out = []
        for k in range(2):
            rank = jnp.sum(jnp.where(hits[k], earlier, 0.0), axis=0, keepdims=True).astype(jnp.int32)
            zz = experts[k] & (C - 1)
            node = shr(experts[k], LC)
            dz = (zz - z + C) & (C - 1)
            dy = (shr(node, LCO) - y + YS) & (YS - 1)
            dc = (node - core + CORES) & (CORES - 1)
            blk = ((dy + dz) & (C - 1)) * B + dc * C + dz if even else dz * B + dy * CORES + dc
            out.append((blk, rank))
        return out

    own = route(ids_ref[...])
    slots = iota((C * MSG, T), 0)
    lane_slot = iota((128, T), 0)
    pick = jnp.zeros((C * MSG, T), F32)
    gate_rows = jnp.zeros((C * MSG, 128), F32)
    gates = gates_ref[...].astype(F32)
    for k, (blk, rank) in enumerate(own):
        pick += (slots == blk * PAD + rank).astype(F32)
        gate_at = jnp.where(lane_slot == rank, gates[k : k + 1], 0.0).astype(BF16)
        gate_rows += mm_nt(hot(slots == blk * PAD + SLOT), gate_at)
    mt[...] = jnp.transpose(pick).astype(BF16)
    pick = pick.astype(BF16)

    pl.semaphore_wait(barrier, count)

    for k in range(1, NX):
        remote(IDS.at[0], IDS.at[NX - k], idss, idsr, along(k))
    remote(TB.at[pl.ds(0, T)], TB.at[pl.ds(3 * T, T)], tbs, tbr.at[0], right)
    remote(TB.at[pl.ds(0, T)], TB.at[pl.ds(T, T)], tbs, tbr.at[1], left)

    for c in range(C):
        rows = slice(c * MSG, (c + 1) * MSG)
        for i in range(DA // TILE):
            cols = slice(i * TILE, (i + 1) * TILE)
            send[rows, cols] = mm(pick[rows], og_ref[:, cols]).astype(BF16)
        send[rows, :128] = (send[rows, :128].astype(F32) + gate_rows[rows]).astype(BF16)
        for d in range(B):
            at = pl.ds((c * B + d) * PAD, PAD)
            if c or d:
                remote(send.at[at, colsA], recv.at[at], s1s, s1r.at[c], peer(c, d))
    recv[:PAD] = send[:PAD, :DA]

    def row_parts(i):
        j = jnp.zeros(i.shape, jnp.int32)
        for k in range(1, NX):
            j += (i >= k * BLK).astype(jnp.int32)
        rest = i - j * BLK
        return j, shr(rest, LB), rest & (B - 1)

    _, r_i, d_i = row_parts(iota((BLK, MSG), 0))
    compact = hot(iota((BLK, MSG), 1) == d_i * PAD + r_i)
    _, r_l, d_l = row_parts(iota((MSG, BLK), 1))
    expand = hot(iota((MSG, BLK), 0) == d_l * PAD + r_l)
    gate_pick = hot(iota((PAD, MSG), 1) == iota((PAD, MSG), 0) * PAD + SLOT)
    of_source = hot((iota((BLK, PAD), 0) & (B - 1)) == iota((BLK, PAD), 1))
    by_source = hot((iota((PAD, BLK), 1) & (B - 1)) == iota((PAD, BLK), 0))
    slot_mask = iota((BLK, 128), 1) == shr(iota((BLK, 128), 0), LB)
    j_i, r_i, d_i = row_parts(iota((ROWS, ROWS), 0))
    perm[...] = hot(iota((ROWS, ROWS), 1) == d_i * MB + j_i * SLOT + r_i)
    j_l, r_l, d_l = row_parts(iota((ROWS, ROWS), 1))
    permT[...] = hot(iota((ROWS, ROWS), 0) == d_l * MB + j_l * SLOT + r_l)

    def sort_saved():
        row, col = iota((Q, Q), 0), iota((Q, Q), 1)
        cc, jj, dd = shr(row, LB + 2), shr(row, LB) & (NX - 1), row & (B - 1)
        if even:
            dz, dc = dd & (C - 1), shr(dd, LC)
            dy = (cc + C - dz) & (C - 1)
        else:
            dz, dy, dc = cc, shr(dd, LCO), dd & (CORES - 1)
        node = ((y + YS - dy) & (YS - 1)) * CORES + ((core + CORES - dc) & (CORES - 1))
        q = node * (C * NX) + ((z + C - dz) & (C - 1)) * NX + ((x + jj) & (NX - 1))
        order = hot(col == q)
        for p in range(SLOT // 2):
            stage(2 * p).wait()
            stage(2 * p + 1).wait()
            pair = [mm(order, XP[staged(2 * p + h)]) for h in range(2)]
            for g in range(C * NX):
                both = jnp.concatenate([v[g * B : (g + 1) * B] for v in pair], axis=0)
                saved[g * BLK + 2 * B * p : g * BLK + 2 * B * (p + 1), :] = both.astype(BF16)
            if p + 2 < SLOT // 2:
                stage(2 * p + 4).start()
                stage(2 * p + 5).start()

    def b_forward():
        h = T // 2
        wait_for(TB.at[pl.ds(3 * T, T)], tbr.at[0])
        remote(TB.at[pl.ds(3 * T, h)], TB.at[pl.ds(2 * T, h)], tbs, tbr.at[2], right)
        wait_for(TB.at[pl.ds(T, T)], tbr.at[1])
        remote(TB.at[pl.ds(T + h, h)], TB.at[pl.ds(2 * T + h, h)], tbs, tbr.at[2], left)

    def b_routes():
        wait_for(IDS.at[pl.ds(1, NX - 1)], idsr)
        return [own] + [route(IDS[j, :2]) for j in range(1, NX)]

    def b_part(ref, c, lead):
        lo = MB if c == 0 else 0
        return ref.at[lead, pl.ds(lo, ROWS - lo)] if lead is not None else ref.at[pl.ds(lo, ROWS - lo)]

    def b_select(c, routes):
        slot = c % 2
        at = iota((ROWS, T), 0)
        parts = []
        for j in range(NX):
            part = jnp.zeros((ROWS, T), F32)
            for blk, rank in routes[j]:
                part += (at == (blk - c * B) * MB + j * SLOT + rank).astype(F32)
            parts.append(part)
            selT[j * T : (j + 1) * T, c * ROWS : (c + 1) * ROWS] = jnp.transpose(part).astype(BF16)
        sel = jnp.concatenate(parts, axis=1).astype(BF16)
        if c == 0:
            wait_for(TB.at[pl.ds(2 * T, T)], tbr.at[2])
        if c >= 2 and (B > 1 or c > 2):
            wait_for(b_part(sendB, c - 2, slot), sbs.at[slot])
        for i in range(DB // TILE):
            cols = slice(i * TILE, (i + 1) * TILE)
            sendB[slot, :, cols] = mm(sel, TB[:, cols]).astype(BF16)
        for d in range(B):
            if c or d:
                remote(
                    sendB.at[slot, pl.ds(d * MB, MB)], Y.at[pl.ds(c * ROWS + d * MB, MB), colsB],
                    sbs.at[slot], sbr.at[c], peer(c, d),
                )
            else:
                Y[:MB, DA:] = sendB[slot, :MB]

    def b_land(c):
        lo = MB if c == 0 else 0
        if ROWS > lo:
            wait_for(Y.at[pl.ds(c * ROWS + lo, ROWS - lo), colsB], sbr.at[c])
        rows = slice(c * ROWS, (c + 1) * ROWS)
        for i in range(DB // TILE):
            cols = slice(DA + i * TILE, DA + (i + 1) * TILE)
            Y[rows, cols] = mm(perm[...], Y[rows, cols]).astype(BF16)

    def yrows(c, j, lo=0, size=None):
        return pl.ds(c * ROWS + j * BLK + lo, BLK if size is None else size)

    def gather_start(c):
        lo = PAD if c == 0 else 0
        if MSG > lo:
            wait_for(recv.at[pl.ds(c * MSG + lo, MSG - lo)], s1r.at[c])
        own_rows = slice(c * ROWS, c * ROWS + BLK)
        for i in range(DA // TILE):
            cols = slice(i * TILE, (i + 1) * TILE)
            Y[own_rows, cols] = mm(compact, recv[c * MSG : (c + 1) * MSG, cols]).astype(BF16)
        GB[c, 0] = mm(gate_pick, recv[c * MSG : (c + 1) * MSG, :128]).astype(BF16)
        remote(Y.at[yrows(c, 0), colsA], Y.at[yrows(c, 3), colsA], ags, agr.at[c, 0], right)
        remote(Y.at[yrows(c, 0), colsA], Y.at[yrows(c, 1), colsA], ags, agr.at[c, 1], left)
        for k in range(1, NX):
            remote(GB.at[c, 0], GB.at[c, NX - k], gbs, gbr.at[c], along(k))

    def gather_forward(c):
        wait_for(Y.at[yrows(c, 3), colsA], agr.at[c, 0])
        remote(Y.at[yrows(c, 3, 0, HALF), colsA], Y.at[yrows(c, 2, 0, HALF), colsA], ags, agr.at[c, 2], right)
        wait_for(Y.at[yrows(c, 1), colsA], agr.at[c, 1])
        remote(Y.at[yrows(c, 1, HALF, HALF), colsA], Y.at[yrows(c, 2, HALF, HALF), colsA], ags, agr.at[c, 2], left)

    def compute(c):
        xs = c % NSLOT
        wait_for(Y.at[yrows(c, 2), colsA], agr.at[c, 2])
        wait_for(GB.at[c, pl.ds(1, NX - 1)], gbr.at[c])
        b_land(c)
        if c == 0:
            wd_copy.wait()
            wait_for(send.at[pl.ds(0, C * MSG - PAD), colsA], s1s)
        NT = min(TILE, H)
        for i in range(H // NT):
            dact[:, i * NT : (i + 1) * NT] = mm_nt(Y[c * ROWS : (c + 1) * ROWS, :], wd[i * NT : (i + 1) * NT, :])
        for j in range(NX):
            rows = slice(j * BLK, (j + 1) * BLK)
            at = c * ROWS + j * BLK
            a = saved[at : at + BLK, :H].astype(F32)
            b = saved[at : at + BLK, H:].astype(F32)
            da = dact[rows, :]
            spread = mm(of_source, GB[c, j])
            scale = jnp.sum(jnp.where(slot_mask, spread, 0.0), axis=1, keepdims=True)
            s = jax.nn.sigmoid(a)
            act = a * s
            hidden = act * b
            part = jnp.sum(hidden * da, axis=1, keepdims=True)
            parts = jnp.where(slot_mask, part, 0.0).astype(BF16)
            GPS[c, j] = mm(by_source, parts).astype(BF16)
            dh = scale * da
            dpre[rows, :H] = (dh * b * s * (1.0 + a * (1.0 - s))).astype(BF16)
            dpre[rows, H:] = (dh * act).astype(BF16)
            dact[rows, :] = scale * hidden
        for k in range(1, NX):
            remote(GPS.at[c, k], GPR.at[c, NX - k], gps, gpr.at[c], along(k))
        if c == 0:
            wgu_copy.wait()
        if c >= NSLOT:
            o = c - NSLOT
            wait_for(XP.at[xs, pl.ds(BLK, ROWS - BLK), colsA], xps.at[o])
            lo = MB if o == 0 else 0
            if ROWS > lo:
                wait_for(XP.at[xs, pl.ds(lo, ROWS - lo), colsB], xpbs.at[o])

        def tile_b(i, _):
            cols = pl.ds(pl.multiple_of(DA + i * TILE, TILE), TILE)
            XP[xs, :, cols] = mm(permT[...], mm_nt(dpre[...], wgu[cols, :]).astype(BF16)).astype(BF16)
            return 0

        lax.fori_loop(0, DB // TILE, tile_b, 0)
        for d in range(B):
            rows = pl.ds(d * MB, MB)
            if c or d:
                remote(
                    XP.at[xs, rows, colsB], backB.at[pl.ds((c * B + d) * MB, MB)],
                    xpbs.at[c], bbr.at[c], source(c, d),
                )
            else:
                backB[:MB] = XP[xs, :MB, DA:]

        def tile_a(i, _):
            cols = pl.ds(pl.multiple_of(i * TILE, TILE), TILE)
            XP[xs, :, cols] = mm_nt(dpre[...], wgu[cols, :]).astype(BF16)
            return 0

        lax.fori_loop(0, DA // TILE, tile_a, 0)

        def part_of(j, lo):
            return XP.at[xs, pl.ds(j * BLK + lo, HALF), colsA]

        remote(part_of(2, 0), RA.at[c, 0], xps.at[c], rar.at[c, 0], right)
        remote(part_of(2, HALF), RA.at[c, 1], xps.at[c], rar.at[c, 1], left)
        remote(part_of(1, HALF), RB.at[c, 0, pl.ds(HALF, HALF)], xps.at[c], rbr.at[c, 0], right)
        remote(part_of(3, 0), RB.at[c, 1, pl.ds(0, HALF)], xps.at[c], rbr.at[c, 1], left)
        send[:H, c * ROWS : (c + 1) * ROWS] = jnp.transpose(dact[...]).astype(BF16)

    def reduce_middle(c):
        xs = c % NSLOT
        for side, j, lo, dev in ((0, 1, 0, right), (1, 3, HALF, left)):
            wait_for(RA.at[c, side], rar.at[c, side])
            rows = slice(j * BLK + lo, j * BLK + lo + HALF)
            XP[xs, rows, :DA] = (XP[xs, rows, :DA].astype(F32) + RA[c, side].astype(F32)).astype(BF16)
            remote(
                XP.at[xs, pl.ds(j * BLK + lo, HALF), colsA], RB.at[c, side, pl.ds(lo, HALF)],
                xps.at[c], rbr.at[c, side], dev,
            )

    def reduce_end(c):
        xs = c % NSLOT
        wait_for(GPR.at[c, pl.ds(1, NX - 1)], gpr.at[c])
        total = GPS[c, 0].astype(F32)
        for k in range(1, NX):
            total += GPR[c, k].astype(F32)
        high = total.astype(BF16)
        low = (total - high.astype(F32)).astype(BF16)
        up = iota((MSG, PAD), 0) - iota((MSG, PAD), 1) * PAD
        gate_back = mm(hot(up == SLOT), high) + mm(hot(up == SLOT + 1), low)
        wait_for(RB.at[c, 0], rbr.at[c, 0])
        wait_for(RB.at[c, 1], rbr.at[c, 1])
        msg = slice(c * MSG, (c + 1) * MSG)
        for i in range(DA // TILE):
            cols = slice(i * TILE, (i + 1) * TILE)
            whole = XP[xs, :BLK, cols].astype(F32) + RB[c, 0, :, cols].astype(F32) + RB[c, 1, :, cols].astype(F32)
            out = mm(expand, whole.astype(BF16))
            if i == 0:
                recv[msg, :128] = (out[:, :128] + gate_back).astype(BF16)
                recv[msg, 128:TILE] = out[:, 128:].astype(BF16)
            else:
                recv[msg, cols] = out.astype(BF16)
        for d in range(B):
            rows = pl.ds((c * B + d) * PAD, PAD)
            if c or d:
                remote(recv.at[rows], back.at[rows], rets, backr.at[c], source(c, d))
        if c == 0:
            back[:PAD] = recv[:PAD]

    def b_sum():
        for c in range(C):
            lo = MB if c == 0 else 0
            if ROWS > lo:
                wait_for(backB.at[pl.ds(c * ROWS + lo, ROWS - lo)], bbr.at[c])
        wait_for(TB.at[pl.ds(0, 3 * T)], tbs)
        for i in range(DB // TILE):
            cols = slice(i * TILE, (i + 1) * TILE)
            TB[:, cols] = mm(selT[...], backB[:, cols]).astype(BF16)
        h = T // 2
        remote(TB.at[pl.ds(2 * T, h)], RAB.at[0], pbs, rabr.at[0], right)
        remote(TB.at[pl.ds(2 * T + h, h)], RAB.at[1], pbs, rabr.at[1], left)
        remote(TB.at[pl.ds(T + h, h)], RBB.at[0, pl.ds(h, h)], pbs, rbbr.at[0], right)
        remote(TB.at[pl.ds(3 * T, h)], RBB.at[1, pl.ds(0, h)], pbs, rbbr.at[1], left)

    def b_middle():
        h = T // 2
        for side, j, lo, dev in ((0, 1, 0, right), (1, 3, h, left)):
            wait_for(RAB.at[side], rabr.at[side])
            rows = slice(j * T + lo, j * T + lo + h)
            TB[rows, :] = (TB[rows, :].astype(F32) + RAB[side].astype(F32)).astype(BF16)
            remote(TB.at[pl.ds(j * T + lo, h)], RBB.at[side, pl.ds(lo, h)], pbs, rbbr.at[side], dev)

    def b_end():
        wait_for(RBB.at[0], rbbr.at[0])
        wait_for(RBB.at[1], rbbr.at[1])
        ig_ref[:, DA:] = (TB[:T].astype(F32) + RBB[0].astype(F32) + RBB[1].astype(F32)).astype(BF16)

    tiles = D // TILE

    def weight_grad(first, last):
        def out_copy(i, s):
            return pltpu.make_async_copy(
                dtile.at[s], dg_hbm.at[:, pl.ds(pl.multiple_of(i * TILE, TILE), TILE)], dsem.at[s]
            )

        def tile(i, _):
            s = i % 2

            @pl.when(i >= first + 2)
            def _():
                out_copy(i - 2, s).wait()

            cols = pl.ds(pl.multiple_of(i * TILE, TILE), TILE)
            dtile[s] = mm(send[:H, : C * ROWS], Y[:, cols]).astype(BF16)
            out_copy(i, s).start()
            return 0

        lax.fori_loop(first, last, tile, 0)
        for i in range(max(last - 2, first), last):
            out_copy(i, i % 2).wait()

    if C == 4:
        b_forward()
        gather_start(0)
        routes = b_routes()
        b_select(0, routes)
        gather_start(1)
        b_select(1, routes)
        gather_forward(0)
        sort_saved()
        gather_start(2)
        gather_forward(1)
        b_select(2, routes)
        gather_start(3)
        b_select(3, routes)
        compute(0)
        gather_forward(2)
        compute(1)
        gather_forward(3)
        reduce_middle(0)
        compute(2)
        reduce_end(0)
        reduce_middle(1)
        compute(3)
        reduce_end(1)
        reduce_middle(2)
        weight_grad(0, tiles // 2)
        b_sum()
        reduce_end(2)
        reduce_middle(3)
        b_middle()
        weight_grad(tiles // 2, tiles)
        reduce_end(3)
        b_end()
    else:
        b_forward()
        sort_saved()
        routes = b_routes()
        for c in range(C):
            b_select(c, routes)
            gather_start(c)
            gather_forward(c)
            compute(c)
            reduce_middle(c)
            reduce_end(c)
        b_sum()
        b_middle()
        b_end()
        weight_grad(0, tiles)

    for c in range(C):
        lo = PAD if c == 0 else 0
        if MSG > lo:
            wait_for(back.at[pl.ds(c * MSG + lo, MSG - lo)], backr.at[c])
    for i in range(DA // TILE):
        cols = slice(i * TILE, (i + 1) * TILE)
        ig_ref[:, cols] = mm(mt[...], back[:, cols]).astype(BF16)
    back_gates = jnp.transpose(back[:, :128].astype(F32)).astype(BF16)
    for k, (blk, rank) in enumerate(own):
        at = slots - blk * PAD
        found = mm(back_gates, hot((at == SLOT) | (at == SLOT + 1)))
        gg_ref[k : k + 1, :] = jnp.sum(jnp.where(lane_slot == rank, found, 0.0), axis=0, keepdims=True)

    wait_for(recv.at[pl.ds(0, C * MSG - PAD)], rets)
    wait_for(Y.at[pl.ds(0, C * 3 * BLK), colsA], ags)
    wait_for(IDS.at[pl.ds(1, NX - 1)], idss)
    wait_for(TB.at[pl.ds(0, 3 * T)], pbs)
    for c in range(C):
        wait_for(GB.at[c, pl.ds(1, NX - 1)], gbs)
        wait_for(GPS.at[c, pl.ds(1, NX - 1)], gps)
    for c in range(max(0, C - 2), C):
        lo = MB if c == 0 else 0
        if ROWS > lo:
            wait_for(sendB.at[c % 2, pl.ds(lo, ROWS - lo)], sbs.at[c % 2])
    for c in range(max(0, C - NSLOT), C):
        lo = MB if c == 0 else 0
        wait_for(XP.at[c % NSLOT, pl.ds(BLK, ROWS - BLK), colsA], xps.at[c])
        if ROWS > lo:
            wait_for(XP.at[c % NSLOT, pl.ds(lo, ROWS - lo), colsB], xpbs.at[c])


def body(out_grad, gates, expert_ids, saved_pre, w_gate_up, w_down):
    T, D = out_grad.shape
    B = lax.axis_size("node")
    C = lax.axis_size("local") // NX
    Q, SLOT = saved_pre.shape[1:3]
    H = w_down.shape[1]
    DA = split(D)
    DB = D - DA
    saved = jnp.transpose(saved_pre[0], (1, 0, 2))
    BLK, MSG = B * SLOT, B * PAD
    ROWS = NX * BLK
    NSLOT = min(3, C)
    vm = pl.BlockSpec(memory_space=pltpu.VMEM)
    anywhere = pl.BlockSpec(memory_space=pl.ANY)
    dma = pltpu.SemaphoreType.DMA
    ig, gg, dg = pl.pallas_call(
        functools.partial(kernel, B, C, SLOT),
        out_shape=(
            jax.ShapeDtypeStruct((T, D), BF16),
            jax.ShapeDtypeStruct((2, T), F32),
            jax.ShapeDtypeStruct((H, D), BF16),
        ),
        in_specs=[vm, vm, vm, anywhere, anywhere, anywhere],
        out_specs=(vm, vm, anywhere),
        scratch_shapes=[
            pltpu.VMEM((D, 2 * H), BF16),
            pltpu.VMEM((H, D), BF16),
            pltpu.VMEM((max(C * MSG, H), max(DA, C * ROWS)), BF16),
            pltpu.VMEM((C * MSG, DA), BF16),
            pltpu.VMEM((C * MSG, DA), BF16),
            pltpu.VMEM((C * ROWS, D), BF16),
            pltpu.VMEM((C, NX, PAD, 128), BF16),
            pltpu.VMEM((NSLOT, ROWS, D), BF16),
            pltpu.VMEM((C, 2, BLK // 2, DA), BF16),
            pltpu.VMEM((C, 2, BLK, DA), BF16),
            pltpu.VMEM((C, NX, PAD, 128), BF16),
            pltpu.VMEM((C, NX, PAD, 128), BF16),
            pltpu.VMEM((C * ROWS, 2 * H), BF16),
            pltpu.VMEM((2, H, TILE), BF16),
            pltpu.VMEM((T, C * MSG), BF16),
            pltpu.VMEM((ROWS, 2 * H), BF16),
            pltpu.VMEM((ROWS, H), F32),
            pltpu.VMEM((NX, 8, T), jnp.int32),
            pltpu.VMEM((NX * T, DB), BF16),
            pltpu.VMEM((2, ROWS, DB), BF16),
            pltpu.VMEM((C * ROWS, DB), BF16),
            pltpu.VMEM((2, T // 2, DB), BF16),
            pltpu.VMEM((2, T, DB), BF16),
            pltpu.VMEM((NX * T, C * ROWS), BF16),
            pltpu.VMEM((ROWS, ROWS), BF16),
            pltpu.VMEM((ROWS, ROWS), BF16),
            dma((2,)),
            dma((4,)),
            dma((2,)),
            dma,
            dma((C,)),
            dma,
            dma((C, 3)),
            dma,
            dma((C,)),
            dma((C,)),
            dma((C, 2)),
            dma((C, 2)),
            dma,
            dma((C,)),
            dma,
            dma((C,)),
            dma,
            dma,
            dma,
            dma((3,)),
            dma((2,)),
            dma((C,)),
            dma((C,)),
            dma((C,)),
            dma,
            dma((2,)),
            dma((2,)),
        ],
        compiler_params=pltpu.CompilerParams(
            collective_id=0, has_side_effects=True, vmem_limit_bytes=63 * 1024 * 1024
        ),
        cost_estimate=pl.CostEstimate(
            flops=2 * C * ROWS * D * 4 * H, bytes_accessed=25_000_000, transcendentals=C * ROWS * H
        ),
        name="moe_backward",
    )(expert_ids.T, gates.T, out_grad, saved, w_gate_up[0], w_down[0])
    return ig, gg.T, dg[None]


def solution(mesh):
    in_specs = (
        P(("node", "local"), None),
        P(("node", "local"), None),
        P(("node", "local"), None),
        P(("node", "local"), None, None, None),
        P(("node", "local"), None, None),
        P(("node", "local"), None, None),
    )
    out_specs = (
        P(("node", "local"), None),
        P(("node", "local"), None),
        P(("node", "local"), None, None),
    )
    return jax.shard_map(body, mesh=mesh, in_specs=in_specs, out_specs=out_specs, check_vma=False)
```

```python
import functools

import jax
import jax.numpy as jnp
from jax import lax
from jax.experimental import pallas as pl
from jax.experimental.pallas import tpu as pltpu
from jax.sharding import PartitionSpec as P

NX = 4
PAD = 16
TILE = 256
MESH = pl.DeviceIdType.MESH
F32 = jnp.float32
BF16 = jnp.bfloat16


def split(D):
    return max(TILE, 11 * D // 14 // TILE * TILE)


def iota(shape, dim):
    return lax.broadcasted_iota(jnp.int32, shape, dim)


def shr(v, bits):
    return lax.shift_right_logical(v, jnp.full(v.shape, bits, jnp.int32))


def log2(size):
    return size.bit_length() - 1


def mm(a, b):
    return jnp.dot(a, b, preferred_element_type=F32)


def mm_nt(a, b):
    return lax.dot_general(a, b, (((1,), (1,)), ((), ())), preferred_element_type=F32)


def hot(mask):
    return mask.astype(F32).astype(BF16)


def plan(B, C):
    cores = 2 if B > C else 1
    even = B // cores == C
    chunks = C * cores if even else C
    return cores, chunks, B * C // chunks, even


def kernel(
    B, C, SLOT, NSLOT,
    ids_ref, gates_ref, og_hbm, saved_hbm, wgu_hbm, wd_hbm,
    ig_ref, gg_ref, dg_ref,
    og_ref, wgu, send, recv, back, Y, GB, XP, RA, RB, GPS, GPR, saved, mt, dpre, dact,
    IDS, TB, sendB, backB, RAB, RBB, selT, perm, permT,
    wsem, ssem, s1s, s1r, ags, agr, gbs, gbr, xps, rar, rbr, gps, gpr, rets, backr,
    idss, idsr, tbs, tbr, sbs, sbr, xpbs, bbr, pbs, rabr, rbbr,
):
    T, D = og_ref.shape
    H = dg_ref.shape[0]
    wd = dg_ref
    DA = split(D)
    DB = D - DA
    CORES, K, G, even = plan(B, C)
    BLK = G * SLOT
    MSG = G * PAD
    MB = NX * SLOT
    ROWS = NX * BLK
    NSB = sendB.shape[0]
    LG, LC = log2(G), log2(C)
    colsA, colsB = pl.ds(0, DA), pl.ds(DA, DB)
    n = lax.axis_index("node")
    l = lax.axis_index("local")
    z, x = l // NX, l % NX
    right = (n, z * NX + (x + 1) % NX)
    left = (n, z * NX + (x + NX - 1) % NX)

    YS = B // CORES
    y, core = n // CORES, n % CORES
    LCO = log2(CORES)

    def offsets(c, d):
        return (d, (c // CORES + C - d) % C, c % CORES) if even else (c, d // CORES, d % CORES)

    def peer(c, d):
        dz, dy, dc = offsets(c, d)
        return (((y + dy) % YS) * CORES + (core + dc) % CORES, ((z + dz) % C) * NX + x)

    def source(c, d):
        dz, dy, dc = offsets(c, d)
        return (((y + YS - dy) % YS) * CORES + (core + CORES - dc) % CORES, ((z + C - dz) % C) * NX + x)

    def along(k):
        return (n, z * NX + (x + k) % NX)

    def remote(src, dst, ssem_, rsem_, dev):
        pltpu.make_async_remote_copy(
            src_ref=src, dst_ref=dst, send_sem=ssem_, recv_sem=rsem_, device_id=dev, device_id_type=MESH
        ).start()

    def wait_for(ref, sem):
        pltpu.make_async_copy(ref, ref, sem).wait()

    barrier = pltpu.get_barrier_semaphore()
    count = 0
    for k in range(1, NX):
        pl.semaphore_signal(barrier, inc=1, device_id=along(k), device_id_type=MESH)
        count += 1
    for c in range(K):
        for d in range(G):
            if c or d:
                pl.semaphore_signal(barrier, inc=1, device_id=peer(c, d), device_id_type=MESH)
                count += 1

    wd_copy = pltpu.make_async_copy(wd_hbm, wd, wsem.at[0])
    wgu_copy = pltpu.make_async_copy(wgu_hbm, wgu, wsem.at[1])

    Q = C * NX * B
    QUADS = SLOT // 4
    first_row = NSLOT * ROWS - 4 * Q

    def stage(r):
        dst = XP.at[pl.ds(first_row + r % 4 * Q, Q), pl.ds(r // 4 * 2 * H, 2 * H)]
        return pltpu.make_async_copy(saved_hbm.at[r], dst, ssem)

    og_copy = pltpu.make_async_copy(og_hbm, og_ref, wsem.at[2])
    og_copy.start()
    for r in range(SLOT):
        stage(r).start()
    wd_copy.start()
    wgu_copy.start()

    IDS[0, :2] = ids_ref[...]
    NE = max(8, B * C)
    before = hot(iota((T, T), 0) < iota((T, T), 1))
    expert_row = iota((NE, T), 0)

    def route(ids):
        experts = [ids[k : k + 1] for k in range(2)]
        hits = [expert_row == e for e in experts]
        per_token = hits[0].astype(F32) + hits[1].astype(F32)
        earlier = mm(per_token.astype(BF16), before)
        out = []
        for k in range(2):
            rank = jnp.sum(jnp.where(hits[k], earlier, 0.0), axis=0, keepdims=True).astype(jnp.int32)
            zz = experts[k] & (C - 1)
            node = shr(experts[k], LC)
            dz = (zz - z + C) & (C - 1)
            dy = (shr(node, LCO) - y + YS) & (YS - 1)
            dc = (node - core + CORES) & (CORES - 1)
            blk = (((dy + dz) & (C - 1)) * CORES + dc) * G + dz if even else dz * G + dy * CORES + dc
            out.append((blk, rank))
        return out

    own = route(ids_ref[...])
    slots = iota((K * MSG, T), 0)
    lane_slot = iota((128, T), 0)
    pick = jnp.zeros((K * MSG, T), F32)
    gate_rows = jnp.zeros((K * MSG, 128), F32)
    gates = gates_ref[...].astype(F32)
    for k, (blk, rank) in enumerate(own):
        pick += (slots == blk * PAD + rank).astype(F32)
        gate_at = jnp.where(lane_slot == rank, gates[k : k + 1], 0.0).astype(BF16)
        gate_rows += mm_nt(hot(slots == blk * PAD + SLOT), gate_at)
    mt[...] = jnp.transpose(pick).astype(BF16)
    pick = pick.astype(BF16)
    og_copy.wait()
    TB[:T] = og_ref[:, DA:]

    pl.semaphore_wait(barrier, count)

    for k in range(1, NX):
        remote(IDS.at[0], IDS.at[NX - k], idss, idsr, along(k))
    remote(TB.at[pl.ds(0, T)], TB.at[pl.ds(3 * T, T)], tbs, tbr.at[0], right)
    remote(TB.at[pl.ds(0, T)], TB.at[pl.ds(T, T)], tbs, tbr.at[1], left)

    HEAD = K // 4 if K >= 4 else K
    for g in range(0, K, HEAD):
        rows = slice(g * MSG, (g + HEAD) * MSG)
        for i in range(DA // TILE):
            cols = slice(i * TILE, (i + 1) * TILE)
            send[rows, cols] = mm(pick[rows], og_ref[:, cols]).astype(BF16)
        send[rows, :128] = (send[rows, :128].astype(F32) + gate_rows[rows]).astype(BF16)
        for c in range(g, g + HEAD):
            for d in range(G):
                at = pl.ds((c * G + d) * PAD, PAD)
                if c or d:
                    remote(send.at[at, colsA], recv.at[at], s1s, s1r.at[c], peer(c, d))
    recv[:PAD] = send[:PAD, :DA]

    def row_parts(i):
        j = jnp.zeros(i.shape, jnp.int32)
        for k in range(1, NX):
            j += (i >= k * BLK).astype(jnp.int32)
        rest = i - j * BLK
        return j, shr(rest, LG), rest & (G - 1)

    _, r_i, d_i = row_parts(iota((BLK, MSG), 0))
    compact = hot(iota((BLK, MSG), 1) == d_i * PAD + r_i)
    _, r_l, d_l = row_parts(iota((MSG, BLK), 1))
    expand = hot(iota((MSG, BLK), 0) == d_l * PAD + r_l)
    gate_pick = hot(iota((PAD, MSG), 1) == iota((PAD, MSG), 0) * PAD + SLOT)
    of_source = hot((iota((BLK, PAD), 0) & (G - 1)) == iota((BLK, PAD), 1))
    by_source = hot((iota((PAD, BLK), 1) & (G - 1)) == iota((PAD, BLK), 0))
    slot_mask = iota((BLK, 128), 1) == shr(iota((BLK, 128), 0), LG)
    j_i, r_i, d_i = row_parts(iota((ROWS, ROWS), 0))
    perm[...] = hot(iota((ROWS, ROWS), 1) == d_i * MB + j_i * SLOT + r_i)
    j_l, r_l, d_l = row_parts(iota((ROWS, ROWS), 1))
    permT[...] = hot(iota((ROWS, ROWS), 0) == d_l * MB + j_l * SLOT + r_l)

    def sort_saved():
        row, col = iota((K * NX * 4 * G, 4 * Q), 0), iota((K * NX * 4 * G, 4 * Q), 1)
        r, d, j, c = shr(row, LG) & 3, row & (G - 1), shr(row, LG + 2) & (NX - 1), shr(row, LG + 4)
        if even:
            dz, dc = d, c & (CORES - 1)
            dy = (shr(c, LCO) + C - dz) & (C - 1)
        else:
            dz, dy, dc = c, shr(d, LCO), d & (CORES - 1)
        node = ((y + YS - dy) & (YS - 1)) * CORES + ((core + CORES - dc) & (CORES - 1))
        q = node * (C * NX) + ((z + C - dz) & (C - 1)) * NX + ((x + j) & (NX - 1))
        order = hot(col == r * Q + q)
        wait_for(XP.at[pl.ds(first_row, 4 * Q), pl.ds(0, QUADS * 2 * H)], ssem)
        NS = min(TILE, 2 * H)
        for p in range(QUADS):
            for i in range(2 * H // NS):
                cols = slice(p * 2 * H + i * NS, p * 2 * H + (i + 1) * NS)
                out = mm(order, XP[first_row : first_row + 4 * Q, cols]).astype(BF16)
                for g in range(K * NX):
                    at = g * BLK + p * 4 * G
                    saved[at : at + 4 * G, i * NS : (i + 1) * NS] = out[g * 4 * G : (g + 1) * 4 * G]

    def b_forward():
        h = T // 2
        wait_for(TB.at[pl.ds(3 * T, T)], tbr.at[0])
        remote(TB.at[pl.ds(3 * T, h)], TB.at[pl.ds(2 * T, h)], tbs, tbr.at[2], right)
        wait_for(TB.at[pl.ds(T, T)], tbr.at[1])
        remote(TB.at[pl.ds(T + h, h)], TB.at[pl.ds(2 * T + h, h)], tbs, tbr.at[2], left)

    def b_routes():
        wait_for(IDS.at[pl.ds(1, NX - 1)], idsr)
        return [own] + [route(IDS[j, :2]) for j in range(1, NX)]

    def b_part(ref, c, lead):
        lo = MB if c == 0 else 0
        return ref.at[lead, pl.ds(lo, ROWS - lo)] if lead is not None else ref.at[pl.ds(lo, ROWS - lo)]

    def b_select(c, routes):
        slot = c % NSB
        at = iota((ROWS, T), 0)
        parts = []
        for j in range(NX):
            part = jnp.zeros((ROWS, T), F32)
            for blk, rank in routes[j]:
                part += (at == (blk - c * G) * MB + j * SLOT + rank).astype(F32)
            parts.append(part)
            selT[j * T : (j + 1) * T, c * ROWS : (c + 1) * ROWS] = jnp.transpose(part).astype(BF16)
        sel = jnp.concatenate(parts, axis=1).astype(BF16)
        if c == 0:
            wait_for(TB.at[pl.ds(2 * T, T)], tbr.at[2])
        if c >= NSB and (G > 1 or c > NSB):
            wait_for(b_part(sendB, c - NSB, slot), sbs.at[slot])
        for i in range(DB // TILE):
            cols = slice(i * TILE, (i + 1) * TILE)
            sendB[slot, :, cols] = mm(sel, TB[:, cols]).astype(BF16)
        for d in range(G):
            if c or d:
                remote(
                    sendB.at[slot, pl.ds(d * MB, MB)], Y.at[pl.ds(c * ROWS + d * MB, MB), colsB],
                    sbs.at[slot], sbr.at[c], peer(c, d),
                )
            else:
                Y[:MB, DA:] = sendB[slot, :MB]

    def b_land(c):
        lo = MB if c == 0 else 0
        if ROWS > lo:
            wait_for(Y.at[pl.ds(c * ROWS + lo, ROWS - lo), colsB], sbr.at[c])
        rows = slice(c * ROWS, (c + 1) * ROWS)
        for i in range(DB // TILE):
            cols = slice(DA + i * TILE, DA + (i + 1) * TILE)
            Y[rows, cols] = mm(perm[...], Y[rows, cols]).astype(BF16)

    def yrows(c, j, lo=0, size=None):
        return pl.ds(c * ROWS + j * BLK + lo, BLK if size is None else size)

    def gather_start(c):
        lo = PAD if c == 0 else 0
        if MSG > lo:
            wait_for(recv.at[pl.ds(c * MSG + lo, MSG - lo)], s1r.at[c])
        own_rows = slice(c * ROWS, c * ROWS + BLK)
        for i in range(DA // TILE):
            cols = slice(i * TILE, (i + 1) * TILE)
            Y[own_rows, cols] = mm(compact, recv[c * MSG : (c + 1) * MSG, cols]).astype(BF16)
        GB[c, 0] = mm(gate_pick, recv[c * MSG : (c + 1) * MSG, :128]).astype(BF16)
        remote(Y.at[yrows(c, 0), colsA], Y.at[yrows(c, 3), colsA], ags, agr.at[c, 0], right)
        remote(Y.at[yrows(c, 0), colsA], Y.at[yrows(c, 1), colsA], ags, agr.at[c, 1], left)
        for k in range(1, NX):
            remote(GB.at[c, 0], GB.at[c, NX - k], gbs, gbr.at[c], along(k))

    def cut_of(c):
        return BLK * (2 - c % 2) // 3

    def gather_forward(c):
        wait_for(Y.at[yrows(c, 3), colsA], agr.at[c, 0])
        cut = cut_of(c)
        remote(Y.at[yrows(c, 3, 0, cut), colsA], Y.at[yrows(c, 2, 0, cut), colsA], ags, agr.at[c, 2], right)
        wait_for(Y.at[yrows(c, 1), colsA], agr.at[c, 1])
        rest = BLK - cut
        remote(Y.at[yrows(c, 1, cut, rest), colsA], Y.at[yrows(c, 2, cut, rest), colsA], ags, agr.at[c, 2], left)

    def compute(c):
        base = c % NSLOT * ROWS
        wait_for(Y.at[yrows(c, 2), colsA], agr.at[c, 2])
        wait_for(GB.at[c, pl.ds(1, NX - 1)], gbr.at[c])
        b_land(c)
        if c == 0:
            wd_copy.wait()
            wait_for(send.at[pl.ds(0, K * MSG - PAD), colsA], s1s)
        NT = min(TILE, H)
        for i in range(H // NT):
            dact[:, i * NT : (i + 1) * NT] = mm_nt(Y[c * ROWS : (c + 1) * ROWS, :], wd[i * NT : (i + 1) * NT, :])
        for j in range(NX):
            rows = slice(j * BLK, (j + 1) * BLK)
            at = c * ROWS + j * BLK
            a = saved[at : at + BLK, :H].astype(F32)
            b = saved[at : at + BLK, H:].astype(F32)
            da = dact[rows, :]
            spread = mm(of_source, GB[c, j])
            scale = jnp.sum(jnp.where(slot_mask, spread, 0.0), axis=1, keepdims=True)
            s = jax.nn.sigmoid(a)
            act = a * s
            hidden = act * b
            part = jnp.sum(hidden * da, axis=1, keepdims=True)
            parts = jnp.where(slot_mask, part, 0.0).astype(BF16)
            GPS[c, j] = mm(by_source, parts).astype(BF16)
            dh = scale * da
            dpre[rows, :H] = (dh * b * s * (1.0 + a * (1.0 - s))).astype(BF16)
            dpre[rows, H:] = (dh * act).astype(BF16)
            dact[rows, :] = scale * hidden
        for k in range(1, NX):
            remote(GPS.at[c, k], GPR.at[c, NX - k], gps, gpr.at[c], along(k))
        if c == 0:
            wgu_copy.wait()
        if c >= NSLOT:
            o = c - NSLOT
            wait_for(XP.at[pl.ds(base + BLK, ROWS - BLK), colsA], xps.at[o])
            lo = MB if o == 0 else 0
            if ROWS > lo:
                wait_for(XP.at[pl.ds(base + lo, ROWS - lo), colsB], xpbs.at[o])

        def tile_b(i, _):
            cols = pl.ds(pl.multiple_of(DA + i * TILE, TILE), TILE)
            XP[base : base + ROWS, cols] = mm(permT[...], mm_nt(dpre[...], wgu[cols, :]).astype(BF16)).astype(BF16)
            return 0

        lax.fori_loop(0, DB // TILE, tile_b, 0)
        for d in range(G):
            if c or d:
                remote(
                    XP.at[pl.ds(base + d * MB, MB), colsB], backB.at[pl.ds((c * G + d) * MB, MB)],
                    xpbs.at[c], bbr.at[c], source(c, d),
                )
            else:
                backB[:MB] = XP[base : base + MB, DA:]

        def tile_a(i, _):
            cols = pl.ds(pl.multiple_of(i * TILE, TILE), TILE)
            XP[base : base + ROWS, cols] = mm_nt(dpre[...], wgu[cols, :]).astype(BF16)
            return 0

        lax.fori_loop(0, DA // TILE, tile_a, 0)

        cut = cut_of(c)
        rest = BLK - cut

        def part_of(j, lo, size):
            return XP.at[pl.ds(base + j * BLK + lo, size), colsA]

        remote(part_of(2, 0, cut), RA.at[c, pl.ds(0, cut)], xps.at[c], rar.at[c, 0], right)
        remote(part_of(2, cut, rest), RA.at[c, pl.ds(cut, rest)], xps.at[c], rar.at[c, 1], left)
        remote(part_of(1, cut, rest), RB.at[c, 0, pl.ds(cut, rest)], xps.at[c], rbr.at[c, 0], right)
        remote(part_of(3, 0, cut), RB.at[c, 1, pl.ds(0, cut)], xps.at[c], rbr.at[c, 1], left)
        send[:H, c * ROWS : (c + 1) * ROWS] = jnp.transpose(dact[...]).astype(BF16)

    def reduce_middle(c):
        base = c % NSLOT * ROWS
        cut = cut_of(c)
        for side, j, lo, size, dev in ((0, 1, 0, cut, right), (1, 3, cut, BLK - cut, left)):
            wait_for(RA.at[c, pl.ds(lo, size)], rar.at[c, side])
            at = base + j * BLK + lo
            rows = slice(at, at + size)
            XP[rows, :DA] = (XP[rows, :DA].astype(F32) + RA[c, lo : lo + size].astype(F32)).astype(BF16)
            remote(XP.at[pl.ds(at, size), colsA], RB.at[c, side, pl.ds(lo, size)], xps.at[c], rbr.at[c, side], dev)

    def reduce_end(c):
        base = c % NSLOT * ROWS
        wait_for(GPR.at[c, pl.ds(1, NX - 1)], gpr.at[c])
        total = GPS[c, 0].astype(F32)
        for k in range(1, NX):
            total += GPR[c, k].astype(F32)
        high = total.astype(BF16)
        low = (total - high.astype(F32)).astype(BF16)
        up = iota((MSG, PAD), 0) - iota((MSG, PAD), 1) * PAD
        gate_back = mm(hot(up == SLOT), high) + mm(hot(up == SLOT + 1), low)
        wait_for(RB.at[c, 0], rbr.at[c, 0])
        wait_for(RB.at[c, 1], rbr.at[c, 1])
        msg = slice(c * MSG, (c + 1) * MSG)
        for i in range(DA // TILE):
            cols = slice(i * TILE, (i + 1) * TILE)
            whole = XP[base : base + BLK, cols].astype(F32) + RB[c, 0, :, cols].astype(F32) + RB[c, 1, :, cols].astype(F32)
            out = mm(expand, whole.astype(BF16))
            if i == 0:
                recv[msg, :128] = (out[:, :128] + gate_back).astype(BF16)
                recv[msg, 128:TILE] = out[:, 128:].astype(BF16)
            else:
                recv[msg, cols] = out.astype(BF16)
        for d in range(G):
            rows = pl.ds((c * G + d) * PAD, PAD)
            if c or d:
                remote(recv.at[rows], back.at[rows], rets, backr.at[c], source(c, d))
        if c == 0:
            back[:PAD] = recv[:PAD]

    def b_sum():
        for c in range(K):
            lo = MB if c == 0 else 0
            if ROWS > lo:
                wait_for(backB.at[pl.ds(c * ROWS + lo, ROWS - lo)], bbr.at[c])
        wait_for(TB.at[pl.ds(0, 3 * T)], tbs)
        for i in range(DB // TILE):
            cols = slice(i * TILE, (i + 1) * TILE)
            TB[:, cols] = mm(selT[...], backB[:, cols]).astype(BF16)
        h = T // 2
        remote(TB.at[pl.ds(2 * T, h)], RAB.at[0], pbs, rabr.at[0], right)
        remote(TB.at[pl.ds(2 * T + h, h)], RAB.at[1], pbs, rabr.at[1], left)
        remote(TB.at[pl.ds(T + h, h)], RBB.at[0, pl.ds(h, h)], pbs, rbbr.at[0], right)
        remote(TB.at[pl.ds(3 * T, h)], RBB.at[1, pl.ds(0, h)], pbs, rbbr.at[1], left)

    def b_middle():
        h = T // 2
        for side, j, lo, dev in ((0, 1, 0, right), (1, 3, h, left)):
            wait_for(RAB.at[side], rabr.at[side])
            rows = slice(j * T + lo, j * T + lo + h)
            TB[rows, :] = (TB[rows, :].astype(F32) + RAB[side].astype(F32)).astype(BF16)
            remote(TB.at[pl.ds(j * T + lo, h)], RBB.at[side, pl.ds(lo, h)], pbs, rbbr.at[side], dev)

    def b_end():
        wait_for(RBB.at[0], rbbr.at[0])
        wait_for(RBB.at[1], rbbr.at[1])
        ig_ref[:, DA:] = (TB[:T].astype(F32) + RBB[0].astype(F32) + RBB[1].astype(F32)).astype(BF16)

    tiles = D // TILE

    def weight_grad(first, last):
        def tile(i, _):
            cols = pl.ds(pl.multiple_of(i * TILE, TILE), TILE)
            dg_ref[:, cols] = mm(send[:H, : K * ROWS], Y[:, cols]).astype(BF16)
            return 0

        lax.fori_loop(first, last, tile, 0)

    b_forward()
    gather_start(0)
    routes = b_routes()
    for c in range(min(2, K)):
        b_select(c, routes)
    gather_start(1)
    gather_forward(0)
    for c in range(2, min(4, K)):
        b_select(c, routes)
    sort_saved()
    for s in range(2, K + 3):
        if s < K:
            gather_start(s)
        if 4 <= s + 2 < K:
            b_select(s + 2, routes)
        if s - 1 < K:
            gather_forward(s - 1)
        if 0 <= s - 3 < K:
            compute(s - 3)
        if 0 <= s - 4 < K:
            reduce_middle(s - 4)
        if 0 <= s - 5 < K:
            reduce_end(s - 5)
    part = tiles // 4
    weight_grad(0, part)
    reduce_middle(K - 1)
    weight_grad(part, 2 * part)
    reduce_end(K - 2)
    b_sum()
    reduce_end(K - 1)
    b_middle()
    weight_grad(2 * part, tiles)
    b_end()

    for c in range(K):
        lo = PAD if c == 0 else 0
        if MSG > lo:
            wait_for(back.at[pl.ds(c * MSG + lo, MSG - lo)], backr.at[c])
    for i in range(DA // TILE):
        cols = slice(i * TILE, (i + 1) * TILE)
        ig_ref[:, cols] = mm(mt[...], back[:, cols]).astype(BF16)
    back_gates = jnp.transpose(back[:, :128].astype(F32)).astype(BF16)
    for k, (blk, rank) in enumerate(own):
        at = slots - blk * PAD
        found = mm(back_gates, hot((at == SLOT) | (at == SLOT + 1)))
        gg_ref[k : k + 1, :] = jnp.sum(jnp.where(lane_slot == rank, found, 0.0), axis=0, keepdims=True)

    wait_for(recv.at[pl.ds(0, K * MSG - PAD)], rets)
    wait_for(Y.at[pl.ds(0, K * 3 * BLK), colsA], ags)
    wait_for(IDS.at[pl.ds(1, NX - 1)], idss)
    wait_for(TB.at[pl.ds(0, 3 * T)], pbs)
    for c in range(K):
        wait_for(GB.at[c, pl.ds(1, NX - 1)], gbs)
        wait_for(GPS.at[c, pl.ds(1, NX - 1)], gps)
    for c in range(max(0, K - NSB), K):
        lo = MB if c == 0 else 0
        if ROWS > lo:
            wait_for(sendB.at[c % NSB, pl.ds(lo, ROWS - lo)], sbs.at[c % NSB])
    for c in range(max(0, K - NSLOT), K):
        base = c % NSLOT * ROWS
        lo = MB if c == 0 else 0
        wait_for(XP.at[pl.ds(base + BLK, ROWS - BLK), colsA], xps.at[c])
        if ROWS > lo:
            wait_for(XP.at[pl.ds(base + lo, ROWS - lo), colsB], xpbs.at[c])


def body(out_grad, gates, expert_ids, saved_pre, w_gate_up, w_down):
    T, D = out_grad.shape
    B = lax.axis_size("node")
    C = lax.axis_size("local") // NX
    Q, SLOT = saved_pre.shape[1:3]
    H = w_down.shape[1]
    DA = split(D)
    DB = D - DA
    saved = jnp.transpose(saved_pre[0], (1, 0, 2))
    _, K, G, _ = plan(B, C)
    BLK, MSG = G * SLOT, G * PAD
    ROWS = NX * BLK
    NSLOT = min(6, K)
    NSB = min(4, K)
    vm = pl.BlockSpec(memory_space=pltpu.VMEM)
    anywhere = pl.BlockSpec(memory_space=pl.ANY)
    dma = pltpu.SemaphoreType.DMA
    ig, gg, dg = pl.pallas_call(
        functools.partial(kernel, B, C, SLOT, NSLOT),
        out_shape=(
            pltpu.VMEM((T, D), BF16),
            pltpu.VMEM((2, T), F32),
            pltpu.VMEM((H, D), BF16),
        ),
        in_specs=[vm, vm, anywhere, anywhere, anywhere, anywhere],
        out_specs=(vm, vm, vm),
        scratch_shapes=[
            pltpu.VMEM((T, D), BF16),
            pltpu.VMEM((D, 2 * H), BF16),
            pltpu.VMEM((max(K * MSG, H), max(DA, K * ROWS)), BF16),
            pltpu.VMEM((K * MSG, DA), BF16),
            pltpu.VMEM((K * MSG, DA), BF16),
            pltpu.VMEM((K * ROWS, D), BF16),
            pltpu.VMEM((K, NX, PAD, 128), BF16),
            pltpu.VMEM((NSLOT * ROWS, D), BF16),
            pltpu.VMEM((K, BLK, DA), BF16),
            pltpu.VMEM((K, 2, BLK, DA), BF16),
            pltpu.VMEM((K, NX, PAD, 128), BF16),
            pltpu.VMEM((K, NX, PAD, 128), BF16),
            pltpu.VMEM((K * ROWS, 2 * H), BF16),
            pltpu.VMEM((T, K * MSG), BF16),
            pltpu.VMEM((ROWS, 2 * H), BF16),
            pltpu.VMEM((ROWS, H), F32),
            pltpu.VMEM((NX, 8, T), jnp.int32),
            pltpu.VMEM((NX * T, DB), BF16),
            pltpu.VMEM((NSB, ROWS, DB), BF16),
            pltpu.VMEM((K * ROWS, DB), BF16),
            pltpu.VMEM((2, T // 2, DB), BF16),
            pltpu.VMEM((2, T, DB), BF16),
            pltpu.VMEM((NX * T, K * ROWS), BF16),
            pltpu.VMEM((ROWS, ROWS), BF16),
            pltpu.VMEM((ROWS, ROWS), BF16),
            dma((3,)),
            dma,
            dma,
            dma((K,)),
            dma,
            dma((K, 3)),
            dma,
            dma((K,)),
            dma((K,)),
            dma((K, 2)),
            dma((K, 2)),
            dma,
            dma((K,)),
            dma,
            dma((K,)),
            dma,
            dma,
            dma,
            dma((3,)),
            dma((NSB,)),
            dma((K,)),
            dma((K,)),
            dma((K,)),
            dma,
            dma((2,)),
            dma((2,)),
        ],
        compiler_params=pltpu.CompilerParams(
            collective_id=0, has_side_effects=True, vmem_limit_bytes=59 * 1024 * 1024
        ),
        cost_estimate=pl.CostEstimate(
            flops=2 * K * ROWS * D * 4 * H, bytes_accessed=25_000_000, transcendentals=K * ROWS * H
        ),
        name="moe_backward",
    )(expert_ids.T, gates.T, out_grad, saved, w_gate_up[0], w_down[0])
    return ig, gg.T, dg[None]


def solution(mesh):
    in_specs = (
        P(("node", "local"), None),
        P(("node", "local"), None),
        P(("node", "local"), None),
        P(("node", "local"), None, None, None),
        P(("node", "local"), None, None),
        P(("node", "local"), None, None),
    )
    out_specs = (
        P(("node", "local"), None),
        P(("node", "local"), None),
        P(("node", "local"), None, None),
    )
    return jax.shard_map(body, mesh=mesh, in_specs=in_specs, out_specs=out_specs, check_vma=False)
```

```python
import functools

import jax
import jax.numpy as jnp
from jax import lax
from jax.experimental import pallas as pl
from jax.experimental.pallas import tpu as pltpu
from jax.sharding import PartitionSpec as P

NX = 4
PAD = 16
TILE = 256
MESH = pl.DeviceIdType.MESH
F32 = jnp.float32
BF16 = jnp.bfloat16


def split(D):
    return max(512, 5 * D // 7 // 512 * 512)


def iota(shape, dim):
    return lax.broadcasted_iota(jnp.int32, shape, dim)


def shr(v, bits):
    return lax.shift_right_logical(v, jnp.full(v.shape, bits, jnp.int32))


def log2(size):
    return size.bit_length() - 1


def mm(a, b):
    return jnp.dot(a, b, preferred_element_type=F32)


def mm_nt(a, b):
    return lax.dot_general(a, b, (((1,), (1,)), ((), ())), preferred_element_type=F32)


def hot(mask):
    return mask.astype(F32).astype(BF16)


def plan(B, C):
    cores = 2 if B > C else 1
    even = B // cores == C
    chunks = C * cores if even else C
    return cores, chunks, B * C // chunks, even


def kernel(
    B, C, SLOT, NSLOT,
    ids_ref, gates_ref, og_hbm, saved_hbm, wgu_hbm, wd_hbm,
    ig_ref, gg_ref, dg_ref,
    og_ref, wgu, send, recv, back, Y, GB, XP, RA, RB, GPS, GPR, saved, mt, dpre, dact,
    IDS, TB, sendB, backB, RAB, RBB, selT, perm, permT,
    wsem, ssem, s1s, s1r, ags, agr, gbs, gbr, xps, rar, rbr, gps, gpr, rets, backr,
    idss, idsr, tbs, tbr, sbs, sbr, xpbs, bbr, pbs, rabr, rbbr,
):
    T, D = og_ref.shape
    H = dg_ref.shape[0]
    wd = dg_ref
    DA = split(D)
    DB = D - DA
    SEG = DA // 4
    segs = [slice(m * SEG, (m + 1) * SEG) for m in range(4)]
    extra = slice(3 * SEG, 3 * SEG + 128)
    W = 3 * SEG + 128
    WIDE = 2 * TILE if DB % (2 * TILE) == 0 else TILE
    CORES, K, G, even = plan(B, C)
    BLK = G * SLOT
    MSG = G * PAD
    MB = NX * SLOT
    ROWS = NX * BLK
    NSB = sendB.shape[0]
    LG, LC = log2(G), log2(C)
    colsA, colsB, colsW = pl.ds(0, DA), pl.ds(DA, DB), pl.ds(0, W)
    n = lax.axis_index("node")
    l = lax.axis_index("local")
    z, x = l // NX, l % NX
    right = (n, z * NX + (x + 1) % NX)
    left = (n, z * NX + (x + NX - 1) % NX)

    YS = B // CORES
    y, core = n // CORES, n % CORES
    LCO = log2(CORES)

    def offsets(c, d):
        return (d, (c // CORES + C - d) % C, c % CORES) if even else (c, d // CORES, d % CORES)

    def peer(c, d):
        dz, dy, dc = offsets(c, d)
        return (((y + dy) % YS) * CORES + (core + dc) % CORES, ((z + dz) % C) * NX + x)

    def source(c, d):
        dz, dy, dc = offsets(c, d)
        return (((y + YS - dy) % YS) * CORES + (core + CORES - dc) % CORES, ((z + C - dz) % C) * NX + x)

    def along(k):
        return (n, z * NX + (x + k) % NX)

    def remote(src, dst, ssem_, rsem_, dev):
        pltpu.make_async_remote_copy(
            src_ref=src, dst_ref=dst, send_sem=ssem_, recv_sem=rsem_, device_id=dev, device_id_type=MESH
        ).start()

    def wait_for(ref, sem):
        pltpu.make_async_copy(ref, ref, sem).wait()

    barrier = pltpu.get_barrier_semaphore()
    count = 0
    for k in range(1, NX):
        pl.semaphore_signal(barrier, inc=1, device_id=along(k), device_id_type=MESH)
        count += 1
    for c in range(K):
        for d in range(G):
            if c or d:
                pl.semaphore_signal(barrier, inc=1, device_id=peer(c, d), device_id_type=MESH)
                count += 1

    wd_copy = pltpu.make_async_copy(wd_hbm, wd, wsem.at[0])
    wgu_copy = pltpu.make_async_copy(wgu_hbm, wgu, wsem.at[1])

    Q = C * NX * B
    QUADS = SLOT // 4
    first_row = NSLOT * ROWS - 4 * Q

    def stage(r):
        dst = XP.at[pl.ds(first_row + r % 4 * Q, Q), pl.ds(r // 4 * 2 * H, 2 * H)]
        return pltpu.make_async_copy(saved_hbm.at[r], dst, ssem)

    og_copy = pltpu.make_async_copy(og_hbm, og_ref, wsem.at[2])
    og_copy.start()
    for r in range(SLOT):
        stage(r).start()
    wd_copy.start()
    wgu_copy.start()

    IDS[0, :2] = ids_ref[...]
    NE = max(8, B * C)
    before = hot(iota((T, T), 0) < iota((T, T), 1))
    expert_row = iota((NE, T), 0)

    def route(ids):
        experts = [ids[k : k + 1] for k in range(2)]
        hits = [expert_row == e for e in experts]
        per_token = hits[0].astype(F32) + hits[1].astype(F32)
        earlier = mm(per_token.astype(BF16), before)
        out = []
        for k in range(2):
            rank = jnp.sum(jnp.where(hits[k], earlier, 0.0), axis=0, keepdims=True).astype(jnp.int32)
            zz = experts[k] & (C - 1)
            node = shr(experts[k], LC)
            dz = (zz - z + C) & (C - 1)
            dy = (shr(node, LCO) - y + YS) & (YS - 1)
            dc = (node - core + CORES) & (CORES - 1)
            blk = (((dy + dz) & (C - 1)) * CORES + dc) * G + dz if even else dz * G + dy * CORES + dc
            out.append((blk, rank))
        return out

    own = route(ids_ref[...])
    def third(v):
        return shr(v * 11, 5)

    slots = iota((K * MSG, T), 0)
    lane_slot = iota((128, T), 0)
    picks = [jnp.zeros((K * MSG, T), F32) for _ in range(4)]
    gate_rows = jnp.zeros((K * MSG, 128), F32)
    gates = gates_ref[...].astype(F32)
    for k, (blk, rank) in enumerate(own):
        at = slots - blk * PAD
        picks[3] += (at == rank).astype(F32)
        for m in range(3):
            tail = jnp.where(rank - 3 * third(rank) == m, SLOT + third(rank), -K * MSG)
            picks[m] += (at == tail).astype(F32)
        gate_at = jnp.where(lane_slot == rank, gates[k : k + 1], 0.0).astype(BF16)
        gate_rows += mm_nt(hot(at == 0), gate_at)
    for m in range(4):
        mt[m] = jnp.transpose(picks[m]).astype(BF16)
    picks = [p.astype(BF16) for p in picks]
    og_copy.wait()
    TB[:T] = og_ref[:, DA:]

    pl.semaphore_wait(barrier, count)

    for k in range(1, NX):
        remote(IDS.at[0], IDS.at[NX - k], idss, idsr, along(k))
    remote(TB.at[pl.ds(0, T)], TB.at[pl.ds(3 * T, T)], tbs, tbr.at[0], right)
    remote(TB.at[pl.ds(0, T)], TB.at[pl.ds(T, T)], tbs, tbr.at[1], left)

    HEAD = max(1, K // 4)

    def a_send(first, last):
        for g in range(first, last, HEAD):
            rows = slice(g * MSG, (g + HEAD) * MSG)
            for m in range(3):
                both = mm(picks[3][rows], og_ref[:, segs[m]]) + mm(picks[m][rows], og_ref[:, segs[3]])
                send[rows, segs[m]] = both.astype(BF16)
            send[rows, extra] = gate_rows[rows].astype(BF16)
            for c in range(g, g + HEAD):
                for d in range(G):
                    at = pl.ds((c * G + d) * PAD, PAD)
                    if c or d:
                        remote(send.at[at, colsW], recv.at[at], s1s, s1r.at[c], peer(c, d))
        if first == 0:
            recv[:PAD] = send[:PAD, :W]

    a_send(0, K // 2)

    def row_parts(i):
        j = jnp.zeros(i.shape, jnp.int32)
        for k in range(1, NX):
            j += (i >= k * BLK).astype(jnp.int32)
        rest = i - j * BLK
        return j, shr(rest, LG), rest & (G - 1)

    def places(shape, dim):
        _, r, d = row_parts(iota(shape, dim))
        at = iota(shape, 1 - dim) - d * PAD
        tails = [hot((at == SLOT + third(r)) & (r - 3 * third(r) == m)) for m in range(3)]
        return tails + [hot(at == r)]

    compact = places((BLK, MSG), 0)
    expand = places((MSG, BLK), 1)
    gate_pick = hot(iota((PAD, MSG), 1) == iota((PAD, MSG), 0) * PAD)
    of_source = hot((iota((BLK, PAD), 0) & (G - 1)) == iota((BLK, PAD), 1))
    by_source = hot((iota((PAD, BLK), 1) & (G - 1)) == iota((PAD, BLK), 0))
    slot_mask = iota((BLK, 128), 1) == shr(iota((BLK, 128), 0), LG)
    j_i, r_i, d_i = row_parts(iota((ROWS, ROWS), 0))
    perm[...] = hot(iota((ROWS, ROWS), 1) == d_i * MB + j_i * SLOT + r_i)
    j_l, r_l, d_l = row_parts(iota((ROWS, ROWS), 1))
    permT[...] = hot(iota((ROWS, ROWS), 0) == d_l * MB + j_l * SLOT + r_l)

    def sort_saved():
        row, col = iota((K * NX * 4 * G, 4 * Q), 0), iota((K * NX * 4 * G, 4 * Q), 1)
        r, d, j, c = shr(row, LG) & 3, row & (G - 1), shr(row, LG + 2) & (NX - 1), shr(row, LG + 4)
        if even:
            dz, dc = d, c & (CORES - 1)
            dy = (shr(c, LCO) + C - dz) & (C - 1)
        else:
            dz, dy, dc = c, shr(d, LCO), d & (CORES - 1)
        node = ((y + YS - dy) & (YS - 1)) * CORES + ((core + CORES - dc) & (CORES - 1))
        q = node * (C * NX) + ((z + C - dz) & (C - 1)) * NX + ((x + j) & (NX - 1))
        order = hot(col == r * Q + q)
        wait_for(XP.at[pl.ds(first_row, 4 * Q), pl.ds(0, QUADS * 2 * H)], ssem)
        NS = min(TILE, 2 * H)
        for p in range(QUADS):
            for i in range(2 * H // NS):
                cols = slice(p * 2 * H + i * NS, p * 2 * H + (i + 1) * NS)
                out = mm(order, XP[first_row : first_row + 4 * Q, cols]).astype(BF16)
                for g in range(K * NX):
                    at = g * BLK + p * 4 * G
                    saved[at : at + 4 * G, i * NS : (i + 1) * NS] = out[g * 4 * G : (g + 1) * 4 * G]

    def b_forward():
        h = T // 2
        wait_for(TB.at[pl.ds(3 * T, T)], tbr.at[0])
        remote(TB.at[pl.ds(3 * T, h)], TB.at[pl.ds(2 * T, h)], tbs, tbr.at[2], right)
        wait_for(TB.at[pl.ds(T, T)], tbr.at[1])
        remote(TB.at[pl.ds(T + h, h)], TB.at[pl.ds(2 * T + h, h)], tbs, tbr.at[2], left)

    def b_routes():
        wait_for(IDS.at[pl.ds(1, NX - 1)], idsr)
        return [own] + [route(IDS[j, :2]) for j in range(1, NX)]

    def b_part(ref, c, lead):
        lo = MB if c == 0 else 0
        return ref.at[lead, pl.ds(lo, ROWS - lo)] if lead is not None else ref.at[pl.ds(lo, ROWS - lo)]

    def b_select(c, routes):
        slot = c % NSB
        at = iota((ROWS, T), 0)
        parts = []
        for j in range(NX):
            part = jnp.zeros((ROWS, T), F32)
            for blk, rank in routes[j]:
                part += (at == (blk - c * G) * MB + j * SLOT + rank).astype(F32)
            parts.append(part)
            selT[j * T : (j + 1) * T, c * ROWS : (c + 1) * ROWS] = jnp.transpose(part).astype(BF16)
        sel = jnp.concatenate(parts, axis=1).astype(BF16)
        if c == 0:
            wait_for(TB.at[pl.ds(2 * T, T)], tbr.at[2])
        if c >= NSB and (G > 1 or c > NSB):
            wait_for(b_part(sendB, c - NSB, slot), sbs.at[slot])
        for i in range(DB // TILE):
            cols = slice(i * TILE, (i + 1) * TILE)
            sendB[slot, :, cols] = mm(sel, TB[:, cols]).astype(BF16)
        for d in range(G):
            if c or d:
                remote(
                    sendB.at[slot, pl.ds(d * MB, MB)], Y.at[pl.ds(c * ROWS + d * MB, MB), colsB],
                    sbs.at[slot], sbr.at[c], peer(c, d),
                )
            else:
                Y[:MB, DA:] = sendB[slot, :MB]

    def b_land(c):
        lo = MB if c == 0 else 0
        if ROWS > lo:
            wait_for(Y.at[pl.ds(c * ROWS + lo, ROWS - lo), colsB], sbr.at[c])
        rows = slice(c * ROWS, (c + 1) * ROWS)
        for i in range(DB // TILE):
            cols = slice(DA + i * TILE, DA + (i + 1) * TILE)
            Y[rows, cols] = mm(perm[...], Y[rows, cols]).astype(BF16)

    def yrows(c, j, lo=0, size=None):
        return pl.ds(c * ROWS + j * BLK + lo, BLK if size is None else size)

    def gather_start(c):
        lo = PAD if c == 0 else 0
        if MSG > lo:
            wait_for(recv.at[pl.ds(c * MSG + lo, MSG - lo)], s1r.at[c])
        own_rows = slice(c * ROWS, c * ROWS + BLK)
        msg = slice(c * MSG, (c + 1) * MSG)
        last = jnp.zeros((BLK, SEG), F32)
        for m in range(3):
            Y[own_rows, segs[m]] = mm(compact[3], recv[msg, segs[m]]).astype(BF16)
            last += mm(compact[m], recv[msg, segs[m]])
        Y[own_rows, segs[3]] = last.astype(BF16)
        GB[c, 0] = mm(gate_pick, recv[msg, extra]).astype(BF16)
        remote(Y.at[yrows(c, 0), colsA], Y.at[yrows(c, 3), colsA], ags, agr.at[c, 0], right)
        remote(Y.at[yrows(c, 0), colsA], Y.at[yrows(c, 1), colsA], ags, agr.at[c, 1], left)
        for k in range(1, NX):
            remote(GB.at[c, 0], GB.at[c, NX - k], gbs, gbr.at[c], along(k))

    def cut_of(c):
        return BLK * (2 - c % 2) // 3

    def gather_forward(c):
        wait_for(Y.at[yrows(c, 3), colsA], agr.at[c, 0])
        cut = cut_of(c)
        remote(Y.at[yrows(c, 3, 0, cut), colsA], Y.at[yrows(c, 2, 0, cut), colsA], ags, agr.at[c, 2], right)
        wait_for(Y.at[yrows(c, 1), colsA], agr.at[c, 1])
        rest = BLK - cut
        remote(Y.at[yrows(c, 1, cut, rest), colsA], Y.at[yrows(c, 2, cut, rest), colsA], ags, agr.at[c, 2], left)

    def compute(c):
        base = c % NSLOT * ROWS
        wait_for(Y.at[yrows(c, 2), colsA], agr.at[c, 2])
        wait_for(GB.at[c, pl.ds(1, NX - 1)], gbr.at[c])
        b_land(c)
        if c == 0:
            wd_copy.wait()
        NT = min(TILE, H)
        for i in range(H // NT):
            dact[:, i * NT : (i + 1) * NT] = mm_nt(Y[c * ROWS : (c + 1) * ROWS, :], wd[i * NT : (i + 1) * NT, :])
        for j in range(NX):
            rows = slice(j * BLK, (j + 1) * BLK)
            at = c * ROWS + j * BLK
            a = saved[at : at + BLK, :H].astype(F32)
            b = saved[at : at + BLK, H:].astype(F32)
            da = dact[rows, :]
            spread = mm(of_source, GB[c, j])
            scale = jnp.sum(jnp.where(slot_mask, spread, 0.0), axis=1, keepdims=True)
            s = jax.nn.sigmoid(a)
            act = a * s
            hidden = act * b
            part = jnp.sum(hidden * da, axis=1, keepdims=True)
            parts = jnp.where(slot_mask, part, 0.0).astype(BF16)
            GPS[c, j] = mm(by_source, parts).astype(BF16)
            dh = scale * da
            dpre[rows, :H] = (dh * b * s * (1.0 + a * (1.0 - s))).astype(BF16)
            dpre[rows, H:] = (dh * act).astype(BF16)
            dact[rows, :] = scale * hidden
        for k in range(1, NX):
            remote(GPS.at[c, k], GPR.at[c, NX - k], gps, gpr.at[c], along(k))
        if c == 0:
            wgu_copy.wait()
        if c >= NSLOT:
            o = c - NSLOT
            wait_for(XP.at[pl.ds(base + BLK, ROWS - BLK), colsA], xps.at[o])
            lo = MB if o == 0 else 0
            if ROWS > lo:
                wait_for(XP.at[pl.ds(base + lo, ROWS - lo), colsB], xpbs.at[o])

        def tile_b(i, _):
            cols = pl.ds(pl.multiple_of(DA + i * WIDE, TILE), WIDE)
            XP[base : base + ROWS, cols] = mm(permT[...], mm_nt(dpre[...], wgu[cols, :]).astype(BF16)).astype(BF16)
            return 0

        lax.fori_loop(0, DB // WIDE, tile_b, 0)
        for d in range(G):
            if c or d:
                remote(
                    XP.at[pl.ds(base + d * MB, MB), colsB], backB.at[pl.ds((c * G + d) * MB, MB)],
                    xpbs.at[c], bbr.at[c], source(c, d),
                )
            else:
                backB[:MB] = XP[base : base + MB, DA:]

        def tile_a(i, _):
            cols = pl.ds(pl.multiple_of(i * WIDE, TILE), WIDE)
            XP[base : base + ROWS, cols] = mm_nt(dpre[...], wgu[cols, :]).astype(BF16)
            return 0

        lax.fori_loop(0, DA // WIDE, tile_a, 0)

        cut = cut_of(c)
        rest = BLK - cut

        def part_of(j, lo, size):
            return XP.at[pl.ds(base + j * BLK + lo, size), colsA]

        remote(part_of(2, 0, cut), RA.at[c, pl.ds(0, cut)], xps.at[c], rar.at[c, 0], right)
        remote(part_of(2, cut, rest), RA.at[c, pl.ds(cut, rest)], xps.at[c], rar.at[c, 1], left)
        remote(part_of(1, cut, rest), RB.at[c, 0, pl.ds(cut, rest)], xps.at[c], rbr.at[c, 0], right)
        remote(part_of(3, 0, cut), RB.at[c, 1, pl.ds(0, cut)], xps.at[c], rbr.at[c, 1], left)
        if c == 0:
            wait_for(send.at[pl.ds(0, K * MSG - PAD), colsW], s1s)
        send[:H, c * ROWS : (c + 1) * ROWS] = jnp.transpose(dact[...]).astype(BF16)

    def reduce_middle(c):
        base = c % NSLOT * ROWS
        cut = cut_of(c)
        for side, j, lo, size, dev in ((0, 1, 0, cut, right), (1, 3, cut, BLK - cut, left)):
            wait_for(RA.at[c, pl.ds(lo, size)], rar.at[c, side])
            at = base + j * BLK + lo
            rows = slice(at, at + size)
            XP[rows, :DA] = (XP[rows, :DA].astype(F32) + RA[c, lo : lo + size].astype(F32)).astype(BF16)
            remote(XP.at[pl.ds(at, size), colsA], RB.at[c, side, pl.ds(lo, size)], xps.at[c], rbr.at[c, side], dev)

    def reduce_end(c):
        base = c % NSLOT * ROWS
        wait_for(GPR.at[c, pl.ds(1, NX - 1)], gpr.at[c])
        total = GPS[c, 0].astype(F32)
        for k in range(1, NX):
            total += GPR[c, k].astype(F32)
        high = total.astype(BF16)
        low = (total - high.astype(F32)).astype(BF16)
        up = iota((MSG, PAD), 0) - iota((MSG, PAD), 1) * PAD
        gate_back = mm(hot(up == 0), high) + mm(hot(up == 1), low)
        wait_for(RB.at[c, 0], rbr.at[c, 0])
        wait_for(RB.at[c, 1], rbr.at[c, 1])
        msg = slice(c * MSG, (c + 1) * MSG)
        def whole(cols):
            part = XP[base : base + BLK, cols].astype(F32) + RB[c, 0, :, cols].astype(F32)
            return (part + RB[c, 1, :, cols].astype(F32)).astype(BF16)

        last = whole(segs[3])
        for m in range(3):
            recv[msg, segs[m]] = (mm(expand[3], whole(segs[m])) + mm(expand[m], last)).astype(BF16)
        recv[msg, extra] = gate_back.astype(BF16)
        for d in range(G):
            rows = pl.ds((c * G + d) * PAD, PAD)
            if c or d:
                remote(recv.at[rows], back.at[rows], rets, backr.at[c], source(c, d))
        if c == 0:
            back[:PAD] = recv[:PAD]

    def b_sum():
        for c in range(K):
            lo = MB if c == 0 else 0
            if ROWS > lo:
                wait_for(backB.at[pl.ds(c * ROWS + lo, ROWS - lo)], bbr.at[c])
        wait_for(TB.at[pl.ds(0, 3 * T)], tbs)
        for i in range(DB // TILE):
            cols = slice(i * TILE, (i + 1) * TILE)
            TB[:, cols] = mm(selT[...], backB[:, cols]).astype(BF16)
        h = T // 2
        remote(TB.at[pl.ds(2 * T, h)], RAB.at[0], pbs, rabr.at[0], right)
        remote(TB.at[pl.ds(2 * T + h, h)], RAB.at[1], pbs, rabr.at[1], left)
        remote(TB.at[pl.ds(T + h, h)], RBB.at[0, pl.ds(h, h)], pbs, rbbr.at[0], right)
        remote(TB.at[pl.ds(3 * T, h)], RBB.at[1, pl.ds(0, h)], pbs, rbbr.at[1], left)

    def b_middle():
        h = T // 2
        for side, j, lo, dev in ((0, 1, 0, right), (1, 3, h, left)):
            wait_for(RAB.at[side], rabr.at[side])
            rows = slice(j * T + lo, j * T + lo + h)
            TB[rows, :] = (TB[rows, :].astype(F32) + RAB[side].astype(F32)).astype(BF16)
            remote(TB.at[pl.ds(j * T + lo, h)], RBB.at[side, pl.ds(lo, h)], pbs, rbbr.at[side], dev)

    def b_end():
        wait_for(RBB.at[0], rbbr.at[0])
        wait_for(RBB.at[1], rbbr.at[1])
        ig_ref[:, DA:] = (TB[:T].astype(F32) + RBB[0].astype(F32) + RBB[1].astype(F32)).astype(BF16)

    tiles = D // WIDE

    def weight_grad(first, last):
        def tile(i, _):
            cols = pl.ds(pl.multiple_of(i * WIDE, TILE), WIDE)
            dg_ref[:, cols] = mm(send[:H, : K * ROWS], Y[:, cols]).astype(BF16)
            return 0

        lax.fori_loop(first, last, tile, 0)

    b_forward()
    gather_start(0)
    routes = b_routes()
    b_select(0, routes)
    b_select(1, routes)
    a_send(K // 2, K)
    gather_start(1)
    gather_forward(0)
    for c in range(2, min(4, K)):
        b_select(c, routes)
    sort_saved()
    for s in range(2, K + 3):
        if s < K:
            gather_start(s)
        if 4 <= s + 2 < K:
            b_select(s + 2, routes)
        if s - 1 < K:
            gather_forward(s - 1)
        if 0 <= s - 3 < K:
            compute(s - 3)
        if 0 <= s - 4 < K:
            reduce_middle(s - 4)
        if 0 <= s - 5 < K:
            reduce_end(s - 5)
    part = tiles // 3
    weight_grad(0, part)
    reduce_middle(K - 1)
    b_sum()
    reduce_end(K - 2)
    weight_grad(part, 2 * part)
    reduce_end(K - 1)
    weight_grad(2 * part, tiles)
    b_middle()
    b_end()

    for c in range(K):
        lo = PAD if c == 0 else 0
        if MSG > lo:
            wait_for(back.at[pl.ds(c * MSG + lo, MSG - lo)], backr.at[c])
    last = jnp.zeros((T, SEG), F32)
    for m in range(3):
        ig_ref[:, segs[m]] = mm(mt[3], back[:, segs[m]]).astype(BF16)
        last += mm(mt[m], back[:, segs[m]])
    ig_ref[:, segs[3]] = last.astype(BF16)
    back_gates = jnp.transpose(back[:, extra].astype(F32)).astype(BF16)
    for k, (blk, rank) in enumerate(own):
        at = slots - blk * PAD
        found = mm(back_gates, hot((at == 0) | (at == 1)))
        gg_ref[k : k + 1, :] = jnp.sum(jnp.where(lane_slot == rank, found, 0.0), axis=0, keepdims=True)

    wait_for(recv.at[pl.ds(0, K * MSG - PAD)], rets)
    wait_for(Y.at[pl.ds(0, K * 3 * BLK), colsA], ags)
    wait_for(IDS.at[pl.ds(1, NX - 1)], idss)
    wait_for(TB.at[pl.ds(0, 3 * T)], pbs)
    for c in range(K):
        wait_for(GB.at[c, pl.ds(1, NX - 1)], gbs)
        wait_for(GPS.at[c, pl.ds(1, NX - 1)], gps)
    for c in range(max(0, K - NSB), K):
        lo = MB if c == 0 else 0
        if ROWS > lo:
            wait_for(sendB.at[c % NSB, pl.ds(lo, ROWS - lo)], sbs.at[c % NSB])
    for c in range(max(0, K - NSLOT), K):
        base = c % NSLOT * ROWS
        lo = MB if c == 0 else 0
        wait_for(XP.at[pl.ds(base + BLK, ROWS - BLK), colsA], xps.at[c])
        if ROWS > lo:
            wait_for(XP.at[pl.ds(base + lo, ROWS - lo), colsB], xpbs.at[c])


def body(out_grad, gates, expert_ids, saved_pre, w_gate_up, w_down):
    T, D = out_grad.shape
    B = lax.axis_size("node")
    C = lax.axis_size("local") // NX
    Q, SLOT = saved_pre.shape[1:3]
    H = w_down.shape[1]
    DA = split(D)
    DB, W = D - DA, 3 * DA // 4 + 128
    saved = jnp.transpose(saved_pre[0], (1, 0, 2))
    _, K, G, _ = plan(B, C)
    BLK, MSG = G * SLOT, G * PAD
    ROWS = NX * BLK
    NSLOT = min(6, K)
    NSB = K
    vm = pl.BlockSpec(memory_space=pltpu.VMEM)
    anywhere = pl.BlockSpec(memory_space=pl.ANY)
    dma = pltpu.SemaphoreType.DMA
    ig, gg, dg = pl.pallas_call(
        functools.partial(kernel, B, C, SLOT, NSLOT),
        out_shape=(
            pltpu.VMEM((T, D), BF16),
            pltpu.VMEM((2, T), F32),
            pltpu.VMEM((H, D), BF16),
        ),
        in_specs=[vm, vm, anywhere, anywhere, anywhere, anywhere],
        out_specs=(vm, vm, vm),
        scratch_shapes=[
            pltpu.VMEM((T, D), BF16),
            pltpu.VMEM((D, 2 * H), BF16),
            pltpu.VMEM((max(K * MSG, H), max(W, K * ROWS)), BF16),
            pltpu.VMEM((K * MSG, W), BF16),
            pltpu.VMEM((K * MSG, W), BF16),
            pltpu.VMEM((K * ROWS, D), BF16),
            pltpu.VMEM((K, NX, PAD, 128), BF16),
            pltpu.VMEM((NSLOT * ROWS, D), BF16),
            pltpu.VMEM((K, BLK, DA), BF16),
            pltpu.VMEM((K, 2, BLK, DA), BF16),
            pltpu.VMEM((K, NX, PAD, 128), BF16),
            pltpu.VMEM((K, NX, PAD, 128), BF16),
            pltpu.VMEM((K * ROWS, 2 * H), BF16),
            pltpu.VMEM((4, T, K * MSG), BF16),
            pltpu.VMEM((ROWS, 2 * H), BF16),
            pltpu.VMEM((ROWS, H), F32),
            pltpu.VMEM((NX, 8, T), jnp.int32),
            pltpu.VMEM((NX * T, DB), BF16),
            pltpu.VMEM((NSB, ROWS, DB), BF16),
            pltpu.VMEM((K * ROWS, DB), BF16),
            pltpu.VMEM((2, T // 2, DB), BF16),
            pltpu.VMEM((2, T, DB), BF16),
            pltpu.VMEM((NX * T, K * ROWS), BF16),
            pltpu.VMEM((ROWS, ROWS), BF16),
            pltpu.VMEM((ROWS, ROWS), BF16),
            dma((3,)),
            dma,
            dma,
            dma((K,)),
            dma,
            dma((K, 3)),
            dma,
            dma((K,)),
            dma((K,)),
            dma((K, 2)),
            dma((K, 2)),
            dma,
            dma((K,)),
            dma,
            dma((K,)),
            dma,
            dma,
            dma,
            dma((3,)),
            dma((NSB,)),
            dma((K,)),
            dma((K,)),
            dma((K,)),
            dma,
            dma((2,)),
            dma((2,)),
        ],
        compiler_params=pltpu.CompilerParams(
            collective_id=0, has_side_effects=True, vmem_limit_bytes=59 * 1024 * 1024
        ),
        cost_estimate=pl.CostEstimate(
            flops=2 * K * ROWS * D * 4 * H, bytes_accessed=25_000_000, transcendentals=K * ROWS * H
        ),
        name="moe_backward",
    )(expert_ids.T, gates.T, out_grad, saved, w_gate_up[0], w_down[0])
    return ig, gg.T, dg[None]


def solution(mesh):
    in_specs = (
        P(("node", "local"), None),
        P(("node", "local"), None),
        P(("node", "local"), None),
        P(("node", "local"), None, None, None),
        P(("node", "local"), None, None),
        P(("node", "local"), None, None),
    )
    out_specs = (
        P(("node", "local"), None),
        P(("node", "local"), None),
        P(("node", "local"), None, None),
    )
    return jax.shard_map(body, mesh=mesh, in_specs=in_specs, out_specs=out_specs, check_vma=False)
```

```python
import functools

import jax
import jax.numpy as jnp
from jax import lax
from jax.experimental import pallas as pl
from jax.experimental.pallas import tpu as pltpu
from jax.sharding import PartitionSpec as P

NX = 4
PAD = 16
TILE = 256
MESH = pl.DeviceIdType.MESH
F32 = jnp.float32
BF16 = jnp.bfloat16


def split(D):
    return max(3 * TILE, 9 * D // 14 // TILE * TILE)


def spare_columns(DA):
    return (DA - 128) // 4 // 128 * 128


def iota(shape, dim):
    return lax.broadcasted_iota(jnp.int32, shape, dim)


def shr(v, bits):
    return lax.shift_right_logical(v, jnp.full(v.shape, bits, jnp.int32))


def log2(size):
    return size.bit_length() - 1


def mm(a, b):
    return jnp.dot(a, b, preferred_element_type=F32)


def mm_nt(a, b):
    return lax.dot_general(a, b, (((1,), (1,)), ((), ())), preferred_element_type=F32)


def hot(mask):
    return mask.astype(F32).astype(BF16)


def plan(B, C):
    cores = 2 if B > C else 1
    even = B // cores == C
    chunks = C * cores if even else C
    return cores, chunks, B * C // chunks, even


def kernel(
    B, C, SLOT, NSLOT,
    ids_ref, gates_ref, og_hbm, saved_hbm, wgu_hbm, wd_hbm,
    ig_ref, gg_ref, dg_ref,
    og_ref, wgu, send, recv, back, Y, GB, XP, RA, RB, GPS, GPR, saved, wT, mt, dpre, dact,
    IDS, TB, sendB, backB, RAB, RBB, selT, perm, permT,
    wsem, ssem, s1s, s1r, ags, agr, gbs, gbr, xps, rar, rbr, gps, gpr, rets, backr,
    idss, idsr, tbs, tbr, sbs, sbr, xpbs, bbr, pbs, rabr, rbbr,
):
    T, D = og_ref.shape
    H = dg_ref.shape[0]
    wd = dg_ref
    DA = split(D)
    DB = D - DA
    S = spare_columns(DA)
    W = DA - S
    segs = [slice(m * S, (m + 1) * S) for m in range(3)] + [slice(3 * S, W)]
    tail = slice(W, DA)
    extra = slice(3 * S, 3 * S + 128)
    WA = 3 * TILE if DA % (3 * TILE) == 0 else TILE
    WB = DB // 2 if DB % 256 == 0 else DB
    WG = 2 * TILE
    CORES, K, G, even = plan(B, C)
    BLK = G * SLOT
    MSG = G * PAD
    MB = NX * SLOT
    ROWS = NX * BLK
    NSB = sendB.shape[0]
    LG, LC = log2(G), log2(C)
    colsA, colsB = pl.ds(0, DA), pl.ds(DA, DB)
    n = lax.axis_index("node")
    l = lax.axis_index("local")
    z, x = l // NX, l % NX
    right = (n, z * NX + (x + 1) % NX)
    left = (n, z * NX + (x + NX - 1) % NX)

    YS = B // CORES
    y, core = n // CORES, n % CORES
    LCO = log2(CORES)

    def offsets(c, d):
        return (d, (c // CORES + C - d) % C, c % CORES) if even else (c, d // CORES, d % CORES)

    def peer(c, d):
        dz, dy, dc = offsets(c, d)
        return (((y + dy) % YS) * CORES + (core + dc) % CORES, ((z + dz) % C) * NX + x)

    def source(c, d):
        dz, dy, dc = offsets(c, d)
        return (((y + YS - dy) % YS) * CORES + (core + CORES - dc) % CORES, ((z + C - dz) % C) * NX + x)

    def along(k):
        return (n, z * NX + (x + k) % NX)

    def remote(src, dst, ssem_, rsem_, dev):
        pltpu.make_async_remote_copy(
            src_ref=src, dst_ref=dst, send_sem=ssem_, recv_sem=rsem_, device_id=dev, device_id_type=MESH
        ).start()

    def wait_for(ref, sem):
        pltpu.make_async_copy(ref, ref, sem).wait()

    barrier = pltpu.get_barrier_semaphore()
    count = 0
    for k in range(1, NX):
        pl.semaphore_signal(barrier, inc=1, device_id=along(k), device_id_type=MESH)
        count += 1
    for c in range(K):
        for d in range(G):
            if c or d:
                pl.semaphore_signal(barrier, inc=1, device_id=peer(c, d), device_id_type=MESH)
                count += 1

    wd_copy = pltpu.make_async_copy(wd_hbm, wd, wsem.at[0])
    wgu_copy = pltpu.make_async_copy(wgu_hbm, wgu, wsem.at[1])

    Q = C * NX * B
    QUADS = SLOT // 4
    first_row = NSLOT * ROWS - 4 * Q

    def stage(r):
        dst = XP.at[pl.ds(first_row + r % 4 * Q, Q), pl.ds(r // 4 * 2 * H, 2 * H)]
        return pltpu.make_async_copy(saved_hbm.at[r], dst, ssem)

    og_copy = pltpu.make_async_copy(og_hbm, og_ref, wsem.at[2])
    og_copy.start()
    for r in range(SLOT):
        stage(r).start()
    wd_copy.start()
    wgu_copy.start()

    IDS[0, :2] = ids_ref[...]
    pl.semaphore_wait(barrier, count)
    remote(og_hbm.at[:, colsB], TB.at[pl.ds(3 * T, T)], tbs, tbr.at[0], right)
    remote(og_hbm.at[:, colsB], TB.at[pl.ds(T, T)], tbs, tbr.at[1], left)
    for k in range(1, NX):
        remote(IDS.at[0], IDS.at[NX - k], idss, idsr, along(k))

    NE = max(8, B * C)
    before = hot(iota((T, T), 0) < iota((T, T), 1))
    expert_row = iota((NE, T), 0)

    def route(ids):
        experts = [ids[k : k + 1] for k in range(2)]
        hits = [expert_row == e for e in experts]
        per_token = hits[0].astype(F32) + hits[1].astype(F32)
        earlier = mm(per_token.astype(BF16), before)
        out = []
        for k in range(2):
            rank = jnp.sum(jnp.where(hits[k], earlier, 0.0), axis=0, keepdims=True).astype(jnp.int32)
            zz = experts[k] & (C - 1)
            node = shr(experts[k], LC)
            dz = (zz - z + C) & (C - 1)
            dy = (shr(node, LCO) - y + YS) & (YS - 1)
            dc = (node - core + CORES) & (CORES - 1)
            blk = (((dy + dz) & (C - 1)) * CORES + dc) * G + dz if even else dz * G + dy * CORES + dc
            out.append((blk, rank))
        return out

    own = route(ids_ref[...])
    def third(v):
        return shr(v * 11, 5)

    slots = iota((K * MSG, T), 0)
    lane_slot = iota((128, T), 0)
    picks = [jnp.zeros((K * MSG, T), F32) for _ in range(4)]
    gate_rows = jnp.zeros((K * MSG, 128), F32)
    gates = gates_ref[...].astype(F32)
    for k, (blk, rank) in enumerate(own):
        at = slots - blk * PAD
        picks[3] += (at == rank).astype(F32)
        for m in range(3):
            spare = jnp.where(rank - 3 * third(rank) == m, SLOT + third(rank), -K * MSG)
            picks[m] += (at == spare).astype(F32)
        gate_at = jnp.where(lane_slot == rank, gates[k : k + 1], 0.0).astype(BF16)
        gate_rows += mm_nt(hot(at == SLOT), gate_at)
    picks_t = [jnp.transpose(p).astype(BF16) for p in picks]
    picks = [p.astype(BF16) for p in picks]
    og_copy.wait()

    HEAD = max(1, K // 4)

    def a_send(first, last):
        for g in range(first, last, HEAD):
            rows = slice(g * MSG, (g + HEAD) * MSG)
            for m in range(3):
                both = mm(picks[3][rows], og_ref[:, segs[m]]) + mm(picks[m][rows], og_ref[:, tail])
                send[rows, segs[m]] = both.astype(BF16)
            rest = mm(picks[3][rows], og_ref[:, segs[3]])
            rest = jnp.concatenate([rest[:, :128] + gate_rows[rows], rest[:, 128:]], axis=1)
            send[rows, segs[3]] = rest.astype(BF16)
            for c in range(g, g + HEAD):
                for d in range(G):
                    at = pl.ds((c * G + d) * PAD, PAD)
                    if c or d:
                        remote(send.at[at], recv.at[at], s1s, s1r.at[c], peer(c, d))
        if first == 0:
            recv[:PAD] = send[:PAD]

    a_send(0, K // 2)
    TB[:T] = og_ref[:, DA:]
    for m in range(4):
        mt[m] = picks_t[m]

    def row_parts(i):
        j = jnp.zeros(i.shape, jnp.int32)
        for k in range(1, NX):
            j += (i >= k * BLK).astype(jnp.int32)
        rest = i - j * BLK
        return j, shr(rest, LG), rest & (G - 1)

    def places(shape, dim):
        _, r, d = row_parts(iota(shape, dim))
        at = iota(shape, 1 - dim) - d * PAD
        tails = [hot((at == SLOT + third(r)) & (r - 3 * third(r) == m)) for m in range(3)]
        return tails + [hot(at == r)]

    compact = places((BLK, MSG), 0)
    expand = places((MSG, BLK), 1)
    gate_pick = hot(iota((PAD, MSG), 1) == iota((PAD, MSG), 0) * PAD + SLOT)
    of_source = hot((iota((BLK, PAD), 0) & (G - 1)) == iota((BLK, PAD), 1))
    by_source = hot((iota((PAD, BLK), 1) & (G - 1)) == iota((PAD, BLK), 0))
    slot_mask = iota((BLK, 128), 1) == shr(iota((BLK, 128), 0), LG)
    j_i, r_i, d_i = row_parts(iota((ROWS, ROWS), 0))
    perm[...] = hot(iota((ROWS, ROWS), 1) == d_i * MB + j_i * SLOT + r_i)
    j_l, r_l, d_l = row_parts(iota((ROWS, ROWS), 1))
    permT[...] = hot(iota((ROWS, ROWS), 0) == d_l * MB + j_l * SLOT + r_l)

    def sort_saved():
        row, col = iota((K * NX * 4 * G, 4 * Q), 0), iota((K * NX * 4 * G, 4 * Q), 1)
        r, d, j, c = shr(row, LG) & 3, row & (G - 1), shr(row, LG + 2) & (NX - 1), shr(row, LG + 4)
        if even:
            dz, dc = d, c & (CORES - 1)
            dy = (shr(c, LCO) + C - dz) & (C - 1)
        else:
            dz, dy, dc = c, shr(d, LCO), d & (CORES - 1)
        node = ((y + YS - dy) & (YS - 1)) * CORES + ((core + CORES - dc) & (CORES - 1))
        q = node * (C * NX) + ((z + C - dz) & (C - 1)) * NX + ((x + j) & (NX - 1))
        order = hot(col == r * Q + q)
        wait_for(XP.at[pl.ds(first_row, 4 * Q), pl.ds(0, QUADS * 2 * H)], ssem)
        NS = min(TILE, 2 * H)
        for p in range(QUADS):
            for i in range(2 * H // NS):
                cols = slice(p * 2 * H + i * NS, p * 2 * H + (i + 1) * NS)
                out = mm(order, XP[first_row : first_row + 4 * Q, cols]).astype(BF16)
                for g in range(K * NX):
                    at = g * BLK + p * 4 * G
                    saved[at : at + 4 * G, i * NS : (i + 1) * NS] = out[g * 4 * G : (g + 1) * 4 * G]

    def b_forward():
        h = T // 2
        wait_for(TB.at[pl.ds(3 * T, T)], tbr.at[0])
        remote(TB.at[pl.ds(3 * T, h)], TB.at[pl.ds(2 * T, h)], tbs, tbr.at[2], right)
        wait_for(TB.at[pl.ds(T, T)], tbr.at[1])
        remote(TB.at[pl.ds(T + h, h)], TB.at[pl.ds(2 * T + h, h)], tbs, tbr.at[2], left)

    def b_routes():
        wait_for(IDS.at[pl.ds(1, NX - 1)], idsr)
        return [own] + [route(IDS[j, :2]) for j in range(1, NX)]

    def b_part(ref, c, lead):
        lo = MB if c == 0 else 0
        return ref.at[lead, pl.ds(lo, ROWS - lo)] if lead is not None else ref.at[pl.ds(lo, ROWS - lo)]

    def b_select(c, routes):
        slot = c % NSB
        at = iota((ROWS, T), 0)
        parts = []
        for j in range(NX):
            part = jnp.zeros((ROWS, T), F32)
            for blk, rank in routes[j]:
                part += (at == (blk - c * G) * MB + j * SLOT + rank).astype(F32)
            parts.append(part)
            selT[j * T : (j + 1) * T, c * ROWS : (c + 1) * ROWS] = jnp.transpose(part).astype(BF16)
        sel = jnp.concatenate(parts, axis=1).astype(BF16)
        if c == 0:
            wait_for(TB.at[pl.ds(2 * T, T)], tbr.at[2])
        if c >= NSB and (G > 1 or c > NSB):
            wait_for(b_part(sendB, c - NSB, slot), sbs.at[slot])
        for i in range(DB // TILE):
            cols = slice(i * TILE, (i + 1) * TILE)
            sendB[slot, :, cols] = mm(sel, TB[:, cols]).astype(BF16)
        for d in range(G):
            if c or d:
                remote(
                    sendB.at[slot, pl.ds(d * MB, MB)], Y.at[pl.ds(c * ROWS + d * MB, MB), colsB],
                    sbs.at[slot], sbr.at[c], peer(c, d),
                )
            else:
                Y[:MB, DA:] = sendB[slot, :MB]

    def b_land(c):
        lo = MB if c == 0 else 0
        if ROWS > lo:
            wait_for(Y.at[pl.ds(c * ROWS + lo, ROWS - lo), colsB], sbr.at[c])
        rows = slice(c * ROWS, (c + 1) * ROWS)
        for i in range(DB // TILE):
            cols = slice(DA + i * TILE, DA + (i + 1) * TILE)
            Y[rows, cols] = mm(perm[...], Y[rows, cols]).astype(BF16)

    def yrows(c, j, lo=0, size=None):
        return pl.ds(c * ROWS + j * BLK + lo, BLK if size is None else size)

    def gather_start(c):
        lo = PAD if c == 0 else 0
        if MSG > lo:
            wait_for(recv.at[pl.ds(c * MSG + lo, MSG - lo)], s1r.at[c])
        own_rows = slice(c * ROWS, c * ROWS + BLK)
        msg = slice(c * MSG, (c + 1) * MSG)
        last = jnp.zeros((BLK, S), F32)
        for m in range(4):
            Y[own_rows, segs[m]] = mm(compact[3], recv[msg, segs[m]]).astype(BF16)
            if m < 3:
                last += mm(compact[m], recv[msg, segs[m]])
        Y[own_rows, tail] = last.astype(BF16)
        GB[c, 0] = mm(gate_pick, recv[msg, extra]).astype(BF16)
        remote(Y.at[yrows(c, 0), colsA], Y.at[yrows(c, 3), colsA], ags, agr.at[c, 0], right)
        remote(Y.at[yrows(c, 0), colsA], Y.at[yrows(c, 1), colsA], ags, agr.at[c, 1], left)
        for k in range(1, NX):
            remote(GB.at[c, 0], GB.at[c, NX - k], gbs, gbr.at[c], along(k))

    def cut_of(c):
        return BLK * (2 - c % 2) // 3

    def gather_forward(c):
        wait_for(Y.at[yrows(c, 3), colsA], agr.at[c, 0])
        cut = cut_of(c)
        remote(Y.at[yrows(c, 3, 0, cut), colsA], Y.at[yrows(c, 2, 0, cut), colsA], ags, agr.at[c, 2], right)
        wait_for(Y.at[yrows(c, 1), colsA], agr.at[c, 1])
        rest = BLK - cut
        remote(Y.at[yrows(c, 1, cut, rest), colsA], Y.at[yrows(c, 2, cut, rest), colsA], ags, agr.at[c, 2], left)

    def compute(c):
        base = c % NSLOT * ROWS
        wait_for(Y.at[yrows(c, 2), colsA], agr.at[c, 2])
        wait_for(GB.at[c, pl.ds(1, NX - 1)], gbr.at[c])
        b_land(c)
        if c == 0:
            wd_copy.wait()
        NT = min(TILE, H)
        for i in range(H // NT):
            dact[:, i * NT : (i + 1) * NT] = mm_nt(Y[c * ROWS : (c + 1) * ROWS, :], wd[i * NT : (i + 1) * NT, :])
        for j in range(NX):
            rows = slice(j * BLK, (j + 1) * BLK)
            at = c * ROWS + j * BLK
            a = saved[at : at + BLK, :H].astype(F32)
            b = saved[at : at + BLK, H:].astype(F32)
            da = dact[rows, :]
            spread = mm(of_source, GB[c, j])
            scale = jnp.sum(jnp.where(slot_mask, spread, 0.0), axis=1, keepdims=True)
            s = jax.nn.sigmoid(a)
            act = a * s
            hidden = act * b
            part = jnp.sum(hidden * da, axis=1, keepdims=True)
            parts = jnp.where(slot_mask, part, 0.0).astype(BF16)
            GPS[c, j] = mm(by_source, parts).astype(BF16)
            dh = scale * da
            dpre[rows, :H] = (dh * b * s * (1.0 + a * (1.0 - s))).astype(BF16)
            dpre[rows, H:] = (dh * act).astype(BF16)
            dact[rows, :] = scale * hidden
        for k in range(1, NX):
            remote(GPS.at[c, k], GPR.at[c, NX - k], gps, gpr.at[c], along(k))
        if c == 0:
            wgu_copy.wait()
        if c >= NSLOT:
            o = c - NSLOT
            wait_for(XP.at[pl.ds(base + BLK, ROWS - BLK), colsA], xps.at[o])
            lo = MB if o == 0 else 0
            if ROWS > lo:
                wait_for(XP.at[pl.ds(base + lo, ROWS - lo), colsB], xpbs.at[o])

        def tile_b(i, _):
            cols = pl.ds(pl.multiple_of(DA + i * WB, 128), WB)
            XP[base : base + ROWS, cols] = mm(permT[...], mm_nt(dpre[...], wgu[cols, :]).astype(BF16)).astype(BF16)
            return 0

        lax.fori_loop(0, DB // WB, tile_b, 0)
        for d in range(G):
            if c or d:
                remote(
                    XP.at[pl.ds(base + d * MB, MB), colsB], backB.at[pl.ds((c * G + d) * MB, MB)],
                    xpbs.at[c], bbr.at[c], source(c, d),
                )
            else:
                backB[:MB] = XP[base : base + MB, DA:]

        def tile_a(i, _):
            cols = pl.ds(pl.multiple_of(i * WA, TILE), WA)
            XP[base : base + ROWS, cols] = mm_nt(dpre[...], wgu[cols, :]).astype(BF16)
            return 0

        lax.fori_loop(0, DA // WA, tile_a, 0)

        cut = cut_of(c)
        rest = BLK - cut

        def part_of(j, lo, size):
            return XP.at[pl.ds(base + j * BLK + lo, size), colsA]

        remote(part_of(2, 0, cut), RA.at[c, pl.ds(0, cut)], xps.at[c], rar.at[c, 0], right)
        remote(part_of(2, cut, rest), RA.at[c, pl.ds(cut, rest)], xps.at[c], rar.at[c, 1], left)
        remote(part_of(1, cut, rest), RB.at[c, 0, pl.ds(cut, rest)], xps.at[c], rbr.at[c, 0], right)
        remote(part_of(3, 0, cut), RB.at[c, 1, pl.ds(0, cut)], xps.at[c], rbr.at[c, 1], left)
        wT[:, c * ROWS : (c + 1) * ROWS] = jnp.transpose(dact[...]).astype(BF16)

    def reduce_middle(c):
        base = c % NSLOT * ROWS
        cut = cut_of(c)
        for side, j, lo, size, dev in ((0, 1, 0, cut, right), (1, 3, cut, BLK - cut, left)):
            wait_for(RA.at[c, pl.ds(lo, size)], rar.at[c, side])
            at = base + j * BLK + lo
            rows = slice(at, at + size)
            XP[rows, :DA] = (XP[rows, :DA].astype(F32) + RA[c, lo : lo + size].astype(F32)).astype(BF16)
            remote(XP.at[pl.ds(at, size), colsA], RB.at[c, side, pl.ds(lo, size)], xps.at[c], rbr.at[c, side], dev)

    def reduce_end(c):
        base = c % NSLOT * ROWS
        wait_for(GPR.at[c, pl.ds(1, NX - 1)], gpr.at[c])
        total = GPS[c, 0].astype(F32)
        for k in range(1, NX):
            total += GPR[c, k].astype(F32)
        high = total.astype(BF16)
        low = (total - high.astype(F32)).astype(BF16)
        up = iota((MSG, PAD), 0) - iota((MSG, PAD), 1) * PAD
        gate_back = mm(hot(up == SLOT), high) + mm(hot(up == SLOT + 1), low)
        wait_for(RB.at[c, 0], rbr.at[c, 0])
        wait_for(RB.at[c, 1], rbr.at[c, 1])
        msg = slice(c * MSG, (c + 1) * MSG)
        def whole(cols):
            part = XP[base : base + BLK, cols].astype(F32) + RB[c, 0, :, cols].astype(F32)
            return (part + RB[c, 1, :, cols].astype(F32)).astype(BF16)

        last = whole(tail)
        for m in range(3):
            recv[msg, segs[m]] = (mm(expand[3], whole(segs[m])) + mm(expand[m], last)).astype(BF16)
        rest = mm(expand[3], whole(segs[3]))
        rest = jnp.concatenate([rest[:, :128] + gate_back, rest[:, 128:]], axis=1)
        recv[msg, segs[3]] = rest.astype(BF16)
        for d in range(G):
            rows = pl.ds((c * G + d) * PAD, PAD)
            if c or d:
                remote(recv.at[rows], back.at[rows], rets, backr.at[c], source(c, d))
        if c == 0:
            back[:PAD] = recv[:PAD]

    def b_sum():
        for c in range(K):
            lo = MB if c == 0 else 0
            if ROWS > lo:
                wait_for(backB.at[pl.ds(c * ROWS + lo, ROWS - lo)], bbr.at[c])
        wait_for(TB.at[pl.ds(0, 3 * T)], tbs)
        for i in range(DB // TILE):
            cols = slice(i * TILE, (i + 1) * TILE)
            TB[:, cols] = mm(selT[...], backB[:, cols]).astype(BF16)
        h = T // 2
        remote(TB.at[pl.ds(2 * T, h)], RAB.at[0], pbs, rabr.at[0], right)
        remote(TB.at[pl.ds(2 * T + h, h)], RAB.at[1], pbs, rabr.at[1], left)
        remote(TB.at[pl.ds(T + h, h)], RBB.at[0, pl.ds(h, h)], pbs, rbbr.at[0], right)
        remote(TB.at[pl.ds(3 * T, h)], RBB.at[1, pl.ds(0, h)], pbs, rbbr.at[1], left)

    def b_middle():
        h = T // 2
        for side, j, lo, dev in ((0, 1, 0, right), (1, 3, h, left)):
            wait_for(RAB.at[side], rabr.at[side])
            rows = slice(j * T + lo, j * T + lo + h)
            TB[rows, :] = (TB[rows, :].astype(F32) + RAB[side].astype(F32)).astype(BF16)
            remote(TB.at[pl.ds(j * T + lo, h)], RBB.at[side, pl.ds(lo, h)], pbs, rbbr.at[side], dev)

    def b_end():
        wait_for(RBB.at[0], rbbr.at[0])
        wait_for(RBB.at[1], rbbr.at[1])
        ig_ref[:, DA:] = (TB[:T].astype(F32) + RBB[0].astype(F32) + RBB[1].astype(F32)).astype(BF16)

    tiles = D // WG

    def weight_grad(first, last):
        def tile(i, _):
            cols = pl.ds(pl.multiple_of(i * WG, TILE), WG)
            dg_ref[:, cols] = mm(wT[...], Y[:, cols]).astype(BF16)
            return 0

        lax.fori_loop(first, last, tile, 0)

    b_forward()
    gather_start(0)
    routes = b_routes()
    b_select(0, routes)
    b_select(1, routes)
    a_send(K // 2, K)
    gather_start(1)
    gather_forward(0)
    for c in range(2, min(4, K)):
        b_select(c, routes)
    sort_saved()
    for c in range(2, min(4, K)):
        gather_start(c)
        if c == 2:
            gather_forward(1)
    if K == 2:
        gather_forward(1)
    for c in range(4, K):
        b_select(c, routes)
    ended = 0
    for c in range(K):
        compute(c)
        if c + 2 < K:
            gather_forward(c + 2)
        if c + 4 < K:
            gather_start(c + 4)
        if c >= 1:
            reduce_middle(c - 1)
        done = c - 2 if c > K // 2 else c - 3
        for o in range(ended, done + 1):
            reduce_end(o)
        ended = max(ended, done + 1)
    part = tiles // 3
    weight_grad(0, part)
    reduce_middle(K - 1)
    for o in range(ended, K - 1):
        reduce_end(o)
    b_sum()
    weight_grad(part, tiles)
    reduce_end(K - 1)
    b_middle()
    b_end()

    for c in range(K):
        lo = PAD if c == 0 else 0
        if MSG > lo:
            wait_for(back.at[pl.ds(c * MSG + lo, MSG - lo)], backr.at[c])
    last = jnp.zeros((T, S), F32)
    for m in range(4):
        ig_ref[:, segs[m]] = mm(mt[3], back[:, segs[m]]).astype(BF16)
        if m < 3:
            last += mm(mt[m], back[:, segs[m]])
    ig_ref[:, tail] = last.astype(BF16)
    back_gates = jnp.transpose(back[:, extra].astype(F32)).astype(BF16)
    for k, (blk, rank) in enumerate(own):
        at = slots - blk * PAD
        found = mm(back_gates, hot((at == SLOT) | (at == SLOT + 1)))
        gg_ref[k : k + 1, :] = jnp.sum(jnp.where(lane_slot == rank, found, 0.0), axis=0, keepdims=True)

    wait_for(send.at[pl.ds(0, K * MSG - PAD)], s1s)
    wait_for(recv.at[pl.ds(0, K * MSG - PAD)], rets)
    wait_for(Y.at[pl.ds(0, K * 3 * BLK), colsA], ags)
    wait_for(IDS.at[pl.ds(1, NX - 1)], idss)
    wait_for(TB.at[pl.ds(0, 3 * T)], pbs)
    for c in range(K):
        wait_for(GB.at[c, pl.ds(1, NX - 1)], gbs)
        wait_for(GPS.at[c, pl.ds(1, NX - 1)], gps)
    for c in range(max(0, K - NSB), K):
        lo = MB if c == 0 else 0
        if ROWS > lo:
            wait_for(sendB.at[c % NSB, pl.ds(lo, ROWS - lo)], sbs.at[c % NSB])
    for c in range(max(0, K - NSLOT), K):
        base = c % NSLOT * ROWS
        lo = MB if c == 0 else 0
        wait_for(XP.at[pl.ds(base + BLK, ROWS - BLK), colsA], xps.at[c])
        if ROWS > lo:
            wait_for(XP.at[pl.ds(base + lo, ROWS - lo), colsB], xpbs.at[c])


def body(out_grad, gates, expert_ids, saved_pre, w_gate_up, w_down):
    T, D = out_grad.shape
    B = lax.axis_size("node")
    C = lax.axis_size("local") // NX
    Q, SLOT = saved_pre.shape[1:3]
    H = w_down.shape[1]
    DA = split(D)
    DB, W = D - DA, DA - spare_columns(DA)
    saved = jnp.transpose(saved_pre[0], (1, 0, 2))
    _, K, G, _ = plan(B, C)
    BLK, MSG = G * SLOT, G * PAD
    ROWS = NX * BLK
    NSLOT = min(6, K)
    NSB = K
    vm = pl.BlockSpec(memory_space=pltpu.VMEM)
    anywhere = pl.BlockSpec(memory_space=pl.ANY)
    dma = pltpu.SemaphoreType.DMA
    ig, gg, dg = pl.pallas_call(
        functools.partial(kernel, B, C, SLOT, NSLOT),
        out_shape=(
            pltpu.VMEM((T, D), BF16),
            pltpu.VMEM((2, T), F32),
            pltpu.VMEM((H, D), BF16),
        ),
        in_specs=[vm, vm, anywhere, anywhere, anywhere, anywhere],
        out_specs=(vm, vm, vm),
        scratch_shapes=[
            pltpu.VMEM((T, D), BF16),
            pltpu.VMEM((D, 2 * H), BF16),
            pltpu.VMEM((K * MSG, W), BF16),
            pltpu.VMEM((K * MSG, W), BF16),
            pltpu.VMEM((K * MSG, W), BF16),
            pltpu.VMEM((K * ROWS, D), BF16),
            pltpu.VMEM((K, NX, PAD, 128), BF16),
            pltpu.VMEM((NSLOT * ROWS, D), BF16),
            pltpu.VMEM((K, BLK, DA), BF16),
            pltpu.VMEM((K, 2, BLK, DA), BF16),
            pltpu.VMEM((K, NX, PAD, 128), BF16),
            pltpu.VMEM((K, NX, PAD, 128), BF16),
            pltpu.VMEM((K * ROWS, 2 * H), BF16),
            pltpu.VMEM((H, K * ROWS), BF16),
            pltpu.VMEM((4, T, K * MSG), BF16),
            pltpu.VMEM((ROWS, 2 * H), BF16),
            pltpu.VMEM((ROWS, H), F32),
            pltpu.VMEM((NX, 8, T), jnp.int32),
            pltpu.VMEM((NX * T, DB), BF16),
            pltpu.VMEM((NSB, ROWS, DB), BF16),
            pltpu.VMEM((K * ROWS, DB), BF16),
            pltpu.VMEM((2, T // 2, DB), BF16),
            pltpu.VMEM((2, T, DB), BF16),
            pltpu.VMEM((NX * T, K * ROWS), BF16),
            pltpu.VMEM((ROWS, ROWS), BF16),
            pltpu.VMEM((ROWS, ROWS), BF16),
            dma((3,)),
            dma,
            dma,
            dma((K,)),
            dma,
            dma((K, 3)),
            dma,
            dma((K,)),
            dma((K,)),
            dma((K, 2)),
            dma((K, 2)),
            dma,
            dma((K,)),
            dma,
            dma((K,)),
            dma,
            dma,
            dma,
            dma((3,)),
            dma((NSB,)),
            dma((K,)),
            dma((K,)),
            dma((K,)),
            dma,
            dma((2,)),
            dma((2,)),
        ],
        compiler_params=pltpu.CompilerParams(
            collective_id=0, has_side_effects=True, vmem_limit_bytes=59 * 1024 * 1024
        ),
        cost_estimate=pl.CostEstimate(
            flops=2 * K * ROWS * D * 4 * H, bytes_accessed=25_000_000, transcendentals=K * ROWS * H
        ),
        name="moe_backward",
    )(expert_ids.T, gates.T, out_grad, saved, w_gate_up[0], w_down[0])
    return ig, gg.T, dg[None]


def solution(mesh):
    in_specs = (
        P(("node", "local"), None),
        P(("node", "local"), None),
        P(("node", "local"), None),
        P(("node", "local"), None, None, None),
        P(("node", "local"), None, None),
        P(("node", "local"), None, None),
    )
    out_specs = (
        P(("node", "local"), None),
        P(("node", "local"), None),
        P(("node", "local"), None, None),
    )
    return jax.shard_map(body, mesh=mesh, in_specs=in_specs, out_specs=out_specs, check_vma=False)
```

```python
import functools

import jax
import jax.numpy as jnp
from jax import lax
from jax.experimental import pallas as pl
from jax.experimental.pallas import tpu as pltpu
from jax.sharding import PartitionSpec as P

NX = 4
PAD = 16
TILE = 256
MESH = pl.DeviceIdType.MESH
F32 = jnp.float32
BF16 = jnp.bfloat16


def split(D):
    return max(3 * TILE, 9 * D // 14 // TILE * TILE)


def spare_columns(DA):
    return (DA - 128) // 4 // 128 * 128


def iota(shape, dim):
    return lax.broadcasted_iota(jnp.int32, shape, dim)


def shr(v, bits):
    return lax.shift_right_logical(v, jnp.full(v.shape, bits, jnp.int32))


def log2(size):
    return size.bit_length() - 1


def mm(a, b):
    return jnp.dot(a, b, preferred_element_type=F32)


def mm_nt(a, b):
    return lax.dot_general(a, b, (((1,), (1,)), ((), ())), preferred_element_type=F32)


def hot(mask):
    return mask.astype(F32).astype(BF16)


def plan(B, C):
    cores = 2 if B > C else 1
    even = B // cores == C
    chunks = C * cores if even else C
    return cores, chunks, B * C // chunks, even


def kernel(
    B, C, SLOT, NSLOT,
    ids_ref, gates_ref, og_hbm, saved_hbm, wgu_hbm, wd_hbm,
    ig_ref, gg_ref, dg_ref,
    og_ref, wgu, send, recv, back, Y, GB, XP, RA, RB, GPS, GPR, saved, wT, early, mt, dpre, dact,
    IDS, TB, sendB, backB, RAB, RBB, selT, perm, permT,
    wsem, ssem, s1s, s1r, ags, agr, gbs, gbr, xps, rar, rbr, gps, gpr, rets, backr,
    idss, idsr, tbs, tbr, sbs, sbr, xpbs, bbr, pbs, rabr, rbbr,
):
    T, D = og_ref.shape
    H = dg_ref.shape[0]
    wd = dg_ref
    DA = split(D)
    DB = D - DA
    S = spare_columns(DA)
    W = DA - S
    segs = [slice(m * S, (m + 1) * S) for m in range(3)] + [slice(3 * S, W)]
    tail = slice(W, DA)
    extra = slice(3 * S, 3 * S + 128)
    WA = 3 * TILE if DA % (3 * TILE) == 0 else TILE
    WB = DB // 2 if DB % 256 == 0 else DB
    WG = 2 * TILE
    CORES, K, G, even = plan(B, C)
    BLK = G * SLOT
    MSG = G * PAD
    MB = NX * SLOT
    ROWS = NX * BLK
    NSB = sendB.shape[0]
    LG, LC = log2(G), log2(C)
    colsA, colsB = pl.ds(0, DA), pl.ds(DA, DB)
    n = lax.axis_index("node")
    l = lax.axis_index("local")
    z, x = l // NX, l % NX
    right = (n, z * NX + (x + 1) % NX)
    left = (n, z * NX + (x + NX - 1) % NX)

    YS = B // CORES
    y, core = n // CORES, n % CORES
    LCO = log2(CORES)

    def offsets(c, d):
        return (d, (c // CORES + C - d) % C, c % CORES) if even else (c, d // CORES, d % CORES)

    def peer(c, d):
        dz, dy, dc = offsets(c, d)
        return (((y + dy) % YS) * CORES + (core + dc) % CORES, ((z + dz) % C) * NX + x)

    def source(c, d):
        dz, dy, dc = offsets(c, d)
        return (((y + YS - dy) % YS) * CORES + (core + CORES - dc) % CORES, ((z + C - dz) % C) * NX + x)

    def along(k):
        return (n, z * NX + (x + k) % NX)

    def remote(src, dst, ssem_, rsem_, dev):
        pltpu.make_async_remote_copy(
            src_ref=src, dst_ref=dst, send_sem=ssem_, recv_sem=rsem_, device_id=dev, device_id_type=MESH
        ).start()

    def wait_for(ref, sem):
        pltpu.make_async_copy(ref, ref, sem).wait()

    barrier = pltpu.get_barrier_semaphore()
    count = 0
    for k in range(1, NX):
        pl.semaphore_signal(barrier, inc=1, device_id=along(k), device_id_type=MESH)
        count += 1
    for c in range(K):
        for d in range(G):
            if c or d:
                pl.semaphore_signal(barrier, inc=1, device_id=peer(c, d), device_id_type=MESH)
                count += 1

    wd_copy = pltpu.make_async_copy(wd_hbm, wd, wsem.at[0])
    wgu_copy = pltpu.make_async_copy(wgu_hbm, wgu, wsem.at[1])

    Q = C * NX * B
    QUADS = SLOT // 4
    first_row = NSLOT * ROWS - 4 * Q

    def stage(r):
        dst = XP.at[pl.ds(first_row + r % 4 * Q, Q), pl.ds(r // 4 * 2 * H, 2 * H)]
        return pltpu.make_async_copy(saved_hbm.at[r], dst, ssem)

    og_copy = pltpu.make_async_copy(og_hbm, og_ref, wsem.at[2])
    og_copy.start()
    for r in range(SLOT):
        stage(r).start()
    wd_copy.start()
    wgu_copy.start()

    IDS[0, :2] = ids_ref[...]
    pl.semaphore_wait(barrier, count)
    remote(og_hbm.at[:, colsB], TB.at[pl.ds(3 * T, T)], tbs, tbr.at[0], right)
    remote(og_hbm.at[:, colsB], TB.at[pl.ds(T, T)], tbs, tbr.at[1], left)
    for k in range(1, NX):
        remote(IDS.at[0], IDS.at[NX - k], idss, idsr, along(k))

    NE = max(8, B * C)
    before = hot(iota((T, T), 0) < iota((T, T), 1))
    expert_row = iota((NE, T), 0)

    def route(ids):
        experts = [ids[k : k + 1] for k in range(2)]
        hits = [expert_row == e for e in experts]
        per_token = hits[0].astype(F32) + hits[1].astype(F32)
        earlier = mm(per_token.astype(BF16), before)
        out = []
        for k in range(2):
            rank = jnp.sum(jnp.where(hits[k], earlier, 0.0), axis=0, keepdims=True).astype(jnp.int32)
            zz = experts[k] & (C - 1)
            node = shr(experts[k], LC)
            dz = (zz - z + C) & (C - 1)
            dy = (shr(node, LCO) - y + YS) & (YS - 1)
            dc = (node - core + CORES) & (CORES - 1)
            blk = (((dy + dz) & (C - 1)) * CORES + dc) * G + dz if even else dz * G + dy * CORES + dc
            out.append((blk, rank))
        return out

    own = route(ids_ref[...])
    def third(v):
        return shr(v * 11, 5)

    slots = iota((K * MSG, T), 0)
    lane_slot = iota((128, T), 0)
    picks = [jnp.zeros((K * MSG, T), F32) for _ in range(4)]
    gate_rows = jnp.zeros((K * MSG, 128), F32)
    gates = gates_ref[...].astype(F32)
    for k, (blk, rank) in enumerate(own):
        at = slots - blk * PAD
        picks[3] += (at == rank).astype(F32)
        for m in range(3):
            spare = jnp.where(rank - 3 * third(rank) == m, SLOT + third(rank), -K * MSG)
            picks[m] += (at == spare).astype(F32)
        gate_at = jnp.where(lane_slot == rank, gates[k : k + 1], 0.0).astype(BF16)
        gate_rows += mm_nt(hot(at == SLOT), gate_at)
    picks_t = [jnp.transpose(p).astype(BF16) for p in picks]
    picks = [p.astype(BF16) for p in picks]
    og_copy.wait()

    HEAD = max(1, K // 4)

    def a_send(first, last):
        for g in range(first, last, HEAD):
            rows = slice(g * MSG, (g + HEAD) * MSG)
            for m in range(3):
                both = mm(picks[3][rows], og_ref[:, segs[m]]) + mm(picks[m][rows], og_ref[:, tail])
                send[rows, segs[m]] = both.astype(BF16)
            rest = mm(picks[3][rows], og_ref[:, segs[3]])
            rest = jnp.concatenate([rest[:, :128] + gate_rows[rows], rest[:, 128:]], axis=1)
            send[rows, segs[3]] = rest.astype(BF16)
            for c in range(g, g + HEAD):
                for d in range(G):
                    at = pl.ds((c * G + d) * PAD, PAD)
                    if c or d:
                        remote(send.at[at], recv.at[at], s1s, s1r.at[c], peer(c, d))
        if first == 0:
            recv[:PAD] = send[:PAD]

    a_send(0, max(1, 3 * K // 4))
    TB[:T] = og_ref[:, DA:]
    for m in range(4):
        mt[m] = picks_t[m]

    def row_parts(i):
        j = jnp.zeros(i.shape, jnp.int32)
        for k in range(1, NX):
            j += (i >= k * BLK).astype(jnp.int32)
        rest = i - j * BLK
        return j, shr(rest, LG), rest & (G - 1)

    def places(shape, dim):
        _, r, d = row_parts(iota(shape, dim))
        at = iota(shape, 1 - dim) - d * PAD
        tails = [hot((at == SLOT + third(r)) & (r - 3 * third(r) == m)) for m in range(3)]
        return tails + [hot(at == r)]

    compact = places((BLK, MSG), 0)
    expand = places((MSG, BLK), 1)
    gate_pick = hot(iota((PAD, MSG), 1) == iota((PAD, MSG), 0) * PAD + SLOT)
    of_source = hot((iota((BLK, PAD), 0) & (G - 1)) == iota((BLK, PAD), 1))
    by_source = hot((iota((PAD, BLK), 1) & (G - 1)) == iota((PAD, BLK), 0))
    slot_mask = iota((BLK, 128), 1) == shr(iota((BLK, 128), 0), LG)
    j_i, r_i, d_i = row_parts(iota((ROWS, ROWS), 0))
    perm[...] = hot(iota((ROWS, ROWS), 1) == d_i * MB + j_i * SLOT + r_i)
    j_l, r_l, d_l = row_parts(iota((ROWS, ROWS), 1))
    permT[...] = hot(iota((ROWS, ROWS), 0) == d_l * MB + j_l * SLOT + r_l)

    def sort_saved():
        row, col = iota((K * NX * 4 * G, 4 * Q), 0), iota((K * NX * 4 * G, 4 * Q), 1)
        r, d, j, c = shr(row, LG) & 3, row & (G - 1), shr(row, LG + 2) & (NX - 1), shr(row, LG + 4)
        if even:
            dz, dc = d, c & (CORES - 1)
            dy = (shr(c, LCO) + C - dz) & (C - 1)
        else:
            dz, dy, dc = c, shr(d, LCO), d & (CORES - 1)
        node = ((y + YS - dy) & (YS - 1)) * CORES + ((core + CORES - dc) & (CORES - 1))
        q = node * (C * NX) + ((z + C - dz) & (C - 1)) * NX + ((x + j) & (NX - 1))
        order = hot(col == r * Q + q)
        wait_for(XP.at[pl.ds(first_row, 4 * Q), pl.ds(0, QUADS * 2 * H)], ssem)
        NS = min(TILE, 2 * H)
        for p in range(QUADS):
            for i in range(2 * H // NS):
                cols = slice(p * 2 * H + i * NS, p * 2 * H + (i + 1) * NS)
                out = mm(order, XP[first_row : first_row + 4 * Q, cols]).astype(BF16)
                for g in range(K * NX):
                    at = g * BLK + p * 4 * G
                    saved[at : at + 4 * G, i * NS : (i + 1) * NS] = out[g * 4 * G : (g + 1) * 4 * G]

    def b_forward():
        h = T // 2
        wait_for(TB.at[pl.ds(3 * T, T)], tbr.at[0])
        remote(TB.at[pl.ds(3 * T, h)], TB.at[pl.ds(2 * T, h)], tbs, tbr.at[2], right)
        wait_for(TB.at[pl.ds(T, T)], tbr.at[1])
        remote(TB.at[pl.ds(T + h, h)], TB.at[pl.ds(2 * T + h, h)], tbs, tbr.at[2], left)

    def b_routes():
        wait_for(IDS.at[pl.ds(1, NX - 1)], idsr)
        return [own] + [route(IDS[j, :2]) for j in range(1, NX)]

    def b_part(ref, c, lead):
        lo = MB if c == 0 else 0
        return ref.at[lead, pl.ds(lo, ROWS - lo)] if lead is not None else ref.at[pl.ds(lo, ROWS - lo)]

    def b_select(c, routes):
        slot = c % NSB
        at = iota((ROWS, T), 0)
        parts = []
        for j in range(NX):
            part = jnp.zeros((ROWS, T), F32)
            for blk, rank in routes[j]:
                part += (at == (blk - c * G) * MB + j * SLOT + rank).astype(F32)
            parts.append(part)
            selT[j * T : (j + 1) * T, c * ROWS : (c + 1) * ROWS] = jnp.transpose(part).astype(BF16)
        sel = jnp.concatenate(parts, axis=1).astype(BF16)
        if c == 0:
            wait_for(TB.at[pl.ds(2 * T, T)], tbr.at[2])
        if c >= NSB and (G > 1 or c > NSB):
            wait_for(b_part(sendB, c - NSB, slot), sbs.at[slot])
        for i in range(DB // TILE):
            cols = slice(i * TILE, (i + 1) * TILE)
            sendB[slot, :, cols] = mm(sel, TB[:, cols]).astype(BF16)
        for d in range(G):
            if c or d:
                remote(
                    sendB.at[slot, pl.ds(d * MB, MB)], Y.at[pl.ds(c * ROWS + d * MB, MB), colsB],
                    sbs.at[slot], sbr.at[c], peer(c, d),
                )
            else:
                Y[:MB, DA:] = sendB[slot, :MB]

    def b_land(c):
        lo = MB if c == 0 else 0
        if ROWS > lo:
            wait_for(Y.at[pl.ds(c * ROWS + lo, ROWS - lo), colsB], sbr.at[c])
        rows = slice(c * ROWS, (c + 1) * ROWS)
        for i in range(DB // TILE):
            cols = slice(DA + i * TILE, DA + (i + 1) * TILE)
            Y[rows, cols] = mm(perm[...], Y[rows, cols]).astype(BF16)

    def yrows(c, j, lo=0, size=None):
        return pl.ds(c * ROWS + j * BLK + lo, BLK if size is None else size)

    def gather_start(c):
        lo = PAD if c == 0 else 0
        if MSG > lo:
            wait_for(recv.at[pl.ds(c * MSG + lo, MSG - lo)], s1r.at[c])
        own_rows = slice(c * ROWS, c * ROWS + BLK)
        msg = slice(c * MSG, (c + 1) * MSG)
        last = jnp.zeros((BLK, S), F32)
        for m in range(4):
            Y[own_rows, segs[m]] = mm(compact[3], recv[msg, segs[m]]).astype(BF16)
            if m < 3:
                last += mm(compact[m], recv[msg, segs[m]])
        Y[own_rows, tail] = last.astype(BF16)
        GB[c, 0] = mm(gate_pick, recv[msg, extra]).astype(BF16)
        remote(Y.at[yrows(c, 0), colsA], Y.at[yrows(c, 3), colsA], ags, agr.at[c, 0], right)
        remote(Y.at[yrows(c, 0), colsA], Y.at[yrows(c, 1), colsA], ags, agr.at[c, 1], left)
        for k in range(1, NX):
            remote(GB.at[c, 0], GB.at[c, NX - k], gbs, gbr.at[c], along(k))

    def cut_of(c):
        return BLK * (2 - c % 2) // 3

    def gather_forward(c):
        wait_for(Y.at[yrows(c, 3), colsA], agr.at[c, 0])
        cut = cut_of(c)
        remote(Y.at[yrows(c, 3, 0, cut), colsA], Y.at[yrows(c, 2, 0, cut), colsA], ags, agr.at[c, 2], right)
        wait_for(Y.at[yrows(c, 1), colsA], agr.at[c, 1])
        rest = BLK - cut
        remote(Y.at[yrows(c, 1, cut, rest), colsA], Y.at[yrows(c, 2, cut, rest), colsA], ags, agr.at[c, 2], left)

    def compute(c):
        base = c % NSLOT * ROWS
        wait_for(Y.at[yrows(c, 2), colsA], agr.at[c, 2])
        wait_for(GB.at[c, pl.ds(1, NX - 1)], gbr.at[c])
        b_land(c)
        if c == 0:
            wd_copy.wait()
        NT = min(TILE, H)
        for i in range(H // NT):
            dact[:, i * NT : (i + 1) * NT] = mm_nt(Y[c * ROWS : (c + 1) * ROWS, :], wd[i * NT : (i + 1) * NT, :])
        for j in range(NX):
            rows = slice(j * BLK, (j + 1) * BLK)
            at = c * ROWS + j * BLK
            a = saved[at : at + BLK, :H].astype(F32)
            b = saved[at : at + BLK, H:].astype(F32)
            da = dact[rows, :]
            spread = mm(of_source, GB[c, j])
            scale = jnp.sum(jnp.where(slot_mask, spread, 0.0), axis=1, keepdims=True)
            s = jax.nn.sigmoid(a)
            act = a * s
            hidden = act * b
            part = jnp.sum(hidden * da, axis=1, keepdims=True)
            parts = jnp.where(slot_mask, part, 0.0).astype(BF16)
            GPS[c, j] = mm(by_source, parts).astype(BF16)
            dh = scale * da
            dpre[rows, :H] = (dh * b * s * (1.0 + a * (1.0 - s))).astype(BF16)
            dpre[rows, H:] = (dh * act).astype(BF16)
            dact[rows, :] = scale * hidden
        for k in range(1, NX):
            remote(GPS.at[c, k], GPR.at[c, NX - k], gps, gpr.at[c], along(k))
        if c == 0:
            wgu_copy.wait()
        if c >= NSLOT:
            o = c - NSLOT
            wait_for(XP.at[pl.ds(base + BLK, ROWS - BLK), colsA], xps.at[o])
            lo = MB if o == 0 else 0
            if ROWS > lo:
                wait_for(XP.at[pl.ds(base + lo, ROWS - lo), colsB], xpbs.at[o])

        def tile_a(i, _):
            cols = pl.ds(pl.multiple_of(i * WA, TILE), WA)
            XP[base : base + ROWS, cols] = mm_nt(dpre[...], wgu[cols, :]).astype(BF16)
            return 0

        lax.fori_loop(0, DA // WA, tile_a, 0)

        cut = cut_of(c)
        rest = BLK - cut

        def part_of(j, lo, size):
            return XP.at[pl.ds(base + j * BLK + lo, size), colsA]

        remote(part_of(2, 0, cut), RA.at[c, pl.ds(0, cut)], xps.at[c], rar.at[c, 0], right)
        remote(part_of(2, cut, rest), RA.at[c, pl.ds(cut, rest)], xps.at[c], rar.at[c, 1], left)
        remote(part_of(1, cut, rest), RB.at[c, 0, pl.ds(cut, rest)], xps.at[c], rbr.at[c, 0], right)
        remote(part_of(3, 0, cut), RB.at[c, 1, pl.ds(0, cut)], xps.at[c], rbr.at[c, 1], left)
        def tile_b(i, _):
            cols = pl.ds(pl.multiple_of(DA + i * WB, 128), WB)
            XP[base : base + ROWS, cols] = mm(permT[...], mm_nt(dpre[...], wgu[cols, :]).astype(BF16)).astype(BF16)
            return 0

        lax.fori_loop(0, DB // WB, tile_b, 0)
        for d in range(G):
            if c or d:
                remote(
                    XP.at[pl.ds(base + d * MB, MB), colsB], backB.at[pl.ds((c * G + d) * MB, MB)],
                    xpbs.at[c], bbr.at[c], source(c, d),
                )
            else:
                backB[:MB] = XP[base : base + MB, DA:]

        wT[:, c * ROWS : (c + 1) * ROWS] = jnp.transpose(dact[...]).astype(BF16)

    def reduce_middle(c):
        base = c % NSLOT * ROWS
        cut = cut_of(c)
        for side, j, lo, size, dev in ((0, 1, 0, cut, right), (1, 3, cut, BLK - cut, left)):
            wait_for(RA.at[c, pl.ds(lo, size)], rar.at[c, side])
            at = base + j * BLK + lo
            rows = slice(at, at + size)
            XP[rows, :DA] = (XP[rows, :DA].astype(F32) + RA[c, lo : lo + size].astype(F32)).astype(BF16)
            remote(XP.at[pl.ds(at, size), colsA], RB.at[c, side, pl.ds(lo, size)], xps.at[c], rbr.at[c, side], dev)

    def reduce_end(c):
        base = c % NSLOT * ROWS
        wait_for(GPR.at[c, pl.ds(1, NX - 1)], gpr.at[c])
        total = GPS[c, 0].astype(F32)
        for k in range(1, NX):
            total += GPR[c, k].astype(F32)
        high = total.astype(BF16)
        low = (total - high.astype(F32)).astype(BF16)
        up = iota((MSG, PAD), 0) - iota((MSG, PAD), 1) * PAD
        gate_back = mm(hot(up == SLOT), high) + mm(hot(up == SLOT + 1), low)
        wait_for(RB.at[c, 0], rbr.at[c, 0])
        wait_for(RB.at[c, 1], rbr.at[c, 1])
        msg = slice(c * MSG, (c + 1) * MSG)
        def whole(cols):
            part = XP[base : base + BLK, cols].astype(F32) + RB[c, 0, :, cols].astype(F32)
            return (part + RB[c, 1, :, cols].astype(F32)).astype(BF16)

        last = whole(tail)
        for m in range(3):
            recv[msg, segs[m]] = (mm(expand[3], whole(segs[m])) + mm(expand[m], last)).astype(BF16)
        rest = mm(expand[3], whole(segs[3]))
        rest = jnp.concatenate([rest[:, :128] + gate_back, rest[:, 128:]], axis=1)
        recv[msg, segs[3]] = rest.astype(BF16)
        for d in range(G):
            rows = pl.ds((c * G + d) * PAD, PAD)
            if c or d:
                remote(recv.at[rows], back.at[rows], rets, backr.at[c], source(c, d))
        if c == 0:
            back[:PAD] = recv[:PAD]

    def b_sum():
        for c in range(K):
            lo = MB if c == 0 else 0
            if ROWS > lo:
                wait_for(backB.at[pl.ds(c * ROWS + lo, ROWS - lo)], bbr.at[c])
        wait_for(TB.at[pl.ds(0, 3 * T)], tbs)
        for i in range(DB // TILE):
            cols = slice(i * TILE, (i + 1) * TILE)
            TB[:, cols] = mm(selT[...], backB[:, cols]).astype(BF16)
        h = T // 2
        remote(TB.at[pl.ds(2 * T, h)], RAB.at[0], pbs, rabr.at[0], right)
        remote(TB.at[pl.ds(2 * T + h, h)], RAB.at[1], pbs, rabr.at[1], left)
        remote(TB.at[pl.ds(T + h, h)], RBB.at[0, pl.ds(h, h)], pbs, rbbr.at[0], right)
        remote(TB.at[pl.ds(3 * T, h)], RBB.at[1, pl.ds(0, h)], pbs, rbbr.at[1], left)

    def b_middle():
        h = T // 2
        for side, j, lo, dev in ((0, 1, 0, right), (1, 3, h, left)):
            wait_for(RAB.at[side], rabr.at[side])
            rows = slice(j * T + lo, j * T + lo + h)
            TB[rows, :] = (TB[rows, :].astype(F32) + RAB[side].astype(F32)).astype(BF16)
            remote(TB.at[pl.ds(j * T + lo, h)], RBB.at[side, pl.ds(lo, h)], pbs, rbbr.at[side], dev)

    def b_end():
        wait_for(RBB.at[0], rbbr.at[0])
        wait_for(RBB.at[1], rbbr.at[1])
        ig_ref[:, DA:] = (TB[:T].astype(F32) + RBB[0].astype(F32) + RBB[1].astype(F32)).astype(BF16)

    tiles = D // WG

    def weight_grad(first, last):
        def tile(i, _):
            cols = pl.ds(pl.multiple_of(i * WG, TILE), WG)
            dg_ref[:, cols] = mm(wT[...], Y[:, cols]).astype(BF16)
            return 0

        lax.fori_loop(first, last, tile, 0)

    b_forward()
    gather_start(0)
    routes = b_routes()
    b_select(0, routes)
    b_select(1, routes)
    a_send(max(1, 3 * K // 4), K)
    gather_start(1)
    gather_forward(0)
    for c in range(2, min(4, K)):
        b_select(c, routes)
    sort_saved()
    for c in range(2, min(4, K)):
        gather_start(c)
        if c == 2:
            gather_forward(1)
    if K == 2:
        gather_forward(1)
    for c in range(4, K):
        b_select(c, routes)
    ended = 0
    for c in range(K):
        compute(c)
        if c + 2 < K:
            gather_forward(c + 2)
        if c + 4 < K:
            gather_start(c + 4)
        if c >= 1:
            reduce_middle(c - 1)
        done = c - 2 if c > K // 2 else c - 3
        for o in range(ended, done + 1):
            reduce_end(o)
        ended = max(ended, done + 1)
    part = tiles // 3
    weight_grad(0, part)
    reduce_middle(K - 1)
    for o in range(ended, K - 1):
        reduce_end(o)
    b_sum()
    weight_grad(part, tiles)
    reduce_end(K - 1)
    b_middle()
    b_end()

    def own_sums(first, last):
        for c in range(first, last):
            lo = PAD if c == 0 else 0
            if MSG > lo:
                wait_for(back.at[pl.ds(c * MSG + lo, MSG - lo)], backr.at[c])
        rows = slice(first * MSG, last * MSG)
        ends = jnp.zeros((T, S), F32)
        sums = []
        for m in range(4):
            sums.append(mm(mt[3, :, rows], back[rows, segs[m]]))
            if m < 3:
                ends += mm(mt[m, :, rows], back[rows, segs[m]])
        back_gates = jnp.transpose(back[rows, extra].astype(F32)).astype(BF16)
        found = []
        for k, (blk, rank) in enumerate(own):
            at = slots[rows] - blk * PAD
            chosen = mm(back_gates, hot((at == SLOT) | (at == SLOT + 1)))
            found.append(jnp.sum(jnp.where(lane_slot == rank, chosen, 0.0), axis=0, keepdims=True))
        return sums + [ends], found

    first_sums, first_found = own_sums(0, K - 1)
    for m in range(5):
        early[:, (segs + [tail])[m]] = first_sums[m]
    last_sums, last_found = own_sums(K - 1, K)
    for m in range(5):
        cols = (segs + [tail])[m]
        ig_ref[:, cols] = (early[:, cols] + last_sums[m]).astype(BF16)
    for k in range(2):
        gg_ref[k : k + 1, :] = first_found[k] + last_found[k]

    wait_for(send.at[pl.ds(0, K * MSG - PAD)], s1s)
    wait_for(recv.at[pl.ds(0, K * MSG - PAD)], rets)
    wait_for(Y.at[pl.ds(0, K * 3 * BLK), colsA], ags)
    wait_for(IDS.at[pl.ds(1, NX - 1)], idss)
    wait_for(TB.at[pl.ds(0, 3 * T)], pbs)
    for c in range(K):
        wait_for(GB.at[c, pl.ds(1, NX - 1)], gbs)
        wait_for(GPS.at[c, pl.ds(1, NX - 1)], gps)
    for c in range(max(0, K - NSB), K):
        lo = MB if c == 0 else 0
        if ROWS > lo:
            wait_for(sendB.at[c % NSB, pl.ds(lo, ROWS - lo)], sbs.at[c % NSB])
    for c in range(max(0, K - NSLOT), K):
        base = c % NSLOT * ROWS
        lo = MB if c == 0 else 0
        wait_for(XP.at[pl.ds(base + BLK, ROWS - BLK), colsA], xps.at[c])
        if ROWS > lo:
            wait_for(XP.at[pl.ds(base + lo, ROWS - lo), colsB], xpbs.at[c])


def body(out_grad, gates, expert_ids, saved_pre, w_gate_up, w_down):
    T, D = out_grad.shape
    B = lax.axis_size("node")
    C = lax.axis_size("local") // NX
    Q, SLOT = saved_pre.shape[1:3]
    H = w_down.shape[1]
    DA = split(D)
    DB, W = D - DA, DA - spare_columns(DA)
    saved = jnp.transpose(saved_pre[0], (1, 0, 2))
    _, K, G, _ = plan(B, C)
    BLK, MSG = G * SLOT, G * PAD
    ROWS = NX * BLK
    NSLOT = min(6, K)
    NSB = K
    vm = pl.BlockSpec(memory_space=pltpu.VMEM)
    anywhere = pl.BlockSpec(memory_space=pl.ANY)
    dma = pltpu.SemaphoreType.DMA
    ig, gg, dg = pl.pallas_call(
        functools.partial(kernel, B, C, SLOT, NSLOT),
        out_shape=(
            pltpu.VMEM((T, D), BF16),
            pltpu.VMEM((2, T), F32),
            pltpu.VMEM((H, D), BF16),
        ),
        in_specs=[vm, vm, anywhere, anywhere, anywhere, anywhere],
        out_specs=(vm, vm, vm),
        scratch_shapes=[
            pltpu.VMEM((T, D), BF16),
            pltpu.VMEM((D, 2 * H), BF16),
            pltpu.VMEM((K * MSG, W), BF16),
            pltpu.VMEM((K * MSG, W), BF16),
            pltpu.VMEM((K * MSG, W), BF16),
            pltpu.VMEM((K * ROWS, D), BF16),
            pltpu.VMEM((K, NX, PAD, 128), BF16),
            pltpu.VMEM((NSLOT * ROWS, D), BF16),
            pltpu.VMEM((K, BLK, DA), BF16),
            pltpu.VMEM((K, 2, BLK, DA), BF16),
            pltpu.VMEM((K, NX, PAD, 128), BF16),
            pltpu.VMEM((K, NX, PAD, 128), BF16),
            pltpu.VMEM((K * ROWS, 2 * H), BF16),
            pltpu.VMEM((H, K * ROWS), BF16),
            pltpu.VMEM((T, DA), F32),
            pltpu.VMEM((4, T, K * MSG), BF16),
            pltpu.VMEM((ROWS, 2 * H), BF16),
            pltpu.VMEM((ROWS, H), F32),
            pltpu.VMEM((NX, 8, T), jnp.int32),
            pltpu.VMEM((NX * T, DB), BF16),
            pltpu.VMEM((NSB, ROWS, DB), BF16),
            pltpu.VMEM((K * ROWS, DB), BF16),
            pltpu.VMEM((2, T // 2, DB), BF16),
            pltpu.VMEM((2, T, DB), BF16),
            pltpu.VMEM((NX * T, K * ROWS), BF16),
            pltpu.VMEM((ROWS, ROWS), BF16),
            pltpu.VMEM((ROWS, ROWS), BF16),
            dma((3,)),
            dma,
            dma,
            dma((K,)),
            dma,
            dma((K, 3)),
            dma,
            dma((K,)),
            dma((K,)),
            dma((K, 2)),
            dma((K, 2)),
            dma,
            dma((K,)),
            dma,
            dma((K,)),
            dma,
            dma,
            dma,
            dma((3,)),
            dma((NSB,)),
            dma((K,)),
            dma((K,)),
            dma((K,)),
            dma,
            dma((2,)),
            dma((2,)),
        ],
        compiler_params=pltpu.CompilerParams(
            collective_id=0, has_side_effects=True, vmem_limit_bytes=59 * 1024 * 1024
        ),
        cost_estimate=pl.CostEstimate(
            flops=2 * K * ROWS * D * 4 * H, bytes_accessed=25_000_000, transcendentals=K * ROWS * H
        ),
        name="moe_backward",
    )(expert_ids.T, gates.T, out_grad, saved, w_gate_up[0], w_down[0])
    return ig, gg.T, dg[None]


def solution(mesh):
    in_specs = (
        P(("node", "local"), None),
        P(("node", "local"), None),
        P(("node", "local"), None),
        P(("node", "local"), None, None, None),
        P(("node", "local"), None, None),
        P(("node", "local"), None, None),
    )
    out_specs = (
        P(("node", "local"), None),
        P(("node", "local"), None),
        P(("node", "local"), None, None),
    )
    return jax.shard_map(body, mesh=mesh, in_specs=in_specs, out_specs=out_specs, check_vma=False)
```

```python
import functools

import jax
import jax.numpy as jnp
from jax import lax
from jax.experimental import pallas as pl
from jax.experimental.pallas import tpu as pltpu
from jax.sharding import PartitionSpec as P

NX = 4
PAD = 16
TILE = 256
MESH = pl.DeviceIdType.MESH
F32 = jnp.float32
BF16 = jnp.bfloat16


def split(D):
    return max(3 * TILE, 9 * D // 14 // TILE * TILE)


def spare_columns(DA):
    return (DA - 128) // 4 // 128 * 128


def iota(shape, dim):
    return lax.broadcasted_iota(jnp.int32, shape, dim)


def shr(v, bits):
    return lax.shift_right_logical(v, jnp.full(v.shape, bits, jnp.int32))


def log2(size):
    return size.bit_length() - 1


def mm(a, b):
    return jnp.dot(a, b, preferred_element_type=F32)


def mm_nt(a, b):
    return lax.dot_general(a, b, (((1,), (1,)), ((), ())), preferred_element_type=F32)


def hot(mask):
    return mask.astype(F32).astype(BF16)


def plan(B, C):
    cores = 2 if B > C else 1
    even = B // cores == C
    chunks = C * cores if even else C
    return cores, chunks, B * C // chunks, even


def kernel(
    B, C, SLOT, NSLOT,
    ids_ref, gates_ref, og_hbm, saved_hbm, wgu_hbm, wd_hbm,
    ig_ref, gg_ref, dg_ref,
    og_ref, wgu, send, recv, back, Y, GB, XP, RA, RB, GPS, GPR, saved, wT, early, mt, dpre, dact,
    IDS, TB, sendB, backB, RAB, RBB, selT, perm, permT,
    wsem, ssem, s1s, s1r, ags, agr, gbs, gbr, xps, rar, rbr, gps, gpr, rets, backr,
    idss, idsr, tbs, tbr, sbs, sbr, xpbs, bbr, pbs, rabr, rbbr,
):
    T, D = og_ref.shape
    H = dg_ref.shape[0]
    wd = dg_ref
    DA = split(D)
    DB = D - DA
    S = spare_columns(DA)
    W = DA - S
    segs = [slice(m * S, (m + 1) * S) for m in range(3)] + [slice(3 * S, W)]
    tail = slice(W, DA)
    extra = slice(3 * S, 3 * S + 128)
    WA = 3 * TILE if DA % (3 * TILE) == 0 else TILE
    WB = DB // 2 if DB % 256 == 0 else DB
    WG = 2 * TILE
    CORES, K, G, even = plan(B, C)
    BLK = G * SLOT
    MSG = G * PAD
    MB = NX * SLOT
    ROWS = NX * BLK
    NSB = sendB.shape[0]
    LG, LC = log2(G), log2(C)
    colsA, colsB = pl.ds(0, DA), pl.ds(DA, DB)
    n = lax.axis_index("node")
    l = lax.axis_index("local")
    z, x = l // NX, l % NX
    right = (n, z * NX + (x + 1) % NX)
    left = (n, z * NX + (x + NX - 1) % NX)

    YS = B // CORES
    y, core = n // CORES, n % CORES
    LCO = log2(CORES)

    def offsets(c, d):
        return (d, (c // CORES + C - d) % C, c % CORES) if even else (c, d // CORES, d % CORES)

    def peer(c, d):
        dz, dy, dc = offsets(c, d)
        return (((y + dy) % YS) * CORES + (core + dc) % CORES, ((z + dz) % C) * NX + x)

    def source(c, d):
        dz, dy, dc = offsets(c, d)
        return (((y + YS - dy) % YS) * CORES + (core + CORES - dc) % CORES, ((z + C - dz) % C) * NX + x)

    def along(k):
        return (n, z * NX + (x + k) % NX)

    def remote(src, dst, ssem_, rsem_, dev):
        pltpu.make_async_remote_copy(
            src_ref=src, dst_ref=dst, send_sem=ssem_, recv_sem=rsem_, device_id=dev, device_id_type=MESH
        ).start()

    def wait_for(ref, sem):
        pltpu.make_async_copy(ref, ref, sem).wait()

    barrier = pltpu.get_barrier_semaphore()
    count = 0
    for k in range(1, NX):
        pl.semaphore_signal(barrier, inc=1, device_id=along(k), device_id_type=MESH)
        count += 1
    for c in range(K):
        for d in range(G):
            if c or d:
                pl.semaphore_signal(barrier, inc=1, device_id=peer(c, d), device_id_type=MESH)
                count += 1

    wd_copy = pltpu.make_async_copy(wd_hbm, wd, wsem.at[0])
    wgu_copy = pltpu.make_async_copy(wgu_hbm, wgu, wsem.at[1])

    Q = C * NX * B
    QUADS = SLOT // 4
    first_row = NSLOT * ROWS - 4 * Q

    def stage(r):
        dst = XP.at[pl.ds(first_row + r % 4 * Q, Q), pl.ds(r // 4 * 2 * H, 2 * H)]
        return pltpu.make_async_copy(saved_hbm.at[r], dst, ssem)

    og_copy = pltpu.make_async_copy(og_hbm, og_ref, wsem.at[2])
    og_copy.start()
    for r in range(SLOT):
        stage(r).start()
    wd_copy.start()
    wgu_copy.start()

    IDS[0, :2] = ids_ref[...]
    pl.semaphore_wait(barrier, count)
    remote(og_hbm.at[:, colsB], TB.at[pl.ds(3 * T, T)], tbs, tbr.at[0], right)
    remote(og_hbm.at[:, colsB], TB.at[pl.ds(T, T)], tbs, tbr.at[1], left)
    for k in range(1, NX):
        remote(IDS.at[0], IDS.at[NX - k], idss, idsr, along(k))

    NE = max(8, B * C)
    before = hot(iota((T, T), 0) < iota((T, T), 1))
    expert_row = iota((NE, T), 0)

    def route(ids):
        experts = [ids[k : k + 1] for k in range(2)]
        hits = [expert_row == e for e in experts]
        per_token = hits[0].astype(F32) + hits[1].astype(F32)
        earlier = mm(per_token.astype(BF16), before)
        out = []
        for k in range(2):
            rank = jnp.sum(jnp.where(hits[k], earlier, 0.0), axis=0, keepdims=True).astype(jnp.int32)
            zz = experts[k] & (C - 1)
            node = shr(experts[k], LC)
            dz = (zz - z + C) & (C - 1)
            dy = (shr(node, LCO) - y + YS) & (YS - 1)
            dc = (node - core + CORES) & (CORES - 1)
            blk = (((dy + dz) & (C - 1)) * CORES + dc) * G + dz if even else dz * G + dy * CORES + dc
            out.append((blk, rank))
        return out

    own = route(ids_ref[...])
    def third(v):
        return shr(v * 11, 5)

    slots = iota((K * MSG, T), 0)
    lane_slot = iota((128, T), 0)
    picks = [jnp.zeros((K * MSG, T), F32) for _ in range(4)]
    gate_rows = jnp.zeros((K * MSG, 128), F32)
    gates = gates_ref[...].astype(F32)
    for k, (blk, rank) in enumerate(own):
        at = slots - blk * PAD
        picks[3] += (at == rank).astype(F32)
        for m in range(3):
            spare = jnp.where(rank - 3 * third(rank) == m, SLOT + third(rank), -K * MSG)
            picks[m] += (at == spare).astype(F32)
        gate_at = jnp.where(lane_slot == rank, gates[k : k + 1], 0.0).astype(BF16)
        gate_rows += mm_nt(hot(at == SLOT), gate_at)
    picks_t = [jnp.transpose(p).astype(BF16) for p in picks]
    picks = [p.astype(BF16) for p in picks]
    og_copy.wait()

    HEAD = max(1, K // 4)

    def a_send(first, last):
        for g in range(first, last, HEAD):
            rows = slice(g * MSG, (g + HEAD) * MSG)
            for m in range(3):
                both = mm(picks[3][rows], og_ref[:, segs[m]]) + mm(picks[m][rows], og_ref[:, tail])
                send[rows, segs[m]] = both.astype(BF16)
            rest = mm(picks[3][rows], og_ref[:, segs[3]])
            rest = jnp.concatenate([rest[:, :128] + gate_rows[rows], rest[:, 128:]], axis=1)
            send[rows, segs[3]] = rest.astype(BF16)
            for c in range(g, g + HEAD):
                for d in range(G):
                    at = pl.ds((c * G + d) * PAD, PAD)
                    if c or d:
                        remote(send.at[at], recv.at[at], s1s, s1r.at[c], peer(c, d))
        if first == 0:
            recv[:PAD] = send[:PAD]

    a_send(0, max(1, 3 * K // 4))
    TB[:T] = og_ref[:, DA:]
    for m in range(4):
        mt[m] = picks_t[m]

    def row_parts(i):
        j = jnp.zeros(i.shape, jnp.int32)
        for k in range(1, NX):
            j += (i >= k * BLK).astype(jnp.int32)
        rest = i - j * BLK
        return j, shr(rest, LG), rest & (G - 1)

    def places(shape, dim):
        _, r, d = row_parts(iota(shape, dim))
        at = iota(shape, 1 - dim) - d * PAD
        tails = [hot((at == SLOT + third(r)) & (r - 3 * third(r) == m)) for m in range(3)]
        return tails + [hot(at == r)]

    compact = places((BLK, MSG), 0)
    expand = places((MSG, BLK), 1)
    gate_pick = hot(iota((PAD, MSG), 1) == iota((PAD, MSG), 0) * PAD + SLOT)
    of_source = hot((iota((BLK, PAD), 0) & (G - 1)) == iota((BLK, PAD), 1))
    by_source = hot((iota((PAD, BLK), 1) & (G - 1)) == iota((PAD, BLK), 0))
    slot_mask = iota((BLK, 128), 1) == shr(iota((BLK, 128), 0), LG)
    j_i, r_i, d_i = row_parts(iota((ROWS, ROWS), 0))
    perm[...] = hot(iota((ROWS, ROWS), 1) == d_i * MB + j_i * SLOT + r_i)
    j_l, r_l, d_l = row_parts(iota((ROWS, ROWS), 1))
    permT[...] = hot(iota((ROWS, ROWS), 0) == d_l * MB + j_l * SLOT + r_l)

    def sort_saved():
        row, col = iota((K * NX * 4 * G, 4 * Q), 0), iota((K * NX * 4 * G, 4 * Q), 1)
        r, d, j, c = shr(row, LG) & 3, row & (G - 1), shr(row, LG + 2) & (NX - 1), shr(row, LG + 4)
        if even:
            dz, dc = d, c & (CORES - 1)
            dy = (shr(c, LCO) + C - dz) & (C - 1)
        else:
            dz, dy, dc = c, shr(d, LCO), d & (CORES - 1)
        node = ((y + YS - dy) & (YS - 1)) * CORES + ((core + CORES - dc) & (CORES - 1))
        q = node * (C * NX) + ((z + C - dz) & (C - 1)) * NX + ((x + j) & (NX - 1))
        order = hot(col == r * Q + q)
        wait_for(XP.at[pl.ds(first_row, 4 * Q), pl.ds(0, QUADS * 2 * H)], ssem)
        NS = min(TILE, 2 * H)
        for p in range(QUADS):
            for i in range(2 * H // NS):
                cols = slice(p * 2 * H + i * NS, p * 2 * H + (i + 1) * NS)
                out = mm(order, XP[first_row : first_row + 4 * Q, cols]).astype(BF16)
                for g in range(K * NX):
                    at = g * BLK + p * 4 * G
                    saved[at : at + 4 * G, i * NS : (i + 1) * NS] = out[g * 4 * G : (g + 1) * 4 * G]

    def b_forward():
        h = T // 2
        wait_for(TB.at[pl.ds(3 * T, T)], tbr.at[0])
        remote(TB.at[pl.ds(3 * T, h)], TB.at[pl.ds(2 * T, h)], tbs, tbr.at[2], right)
        wait_for(TB.at[pl.ds(T, T)], tbr.at[1])
        remote(TB.at[pl.ds(T + h, h)], TB.at[pl.ds(2 * T + h, h)], tbs, tbr.at[2], left)

    def b_routes():
        wait_for(IDS.at[pl.ds(1, NX - 1)], idsr)
        return [own] + [route(IDS[j, :2]) for j in range(1, NX)]

    def b_part(ref, c, lead):
        lo = MB if c == 0 else 0
        return ref.at[lead, pl.ds(lo, ROWS - lo)] if lead is not None else ref.at[pl.ds(lo, ROWS - lo)]

    def b_select(c, routes):
        slot = c % NSB
        at = iota((ROWS, T), 0)
        parts = []
        for j in range(NX):
            part = jnp.zeros((ROWS, T), F32)
            for blk, rank in routes[j]:
                part += (at == (blk - c * G) * MB + j * SLOT + rank).astype(F32)
            parts.append(part)
            selT[j * T : (j + 1) * T, c * ROWS : (c + 1) * ROWS] = jnp.transpose(part).astype(BF16)
        sel = jnp.concatenate(parts, axis=1).astype(BF16)
        if c == 0:
            wait_for(TB.at[pl.ds(2 * T, T)], tbr.at[2])
        if c >= NSB and (G > 1 or c > NSB):
            wait_for(b_part(sendB, c - NSB, slot), sbs.at[slot])
        for i in range(DB // TILE):
            cols = slice(i * TILE, (i + 1) * TILE)
            sendB[slot, :, cols] = mm(sel, TB[:, cols]).astype(BF16)
        for d in range(G):
            if c or d:
                remote(
                    sendB.at[slot, pl.ds(d * MB, MB)], Y.at[pl.ds(c * ROWS + d * MB, MB), colsB],
                    sbs.at[slot], sbr.at[c], peer(c, d),
                )
            else:
                Y[:MB, DA:] = sendB[slot, :MB]

    def b_land(c):
        lo = MB if c == 0 else 0
        if ROWS > lo:
            wait_for(Y.at[pl.ds(c * ROWS + lo, ROWS - lo), colsB], sbr.at[c])
        rows = slice(c * ROWS, (c + 1) * ROWS)
        for i in range(DB // TILE):
            cols = slice(DA + i * TILE, DA + (i + 1) * TILE)
            Y[rows, cols] = mm(perm[...], Y[rows, cols]).astype(BF16)

    def yrows(c, j, lo=0, size=None):
        return pl.ds(c * ROWS + j * BLK + lo, BLK if size is None else size)

    def gather_start(c):
        lo = PAD if c == 0 else 0
        if MSG > lo:
            wait_for(recv.at[pl.ds(c * MSG + lo, MSG - lo)], s1r.at[c])
        own_rows = slice(c * ROWS, c * ROWS + BLK)
        msg = slice(c * MSG, (c + 1) * MSG)
        last = jnp.zeros((BLK, S), F32)
        for m in range(4):
            Y[own_rows, segs[m]] = mm(compact[3], recv[msg, segs[m]]).astype(BF16)
            if m < 3:
                last += mm(compact[m], recv[msg, segs[m]])
        Y[own_rows, tail] = last.astype(BF16)
        GB[c, 0] = mm(gate_pick, recv[msg, extra]).astype(BF16)
        remote(Y.at[yrows(c, 0), colsA], Y.at[yrows(c, 3), colsA], ags, agr.at[c, 0], right)
        remote(Y.at[yrows(c, 0), colsA], Y.at[yrows(c, 1), colsA], ags, agr.at[c, 1], left)
        for k in range(1, NX):
            remote(GB.at[c, 0], GB.at[c, NX - k], gbs, gbr.at[c], along(k))

    def cut_of(c):
        return BLK * (2 - c % 2) // 3

    def gather_forward(c):
        wait_for(Y.at[yrows(c, 3), colsA], agr.at[c, 0])
        cut = cut_of(c)
        remote(Y.at[yrows(c, 3, 0, cut), colsA], Y.at[yrows(c, 2, 0, cut), colsA], ags, agr.at[c, 2], right)
        wait_for(Y.at[yrows(c, 1), colsA], agr.at[c, 1])
        rest = BLK - cut
        remote(Y.at[yrows(c, 1, cut, rest), colsA], Y.at[yrows(c, 2, cut, rest), colsA], ags, agr.at[c, 2], left)

    def compute(c):
        base = c % NSLOT * ROWS
        wait_for(Y.at[yrows(c, 2), colsA], agr.at[c, 2])
        wait_for(GB.at[c, pl.ds(1, NX - 1)], gbr.at[c])
        b_land(c)
        if c == 0:
            wd_copy.wait()
        NT = min(TILE, H)
        for i in range(H // NT):
            dact[:, i * NT : (i + 1) * NT] = mm_nt(Y[c * ROWS : (c + 1) * ROWS, :], wd[i * NT : (i + 1) * NT, :])
        for j in range(NX):
            rows = slice(j * BLK, (j + 1) * BLK)
            at = c * ROWS + j * BLK
            a = saved[at : at + BLK, :H].astype(F32)
            b = saved[at : at + BLK, H:].astype(F32)
            da = dact[rows, :]
            spread = mm(of_source, GB[c, j])
            scale = jnp.sum(jnp.where(slot_mask, spread, 0.0), axis=1, keepdims=True)
            s = jax.nn.sigmoid(a)
            act = a * s
            hidden = act * b
            part = jnp.sum(hidden * da, axis=1, keepdims=True)
            parts = jnp.where(slot_mask, part, 0.0).astype(BF16)
            GPS[c, j] = mm(by_source, parts).astype(BF16)
            dh = scale * da
            dpre[rows, :H] = (dh * b * s * (1.0 + a * (1.0 - s))).astype(BF16)
            dpre[rows, H:] = (dh * act).astype(BF16)
            dact[rows, :] = scale * hidden
        for k in range(1, NX):
            remote(GPS.at[c, k], GPR.at[c, NX - k], gps, gpr.at[c], along(k))
        if c == 0:
            wgu_copy.wait()
        if c >= NSLOT:
            o = c - NSLOT
            wait_for(XP.at[pl.ds(base + BLK, ROWS - BLK), colsA], xps.at[o])
            lo = MB if o == 0 else 0
            if ROWS > lo:
                wait_for(XP.at[pl.ds(base + lo, ROWS - lo), colsB], xpbs.at[o])

        def tile_a(i, _):
            cols = pl.ds(pl.multiple_of(i * WA, TILE), WA)
            XP[base : base + ROWS, cols] = mm_nt(dpre[...], wgu[cols, :]).astype(BF16)
            return 0

        lax.fori_loop(0, DA // WA, tile_a, 0)

        cut = cut_of(c)
        rest = BLK - cut

        def part_of(j, lo, size):
            return XP.at[pl.ds(base + j * BLK + lo, size), colsA]

        remote(part_of(2, 0, cut), RA.at[c, pl.ds(0, cut)], xps.at[c], rar.at[c, 0], right)
        remote(part_of(2, cut, rest), RA.at[c, pl.ds(cut, rest)], xps.at[c], rar.at[c, 1], left)
        remote(part_of(1, cut, rest), RB.at[c, 0, pl.ds(cut, rest)], xps.at[c], rbr.at[c, 0], right)
        remote(part_of(3, 0, cut), RB.at[c, 1, pl.ds(0, cut)], xps.at[c], rbr.at[c, 1], left)
        def tile_b(i, _):
            cols = pl.ds(pl.multiple_of(DA + i * WB, 128), WB)
            XP[base : base + ROWS, cols] = mm(permT[...], mm_nt(dpre[...], wgu[cols, :]).astype(BF16)).astype(BF16)
            return 0

        lax.fori_loop(0, DB // WB, tile_b, 0)
        for d in range(G):
            if c or d:
                remote(
                    XP.at[pl.ds(base + d * MB, MB), colsB], backB.at[pl.ds((c * G + d) * MB, MB)],
                    xpbs.at[c], bbr.at[c], source(c, d),
                )
            else:
                backB[:MB] = XP[base : base + MB, DA:]

        wT[:, c * ROWS : (c + 1) * ROWS] = jnp.transpose(dact[...]).astype(BF16)

    def reduce_middle(c):
        base = c % NSLOT * ROWS
        cut = cut_of(c)
        for side, j, lo, size, dev in ((0, 1, 0, cut, right), (1, 3, cut, BLK - cut, left)):
            wait_for(RA.at[c, pl.ds(lo, size)], rar.at[c, side])
            at = base + j * BLK + lo
            rows = slice(at, at + size)
            XP[rows, :DA] = (XP[rows, :DA].astype(F32) + RA[c, lo : lo + size].astype(F32)).astype(BF16)
            remote(XP.at[pl.ds(at, size), colsA], RB.at[c, side, pl.ds(lo, size)], xps.at[c], rbr.at[c, side], dev)

    def reduce_end(c):
        base = c % NSLOT * ROWS
        wait_for(GPR.at[c, pl.ds(1, NX - 1)], gpr.at[c])
        total = GPS[c, 0].astype(F32)
        for k in range(1, NX):
            total += GPR[c, k].astype(F32)
        high = total.astype(BF16)
        low = (total - high.astype(F32)).astype(BF16)
        up = iota((MSG, PAD), 0) - iota((MSG, PAD), 1) * PAD
        gate_back = mm(hot(up == SLOT), high) + mm(hot(up == SLOT + 1), low)
        wait_for(RB.at[c, 0], rbr.at[c, 0])
        wait_for(RB.at[c, 1], rbr.at[c, 1])
        msg = slice(c * MSG, (c + 1) * MSG)
        def whole(cols):
            part = XP[base : base + BLK, cols].astype(F32) + RB[c, 0, :, cols].astype(F32)
            return (part + RB[c, 1, :, cols].astype(F32)).astype(BF16)

        last = whole(tail)
        for m in range(3):
            recv[msg, segs[m]] = (mm(expand[3], whole(segs[m])) + mm(expand[m], last)).astype(BF16)
        rest = mm(expand[3], whole(segs[3]))
        rest = jnp.concatenate([rest[:, :128] + gate_back, rest[:, 128:]], axis=1)
        recv[msg, segs[3]] = rest.astype(BF16)
        for d in range(G):
            rows = pl.ds((c * G + d) * PAD, PAD)
            if c or d:
                remote(recv.at[rows], back.at[rows], rets, backr.at[c], source(c, d))
        if c == 0:
            back[:PAD] = recv[:PAD]

    def b_sum():
        for c in range(K):
            lo = MB if c == 0 else 0
            if ROWS > lo:
                wait_for(backB.at[pl.ds(c * ROWS + lo, ROWS - lo)], bbr.at[c])
        wait_for(TB.at[pl.ds(0, 3 * T)], tbs)
        for i in range(DB // TILE):
            cols = slice(i * TILE, (i + 1) * TILE)
            TB[:, cols] = mm(selT[...], backB[:, cols]).astype(BF16)
        h = T // 2
        remote(TB.at[pl.ds(2 * T, h)], RAB.at[0], pbs, rabr.at[0], right)
        remote(TB.at[pl.ds(2 * T + h, h)], RAB.at[1], pbs, rabr.at[1], left)
        remote(TB.at[pl.ds(T + h, h)], RBB.at[0, pl.ds(h, h)], pbs, rbbr.at[0], right)
        remote(TB.at[pl.ds(3 * T, h)], RBB.at[1, pl.ds(0, h)], pbs, rbbr.at[1], left)

    def b_middle():
        h = T // 2
        for side, j, lo, dev in ((0, 1, 0, right), (1, 3, h, left)):
            wait_for(RAB.at[side], rabr.at[side])
            rows = slice(j * T + lo, j * T + lo + h)
            TB[rows, :] = (TB[rows, :].astype(F32) + RAB[side].astype(F32)).astype(BF16)
            remote(TB.at[pl.ds(j * T + lo, h)], RBB.at[side, pl.ds(lo, h)], pbs, rbbr.at[side], dev)

    def b_end():
        wait_for(RBB.at[0], rbbr.at[0])
        wait_for(RBB.at[1], rbbr.at[1])
        ig_ref[:, DA:] = (TB[:T].astype(F32) + RBB[0].astype(F32) + RBB[1].astype(F32)).astype(BF16)

    tiles = D // WG

    def weight_grad(first, last):
        def tile(i, _):
            cols = pl.ds(pl.multiple_of(i * WG, TILE), WG)
            dg_ref[:, cols] = mm(wT[...], Y[:, cols]).astype(BF16)
            return 0

        lax.fori_loop(first, last, tile, 0)

    b_forward()
    gather_start(0)
    routes = b_routes()
    b_select(0, routes)
    a_send(max(1, 3 * K // 4), K)
    b_select(1, routes)
    gather_start(1)
    gather_forward(0)
    for c in range(2, min(4, K)):
        b_select(c, routes)
    sort_saved()
    for c in range(2, min(4, K)):
        gather_start(c)
        if c == 2:
            gather_forward(1)
    if K == 2:
        gather_forward(1)
    for c in range(4, K):
        b_select(c, routes)
    ended = 0
    for c in range(K):
        compute(c)
        if c + 2 < K:
            gather_forward(c + 2)
        if c + 4 < K:
            gather_start(c + 4)
        if c >= 1:
            reduce_middle(c - 1)
        done = c - 2 if c > K // 2 else c - 3
        for o in range(ended, done + 1):
            reduce_end(o)
        ended = max(ended, done + 1)
    part = tiles // 3
    weight_grad(0, part)
    reduce_middle(K - 1)
    for o in range(ended, K - 1):
        reduce_end(o)
    b_sum()
    weight_grad(part, tiles)
    reduce_end(K - 1)
    b_middle()
    b_end()

    def own_sums(first, last):
        for c in range(first, last):
            lo = PAD if c == 0 else 0
            if MSG > lo:
                wait_for(back.at[pl.ds(c * MSG + lo, MSG - lo)], backr.at[c])
        rows = slice(first * MSG, last * MSG)
        ends = jnp.zeros((T, S), F32)
        sums = []
        for m in range(4):
            sums.append(mm(mt[3, :, rows], back[rows, segs[m]]))
            if m < 3:
                ends += mm(mt[m, :, rows], back[rows, segs[m]])
        back_gates = jnp.transpose(back[rows, extra].astype(F32)).astype(BF16)
        found = []
        for k, (blk, rank) in enumerate(own):
            at = slots[rows] - blk * PAD
            chosen = mm(back_gates, hot((at == SLOT) | (at == SLOT + 1)))
            found.append(jnp.sum(jnp.where(lane_slot == rank, chosen, 0.0), axis=0, keepdims=True))
        return sums + [ends], found

    first_sums, first_found = own_sums(0, K - 1)
    for m in range(5):
        early[:, (segs + [tail])[m]] = first_sums[m]
    last_sums, last_found = own_sums(K - 1, K)
    for m in range(5):
        cols = (segs + [tail])[m]
        ig_ref[:, cols] = (early[:, cols] + last_sums[m]).astype(BF16)
    for k in range(2):
        gg_ref[k : k + 1, :] = first_found[k] + last_found[k]

    wait_for(send.at[pl.ds(0, K * MSG - PAD)], s1s)
    wait_for(recv.at[pl.ds(0, K * MSG - PAD)], rets)
    wait_for(Y.at[pl.ds(0, K * 3 * BLK), colsA], ags)
    wait_for(IDS.at[pl.ds(1, NX - 1)], idss)
    wait_for(TB.at[pl.ds(0, 3 * T)], pbs)
    for c in range(K):
        wait_for(GB.at[c, pl.ds(1, NX - 1)], gbs)
        wait_for(GPS.at[c, pl.ds(1, NX - 1)], gps)
    for c in range(max(0, K - NSB), K):
        lo = MB if c == 0 else 0
        if ROWS > lo:
            wait_for(sendB.at[c % NSB, pl.ds(lo, ROWS - lo)], sbs.at[c % NSB])
    for c in range(max(0, K - NSLOT), K):
        base = c % NSLOT * ROWS
        lo = MB if c == 0 else 0
        wait_for(XP.at[pl.ds(base + BLK, ROWS - BLK), colsA], xps.at[c])
        if ROWS > lo:
            wait_for(XP.at[pl.ds(base + lo, ROWS - lo), colsB], xpbs.at[c])


def body(out_grad, gates, expert_ids, saved_pre, w_gate_up, w_down):
    T, D = out_grad.shape
    B = lax.axis_size("node")
    C = lax.axis_size("local") // NX
    Q, SLOT = saved_pre.shape[1:3]
    H = w_down.shape[1]
    DA = split(D)
    DB, W = D - DA, DA - spare_columns(DA)
    saved = jnp.transpose(saved_pre[0], (1, 0, 2))
    _, K, G, _ = plan(B, C)
    BLK, MSG = G * SLOT, G * PAD
    ROWS = NX * BLK
    NSLOT = min(6, K)
    NSB = K
    vm = pl.BlockSpec(memory_space=pltpu.VMEM)
    anywhere = pl.BlockSpec(memory_space=pl.ANY)
    dma = pltpu.SemaphoreType.DMA
    ig, gg, dg = pl.pallas_call(
        functools.partial(kernel, B, C, SLOT, NSLOT),
        out_shape=(
            pltpu.VMEM((T, D), BF16),
            pltpu.VMEM((2, T), F32),
            pltpu.VMEM((H, D), BF16),
        ),
        in_specs=[vm, vm, anywhere, anywhere, anywhere, anywhere],
        out_specs=(vm, vm, vm),
        scratch_shapes=[
            pltpu.VMEM((T, D), BF16),
            pltpu.VMEM((D, 2 * H), BF16),
            pltpu.VMEM((K * MSG, W), BF16),
            pltpu.VMEM((K * MSG, W), BF16),
            pltpu.VMEM((K * MSG, W), BF16),
            pltpu.VMEM((K * ROWS, D), BF16),
            pltpu.VMEM((K, NX, PAD, 128), BF16),
            pltpu.VMEM((NSLOT * ROWS, D), BF16),
            pltpu.VMEM((K, BLK, DA), BF16),
            pltpu.VMEM((K, 2, BLK, DA), BF16),
            pltpu.VMEM((K, NX, PAD, 128), BF16),
            pltpu.VMEM((K, NX, PAD, 128), BF16),
            pltpu.VMEM((K * ROWS, 2 * H), BF16),
            pltpu.VMEM((H, K * ROWS), BF16),
            pltpu.VMEM((T, DA), F32),
            pltpu.VMEM((4, T, K * MSG), BF16),
            pltpu.VMEM((ROWS, 2 * H), BF16),
            pltpu.VMEM((ROWS, H), F32),
            pltpu.VMEM((NX, 8, T), jnp.int32),
            pltpu.VMEM((NX * T, DB), BF16),
            pltpu.VMEM((NSB, ROWS, DB), BF16),
            pltpu.VMEM((K * ROWS, DB), BF16),
            pltpu.VMEM((2, T // 2, DB), BF16),
            pltpu.VMEM((2, T, DB), BF16),
            pltpu.VMEM((NX * T, K * ROWS), BF16),
            pltpu.VMEM((ROWS, ROWS), BF16),
            pltpu.VMEM((ROWS, ROWS), BF16),
            dma((3,)),
            dma,
            dma,
            dma((K,)),
            dma,
            dma((K, 3)),
            dma,
            dma((K,)),
            dma((K,)),
            dma((K, 2)),
            dma((K, 2)),
            dma,
            dma((K,)),
            dma,
            dma((K,)),
            dma,
            dma,
            dma,
            dma((3,)),
            dma((NSB,)),
            dma((K,)),
            dma((K,)),
            dma((K,)),
            dma,
            dma((2,)),
            dma((2,)),
        ],
        compiler_params=pltpu.CompilerParams(
            collective_id=0, has_side_effects=True, vmem_limit_bytes=59 * 1024 * 1024
        ),
        cost_estimate=pl.CostEstimate(
            flops=2 * K * ROWS * D * 4 * H, bytes_accessed=25_000_000, transcendentals=K * ROWS * H
        ),
        name="moe_backward",
    )(expert_ids.T, gates.T, out_grad, saved, w_gate_up[0], w_down[0])
    return ig, gg.T, dg[None]


def solution(mesh):
    in_specs = (
        P(("node", "local"), None),
        P(("node", "local"), None),
        P(("node", "local"), None),
        P(("node", "local"), None, None, None),
        P(("node", "local"), None, None),
        P(("node", "local"), None, None),
    )
    out_specs = (
        P(("node", "local"), None),
        P(("node", "local"), None),
        P(("node", "local"), None, None),
    )
    return jax.shard_map(body, mesh=mesh, in_specs=in_specs, out_specs=out_specs, check_vma=False)
```
